256 devices in a mesh: slab: 16 (over x_hi, z), gx: 16 (over x_lo, y, core).
Axes of the slice: x: 4 (x_hi: 2, x_lo: 2; x = x_hi * 2 + x_lo), y: 4, z: 8, core: 2. Of those that a mesh axis runs over, the one named last changes fastest.
Arguments:
- stem_features: bfloat16 [32, 16, 32, 4096], P(None, 'slab', None, 'gx'), may hold values from -6 to 6
- labels: int32 [16, 32, 4096], P(None, 'slab', 'gx'), may hold values from 0 to 1
- conv_a: bfloat16 [32, 3, 3, 32], replicated, may hold values from -0.5 to 0.5
- conv_b: bfloat16 [32, 3, 3, 32], replicated, may hold values from -0.5 to 0.5
- conv_c: bfloat16 [32, 3, 3, 32], replicated, may hold values from -0.5 to 0.5
- conv_d: bfloat16 [32, 3, 3, 32], replicated, may hold values from -0.5 to 0.5
- head_one: bfloat16 [32], replicated, may hold values from -1 to 1
- head_two: bfloat16 [32], replicated, may hold values from -1 to 1
Outputs:
- probability: float32 [16, 32, 4096], P(None, 'slab', 'gx')
- stem_grad: bfloat16 [32, 16, 32, 4096], P(None, 'slab', None, 'gx')
- grad_conv_a: float32 [32, 3, 3, 32], replicated
- grad_conv_b: float32 [32, 3, 3, 32], replicated
- grad_conv_c: float32 [32, 3, 3, 32], replicated
- grad_conv_d: float32 [32, 3, 3, 32], replicated
- grad_head_one: float32 [32], replicated
- grad_head_two: float32 [32], replicated
The draws below stay inside these ranges and needn't reach their ends.
All inputs are finite; a program needn't handle non-finite values.
Results may differ from the reference program's by a relative error of at most 0.0095.
Values may be sent and summed in bfloat16 or wider, within the bound.
No kernel may reach another device: no remote copies, remote signals or barrier semaphores. Data moves between devices by JAX's collectives and lax.ppermute only.
A program may use at most 128 MiB of HBM per device.

```python
import jax
import jax.numpy as jnp
from jax import lax

C = 32
ZD = 1
Y = 32
XD = 256
Z = 16
X = 4096


def plant(result, stream_key, low, top_value):
    extent = result.shape
    place = [jax.random.randint(jax.random.fold_in(stream_key, axis), (), 0, extent[axis]) for axis in range(len(extent))]
    result = result.at[tuple(place)].set(low)
    longest = extent.index(max(extent))
    place[longest] = (place[longest] + 1) % extent[longest]
    return result.at[tuple(place)].set(top_value)


def block_levels(own_key, dims, shards, least, high):
    def one(position, blocks):
        draws = jax.random.uniform(jax.random.fold_in(jax.random.fold_in(own_key, 6), position), (blocks,), jnp.float32, least / len(shards), high / len(shards))
        return jnp.repeat(jnp.exp(draws), dims[position] // blocks).reshape((-1,) + (1,) * (len(dims) - position - 1))

    factor_of = one(*shards[0])
    for cut in shards[1:]:
        factor_of = factor_of * one(*cut)
    return factor_of


def centred(own_key, extent, spread, most, shards=(), held_as=jnp.bfloat16):
    drawn = jax.random.normal(own_key, extent, jnp.float32) * spread
    if len(shards) > 0:
        drawn = block_levels(own_key, extent, shards, -0.22, 0.18) * drawn
    return jnp.clip(drawn, min=-most, max=most).astype(held_as)


def setup_inputs(seed: int = 0) -> dict:
    key_list = jax.random.split(jax.random.key(seed), 9)
    stem_features = centred(key_list[0], (C, Z, Y, X), 1.0, 6.0, ((1, 16), (3, 16)))
    labels = plant(jax.random.randint(key_list[1], (Z, Y, X), 0, 2), jax.random.fold_in(key_list[1], 1), 0, 1).astype(jnp.int32)
    conv_a = centred(key_list[2], (C, 3, 3, C), (9 * C // 2) ** -0.5, 0.5)
    conv_b = centred(key_list[3], (C, 3, 3, C), (9 * C // 2) ** -0.5, 0.5)
    conv_c = centred(key_list[4], (C, 3, 3, C), (9 * C // 2) ** -0.5, 0.5)
    conv_d = centred(key_list[5], (C, 3, 3, C), (9 * C // 2) ** -0.5, 0.5)
    head_one = centred(key_list[6], (C,), C ** -0.5, 1.0)
    head_two = centred(key_list[7], (C,), C ** -0.5, 1.0)
    return {"stem_features": stem_features, "labels": labels, "conv_a": conv_a, "conv_b": conv_b, "conv_c": conv_c, "conv_d": conv_d, "head_one": head_one, "head_two": head_two}


def pad_field(source, dilation, plane_dim):
    widths = [(0, 0)] * source.ndim
    widths[plane_dim] = (dilation, dilation)
    widths[3] = (dilation, dilation)
    return jnp.pad(source, widths)

def tap_columns(padded, dilation, plane_dim, row_tap, out_plane, out_cols):
    rows_cut = lax.slice_in_dim(padded, row_tap * dilation, row_tap * dilation + out_plane, axis=plane_dim)
    pieces = [lax.slice_in_dim(rows_cut, col_tap * dilation, col_tap * dilation + out_cols, axis=3) for col_tap in range(3)]
    return jnp.concatenate(pieces, axis=0)

def conv_valid(padded, weight, dilation, plane_dim):
    out_plane = padded.shape[plane_dim] - 2 * dilation
    out_cols = padded.shape[3] - 2 * dilation
    summed = None
    for row_tap in range(3):
        weight_row = weight[:, row_tap].reshape(weight.shape[0], -1).astype(jnp.float32)
        columns = tap_columns(padded, dilation, plane_dim, row_tap, out_plane, out_cols).astype(jnp.float32)
        term = jnp.einsum('ok,kabx->oabx', weight_row, columns, precision=lax.Precision.HIGHEST)
        summed = term if summed is None else summed + term
    return summed

def conv_same(source, weight, dilation, plane_dim):
    return conv_valid(pad_field(source, dilation, plane_dim), weight, dilation, plane_dim)

def flipped(weight):
    return jnp.transpose(weight[:, ::-1, ::-1, :], (3, 1, 2, 0))

def weight_grad(delta_out, padded, dilation, plane_dim):
    out_plane = delta_out.shape[plane_dim]
    out_cols = delta_out.shape[3]
    grad_rows = []
    for row_tap in range(3):
        columns = tap_columns(padded, dilation, plane_dim, row_tap, out_plane, out_cols).astype(jnp.float32)
        grad_row = jnp.einsum('oabx,kabx->ok', delta_out.astype(jnp.float32), columns, precision=lax.Precision.HIGHEST)
        grad_rows.append(grad_row.reshape(delta_out.shape[0], 3, -1))
    return jnp.stack(grad_rows, axis=1)

def rectify(value):
    return jax.nn.softplus(value).astype(jnp.bfloat16)

def slope(stored):
    return 1.0 - jnp.exp(-stored.astype(jnp.float32))

def reference(stem_features, labels, conv_a, conv_b, conv_c, conv_d, head_one, head_two):
    readout_one = head_one.astype(jnp.float32)
    readout_two = head_two.astype(jnp.float32)

    def forward_slab(stem_slice):
        source = stem_slice[:, None]
        hidden_one = rectify(conv_same(source, conv_a, 1, 2))
        hidden_two = rectify(conv_same(hidden_one, conv_b, 2, 2))
        logit_one = jnp.einsum('c,cabx->abx', readout_one, hidden_two.astype(jnp.float32)).astype(jnp.bfloat16)
        return (hidden_two[:, 0], logit_one[0])
    stem_slabs = jnp.moveaxis(stem_features, 1, 0)
    hidden_all, logit_all = lax.map(forward_slab, stem_slabs)

    def refine_row(element):
        features_row, logit_row, label_row = element
        hidden_two = features_row[:, :, None]
        logit_one = logit_row[:, None].astype(jnp.float32)
        target = label_row[:, None].astype(jnp.float32)
        refined_one = rectify(conv_same(hidden_two, conv_c, 1, 1))
        refined_two = rectify(conv_same(refined_one, conv_d, 2, 1))
        logit_two = jnp.einsum('c,cabx->abx', readout_two, refined_two.astype(jnp.float32)) + logit_one
        probability = jax.nn.sigmoid(logit_two)
        error_two = probability - target
        error_one = jax.nn.sigmoid(logit_one) - target + error_two
        grad_two = jnp.einsum('abx,cabx->c', error_two, refined_two.astype(jnp.float32))
        grad_one = jnp.einsum('abx,cabx->c', error_one, hidden_two.astype(jnp.float32))
        delta_two = (readout_two[:, None, None, None] * error_two[None] * slope(refined_two)).astype(jnp.bfloat16)
        grad_d = weight_grad(delta_two, pad_field(refined_one, 2, 1), 2, 1)
        delta_one = (conv_same(delta_two, flipped(conv_d), 2, 1) * slope(refined_one)).astype(jnp.bfloat16)
        grad_c = weight_grad(delta_one, pad_field(hidden_two, 1, 1), 1, 1)
        back_two = (conv_same(delta_one, flipped(conv_c), 1, 1) + readout_one[:, None, None, None] * error_one[None]).astype(jnp.bfloat16)
        return (probability[:, 0], back_two[:, :, 0], grad_one, grad_two, grad_c, grad_d)
    rows_in = (jnp.transpose(hidden_all, (2, 1, 0, 3)), jnp.transpose(logit_all, (1, 0, 2)), jnp.transpose(labels, (1, 0, 2)))
    prob_rows, back_rows, grads_one, grads_two, grads_c, grads_d = lax.map(refine_row, rows_in)
    back_slabs = jnp.transpose(back_rows, (2, 1, 0, 3))

    def backward_slab(element):
        stem_slice, back_slice = element
        source = stem_slice[:, None]
        hidden_one = rectify(conv_same(source, conv_a, 1, 2))
        hidden_two = rectify(conv_same(hidden_one, conv_b, 2, 2))
        delta_b = (back_slice[:, None].astype(jnp.float32) * slope(hidden_two)).astype(jnp.bfloat16)
        grad_b = weight_grad(delta_b, pad_field(hidden_one, 2, 2), 2, 2)
        delta_a = (conv_same(delta_b, flipped(conv_b), 2, 2) * slope(hidden_one)).astype(jnp.bfloat16)
        grad_a = weight_grad(delta_a, pad_field(source, 1, 2), 1, 2)
        stem_back = conv_same(delta_a, flipped(conv_a), 1, 2).astype(jnp.bfloat16)
        return (stem_back[:, 0], grad_a, grad_b)
    back_stem, grads_a, grads_b = lax.map(backward_slab, (stem_slabs, back_slabs))
    factor = 1.0 / (ZD * Y * XD)
    probability = jnp.transpose(prob_rows, (1, 0, 2))
    stem_grad = jnp.moveaxis(back_stem, 0, 1)
    return (probability, stem_grad, lax.optimization_barrier(jnp.sum(grads_a, axis=0)) * factor, lax.optimization_barrier(jnp.sum(grads_b, axis=0)) * factor, lax.optimization_barrier(jnp.sum(grads_c, axis=0)) * factor, lax.optimization_barrier(jnp.sum(grads_d, axis=0)) * factor, lax.optimization_barrier(jnp.sum(grads_one, axis=0)) * factor, lax.optimization_barrier(jnp.sum(grads_two, axis=0)) * factor)
```

```python
import functools

import jax
import jax.numpy as jnp
from jax import lax
from jax.experimental import pallas as pl
from jax.experimental.pallas import tpu as pltpu
from jax.sharding import PartitionSpec as P

HALO = 16
C = 32
F32 = jnp.float32
BF16 = jnp.bfloat16
VMEM = pl.BlockSpec(memory_space=pltpu.VMEM)
SMEM = pl.BlockSpec(memory_space=pltpu.SMEM)
PARAMS = pltpu.CompilerParams(vmem_limit_bytes=56 * 1024 * 1024)
CONTRACT_ROWS = (((0,), (0,)), ((), ()))
CONTRACT_LANES = (((1,), (1,)), ((), ()))


def softplus(v):
    small = jnp.exp(-jnp.abs(v))
    tail = jnp.where(small < 1e-4, small, jnp.log(1.0 + small))
    return jnp.maximum(v, 0.0) + tail


def slope(stored):
    return 1.0 - jnp.exp(-stored.astype(F32))


def gated(value, gates):
    rows = value.shape[0]
    return jnp.concatenate(
        [value[:HALO] * gates[0], value[HALO : rows - HALO], value[rows - HALO :] * gates[1]], axis=0
    )


def clear_margins(shifted):
    lanes = shifted.shape[-1]
    edge = jnp.zeros(shifted.shape[:-1] + (128,), BF16)
    shifted[..., 0:128] = edge
    shifted[..., lanes - 128 : lanes] = edge


def store_shifted(shifted, plane, start, value, step):
    rows, lanes = value.shape
    where = slice(128 + start, 128 + start + lanes)
    shifted[plane, 1, :, where] = value.astype(BF16)
    shifted[plane, 0, :, where] = pltpu.roll(value, step, 0).astype(BF16)
    shifted[plane, 2, :, where] = pltpu.roll(value, rows - step, 0).astype(BF16)


def conv_window(shifted, plane, window, band):
    lanes = slice(256 * window, 256 * window + 512)
    total = None
    for tap in range(3):
        term = jnp.dot(
            shifted[plane, tap, :, lanes],
            band[512 * tap : 512 * tap + 512, :],
            preferred_element_type=F32,
        )
        total = term if total is None else total + term
    return total


def windows_of(shifted):
    planes = shifted.shape[0]
    windows = (shifted.shape[-1] - 256) // 256
    return [(plane, window) for plane in range(planes) for window in range(windows)]


def weight_grad(delta, shifted, step, grads, first_piece):
    rows = delta.shape[2]
    own = slice(HALO, rows - HALO)
    for tap in range(3):
        total = None
        for plane, window in windows_of(shifted):
            term = lax.dot_general(
                delta[plane, 1, own, 128 + 256 * window : 384 + 256 * window],
                shifted[plane, tap, own, 256 * window : 256 * window + 512],
                CONTRACT_ROWS,
                preferred_element_type=F32,
            )
            total = term if total is None else total + term
        folded = None
        for r in range(4):
            near = total[32 * r : 32 * r + 32, 0:384]
            far = total[32 * r + 128 : 32 * r + 160, 128:512]
            part = near + far
            if r:
                part = pltpu.roll(part, 384 - 32 * r, 1)
            folded = part if folded is None else folded + part
        for row_tap in range(3):
            at = 32 * (4 + step * (row_tap - 1))
            put_piece(grads, first_piece + 3 * row_tap + tap, folded[:, at : at + 32])


def put_piece(grads, index, value):
    row, lane = 32 * (index // 4), 32 * (index % 4)
    grads[row : row + value.shape[0], lane : lane + 32] = value


def band_kernel(steps, base, *bands):
    lane = lax.broadcasted_iota(jnp.int32, (32, 128), 1) // 32
    for conv, (step, band) in enumerate(zip(steps, bands)):
        for col_tap in range(3):
            blocks = []
            for row_tap in range(3):
                at = 32 * (9 * conv + 3 * row_tap + col_tap)
                blocks.append(base[at : at + 32, :].astype(F32))
            cut = [[jnp.where(lane == q, block, 0.0) for q in range(4)] for block in blocks]
            for source in range(16):
                for group in range(2):
                    panel = None
                    for q in range(4):
                        off = source - 4 - (4 * group + q)
                        if off % step == 0 and abs(off) <= step:
                            term = cut[off // step + 1][q]
                            panel = term if panel is None else panel + term
                    if panel is None:
                        panel = jnp.zeros((32, 128), F32)
                    row = 512 * col_tap + 32 * source
                    band[row : row + 32, 128 * group : 128 * group + 128] = panel.astype(BF16)


def forward_xy_kernel(gate_ref, stem, band_a, band_b, hidden_one, hidden_two, message, stem_s, one_s):
    gates = (gate_ref[0], gate_ref[1])
    clear_margins(stem_s)
    clear_margins(one_s)
    for window in range(4):
        lanes = slice(256 * window, 256 * window + 256)
        store_shifted(stem_s, 0, 256 * window, stem[:, lanes].astype(F32), 1)
    for window in range(4):
        value = gated(softplus(conv_window(stem_s, 0, window, band_a)), gates)
        hidden_one[:, 256 * window : 256 * window + 256] = value.astype(BF16)
        store_shifted(one_s, 0, 256 * window, value, 2)
    for window in range(4):
        value = gated(softplus(conv_window(one_s, 0, window, band_b)), gates).astype(BF16)
        hidden_two[:, 256 * window : 256 * window + 256] = value
        half = value.shape[0] // 2
        for peer in range(4):
            lanes = slice(64 * peer, 64 * peer + 64)
            message[4 * window + peer] = jnp.concatenate(
                [value[:half, lanes], value[half:, lanes]], axis=1
            )


def section_xz_kernel(
    gate_ref, message, labels, head_one, head_two, band_c, band_d, band_dt, band_ct,
    probability, back, grads,
    two_s, ref_one_s, ref_two, delta_two_s, delta_one_s,
):
    gates = (gate_ref[0], gate_ref[1])
    rows = labels.shape[0]
    half = rows // 2
    own = slice(HALO, rows - HALO)
    for shifted in (two_s, ref_one_s, delta_two_s, delta_one_s):
        clear_margins(shifted)
    for plane in range(2):
        for group in range(4):
            parts = []
            for side in range(2):
                at = 64 * side + 32 * plane
                parts.append(
                    jnp.concatenate(
                        [message[4 * group + q][:, at : at + 32] for q in range(4)], axis=1
                    )
                )
            value = jnp.concatenate(parts, axis=0).astype(F32)
            store_shifted(two_s, plane, 128 * group, value, 1)
    for plane, window in windows_of(two_s):
        value = gated(softplus(conv_window(two_s, plane, window, band_c)), gates)
        store_shifted(ref_one_s, plane, 256 * window, value, 2)
    for plane, window in windows_of(two_s):
        value = softplus(conv_window(ref_one_s, plane, window, band_d))
        ref_two[plane, :, 256 * window : 256 * window + 256] = value.astype(BF16)

    voxel = lax.broadcasted_iota(jnp.int32, (32, 1024), 0)
    lane = lax.broadcasted_iota(jnp.int32, (32, 1024), 1) // 32
    same = voxel == lane
    spread_one = jnp.where(same, head_one[...], 0.0).astype(BF16)
    spread_two = jnp.where(same, head_two[...], 0.0).astype(BF16)
    first, second = None, None
    for plane in range(2):
        lanes = slice(512 * plane, 512 * plane + 512)
        one = lax.dot_general(
            two_s[plane, 1, :, 128:640], spread_one[:, lanes], CONTRACT_LANES,
            preferred_element_type=F32,
        )
        two = lax.dot_general(
            ref_two[plane], spread_two[:, lanes], CONTRACT_LANES, preferred_element_type=F32
        )
        first = one if first is None else first + one
        second = two if second is None else second + two
    first = first.astype(BF16).astype(F32)
    second = second + first
    share = 1.0 / (1.0 + jnp.exp(-second))
    probability[...] = share[own]
    error_two = gated(share - labels[...], gates)
    error_one = 1.0 / (1.0 + jnp.exp(-first)) - labels[...] + error_two

    def split(error):
        high = error.astype(BF16)
        low = (error - high.astype(F32)).astype(BF16)
        return jnp.concatenate([high, low], axis=1)

    error_two = split(error_two)
    error_one = split(error_one)
    spread_one = jnp.concatenate([spread_one, spread_one], axis=0)
    spread_two = jnp.concatenate([spread_two, spread_two], axis=0)
    same = jnp.concatenate([same, same], axis=0)

    def head_grad(error, planes):
        total = None
        for plane, feature in enumerate(planes):
            full = lax.dot_general(
                error[own], feature, CONTRACT_ROWS, preferred_element_type=F32
            )
            kept = jnp.where(same[:, 512 * plane : 512 * plane + 512], full, 0.0)
            kept = jnp.sum(kept, axis=0, keepdims=True)
            kept = kept[:, 0:128] + kept[:, 128:256] + kept[:, 256:384] + kept[:, 384:512]
            total = kept if total is None else total + kept
        total = total + pltpu.roll(total, 64, 1)
        total = total + pltpu.roll(total, 32, 1)
        return total[:, 0:32]

    grads[...] = jnp.zeros(grads.shape, F32)
    put_piece(grads, 18, head_grad(error_one, [two_s[plane, 1, own, 128:640] for plane in range(2)]))
    put_piece(grads, 19, head_grad(error_two, [ref_two[plane, own, :] for plane in range(2)]))

    for plane, window in windows_of(two_s):
        at = 256 * window
        lanes = slice(512 * plane + at, 512 * plane + at + 256)
        value = jnp.dot(error_two, spread_two[:, lanes], preferred_element_type=F32)
        value = value * slope(ref_two[plane, :, at : at + 256])
        store_shifted(delta_two_s, plane, at, value, 2)
    weight_grad(delta_two_s, ref_one_s, 2, grads, 9)
    for plane, window in windows_of(two_s):
        at = 256 * window
        value = conv_window(delta_two_s, plane, window, band_dt)
        value = gated(value * slope(ref_one_s[plane, 1, :, 128 + at : 384 + at]), gates)
        store_shifted(delta_one_s, plane, at, value, 1)
    weight_grad(delta_one_s, two_s, 1, grads, 0)
    for window in range(2):
        values = []
        for plane in range(2):
            at = 256 * window
            lanes = slice(512 * plane + at, 512 * plane + at + 256)
            value = conv_window(delta_one_s, plane, window, band_ct)
            value = value + jnp.dot(error_one, spread_one[:, lanes], preferred_element_type=F32)
            values.append(value.astype(BF16))
        for z in range(8):
            lanes = slice(32 * z, 32 * z + 32)
            back[8 * window + z] = jnp.concatenate(
                [
                    values[0][:half, lanes], values[1][:half, lanes],
                    values[0][half:, lanes], values[1][half:, lanes],
                ],
                axis=1,
            )


def backward_xy_kernel(
    gate_ref, back, stem, hidden_one, hidden_two, band_bt, band_at,
    stem_grad, grads,
    stem_s, one_s, delta_b_s, delta_a_s,
):
    gates = (gate_ref[0], gate_ref[1])
    rows = stem.shape[0]
    for shifted in (stem_s, one_s, delta_b_s, delta_a_s):
        clear_margins(shifted)
    for window in range(4):
        lanes = slice(256 * window, 256 * window + 256)
        store_shifted(stem_s, 0, 256 * window, stem[:, lanes].astype(F32), 1)
        store_shifted(one_s, 0, 256 * window, hidden_one[:, lanes].astype(F32), 2)
    for group in range(8):
        parts = []
        for side in range(2):
            at = 64 * side
            parts.append(
                jnp.concatenate(
                    [back[2 * group + q][:, at : at + 64] for q in range(2)], axis=1
                )
            )
        value = jnp.concatenate(parts, axis=0).astype(F32)
        value = gated(value * slope(hidden_two[:, 128 * group : 128 * group + 128]), gates)
        store_shifted(delta_b_s, 0, 128 * group, value, 2)
    grads[...] = jnp.zeros(grads.shape, F32)
    for window in range(4):
        at = 256 * window
        value = conv_window(delta_b_s, 0, window, band_bt)
        value = gated(value * slope(hidden_one[:, at : at + 256]), gates)
        store_shifted(delta_a_s, 0, at, value, 1)
    weight_grad(delta_b_s, one_s, 2, grads, 9)
    weight_grad(delta_a_s, stem_s, 1, grads, 0)
    for window in range(4):
        at = 256 * window
        value = conv_window(delta_a_s, 0, window, band_at)
        stem_grad[:, at : at + 256] = value[HALO : rows - HALO].astype(BF16)


def call(kernel, outs, specs, scratch=(), flops=0):
    return pl.pallas_call(
        kernel,
        out_shape=outs,
        in_specs=specs,
        out_specs=jax.tree.map(lambda _: VMEM, outs),
        scratch_shapes=scratch,
        compiler_params=PARAMS,
        cost_estimate=pl.CostEstimate(flops=flops, bytes_accessed=1 << 20, transcendentals=0),
    )


def shape(dims, dtype):
    return jax.ShapeDtypeStruct(dims, dtype)


def sum_everywhere(grads, slab, gx):
    peers, rows = lax.axis_size(gx), grads.shape[0]
    mine = lax.all_to_all(grads, gx, 0, 0, tiled=True)
    mine = jnp.sum(mine.reshape(peers, rows // peers, 128), axis=0)
    copies = lax.axis_size(slab)
    spread = jnp.broadcast_to(mine[None], (copies,) + mine.shape)
    mine = jnp.sum(lax.all_to_all(spread, slab, 0, 0, tiled=True), axis=0)
    spread = jnp.broadcast_to(mine[None], (peers,) + mine.shape)
    return lax.all_to_all(spread, gx, 0, 0, tiled=True).reshape(rows, 128)


def per_device(stem_features, labels, conv_a, conv_b, conv_c, conv_d, head_one, head_two):
    _, depth, height, cols = stem_features.shape
    rows = cols + 2 * HALO
    half = rows // 2
    peers = lax.axis_size("gx")
    me = lax.axis_index("gx")
    gates = jnp.stack([me > 0, me < peers - 1]).astype(F32)

    weights = jnp.stack([conv_a, conv_b, conv_c, conv_d])
    ahead = jnp.transpose(weights, (0, 2, 3, 4, 1))
    behind = jnp.transpose(weights[:, :, ::-1, ::-1, :], (0, 2, 3, 1, 4))
    base = jnp.concatenate([ahead, behind], axis=0).reshape(8 * 9 * C, C)
    base = jnp.tile(base, (1, 4))
    bands = call(
        functools.partial(band_kernel, (1, 2, 1, 2, 1, 2, 1, 2)),
        [shape((1536, 256), BF16)] * 8,
        [VMEM],
        flops=1 << 28,
    )(base)
    band_a, band_b, band_c, band_d, band_at, band_bt, band_ct, band_dt = bands

    stem = jnp.transpose(stem_features[:, 0], (2, 1, 0)).reshape(cols, height * C)
    marks = jnp.transpose(labels, (2, 1, 0)).reshape(cols, 32).astype(BF16)
    marks = jnp.pad(marks, ((0, 0), (0, 96)))
    both = jnp.concatenate([stem, marks], axis=1)
    up = [(i, i + 1) for i in range(peers - 1)]
    down = [(j, i) for i, j in up]
    before = lax.ppermute(both[cols - HALO :], "gx", up)
    after = lax.ppermute(both[:HALO], "gx", down)
    both = jnp.concatenate([before, both, after], axis=0)
    stem = both[:, : height * C]
    marks = both[:, height * C : height * C + 32].astype(F32)

    wide = pltpu.VMEM((1, 3, rows, 1280), BF16)
    tall = pltpu.VMEM((2, 3, rows, 768), BF16)
    hidden_one, hidden_two, message = call(
        forward_xy_kernel,
        [shape((rows, 1024), BF16), shape((rows, 1024), BF16), shape((16, half, 128), BF16)],
        [SMEM] + [VMEM] * 3,
        [wide, wide],
        flops=1 << 30,
    )(gates, stem, band_a, band_b)
    message = lax.all_to_all(message, "slab", 0, 0, tiled=True)
    tile_one = jnp.tile(head_one.astype(F32), 32)[None]
    tile_two = jnp.tile(head_two.astype(F32), 32)[None]
    probability, back, grads_cd = call(
        section_xz_kernel,
        [shape((cols, 32), F32), shape((16, half, 128), BF16), shape((160, 128), F32)],
        [SMEM] + [VMEM] * 8,
        [tall, tall, pltpu.VMEM((2, rows, 512), BF16), tall, tall],
        flops=1 << 31,
    )(gates, message, marks, tile_one, tile_two, band_c, band_d, band_dt, band_ct)
    back = lax.all_to_all(back, "slab", 0, 0, tiled=True)
    stem_grad, grads_ab = call(
        backward_xy_kernel,
        [shape((cols, 1024), BF16), shape((160, 128), F32)],
        [SMEM] + [VMEM] * 6,
        [wide, wide, wide, wide],
        flops=1 << 31,
    )(gates, back, stem, hidden_one, hidden_two, band_bt, band_at)

    stem_grad = jnp.transpose(stem_grad.reshape(cols, height, C), (2, 1, 0))[:, None]
    probability = jnp.transpose(probability.reshape(cols, 2, 16), (2, 1, 0))

    factor = 1.0 / (depth * height * cols)
    total = sum_everywhere(jnp.concatenate([grads_ab, grads_cd], axis=0), "slab", "gx") * factor
    pieces = total.reshape(2, 5, 32, 4, 32).transpose(0, 1, 3, 2, 4).reshape(2, 20, 32, 32)

    def kernel_grad(pair, first):
        taken = pieces[pair, first : first + 9].reshape(3, 3, 32, 32)
        return jnp.transpose(taken, (2, 0, 1, 3))

    return (
        probability,
        stem_grad,
        kernel_grad(0, 0),
        kernel_grad(0, 9),
        kernel_grad(1, 0),
        kernel_grad(1, 9),
        pieces[1, 18, 0],
        pieces[1, 19, 0],
    )


def solution(mesh):
    return jax.shard_map(
        per_device,
        mesh=mesh,
        in_specs=(P(None, "slab", None, "gx"), P(None, "slab", "gx"), P(), P(), P(), P(), P(), P()),
        out_specs=(
            P(None, "slab", "gx"),
            P(None, "slab", None, "gx"),
            P(),
            P(),
            P(),
            P(),
            P(),
            P(),
        ),
        check_vma=False,
    )
```

```python
import functools

import jax
import jax.numpy as jnp
from jax import lax
from jax.experimental import pallas as pl
from jax.experimental.pallas import tpu as pltpu
from jax.sharding import PartitionSpec as P

HALO = 16
C = 32
F32 = jnp.float32
BF16 = jnp.bfloat16
VMEM = pl.BlockSpec(memory_space=pltpu.VMEM)
CONTRACT_ROWS = (((0,), (0,)), ((), ()))
CONTRACT_LANES = (((1,), (1,)), ((), ()))


def softplus(v):
    small = jnp.exp(-jnp.abs(v))
    tail = jnp.where(small < 1e-4, small, jnp.log(1.0 + small))
    return jnp.maximum(v, 0.0) + tail


def slope(stored):
    return 1.0 - jnp.exp(-stored.astype(F32))


def edge_gates():
    me, peers = lax.axis_index("gx"), lax.axis_size("gx")
    return jnp.where(me > 0, 1.0, 0.0), jnp.where(me < peers - 1, 1.0, 0.0)


def gated(value, gates):
    rows = value.shape[0]
    return jnp.concatenate(
        [value[:HALO] * gates[0], value[HALO : rows - HALO], value[rows - HALO :] * gates[1]], axis=0
    )


def clear_margins(shifted):
    lanes = shifted.shape[-1]
    edge = jnp.zeros(shifted.shape[:-1] + (128,), BF16)
    shifted[..., 0:128] = edge
    shifted[..., lanes - 128 : lanes] = edge


def store_shifted(shifted, plane, start, value, step):
    rows, lanes = value.shape
    where = slice(128 + start, 128 + start + lanes)
    shifted[plane, 1, :, where] = value.astype(BF16)
    shifted[plane, 0, :, where] = pltpu.roll(value, step, 0).astype(BF16)
    shifted[plane, 2, :, where] = pltpu.roll(value, rows - step, 0).astype(BF16)


def conv_window(shifted, plane, window, band):
    lanes = slice(256 * window, 256 * window + 512)
    total = None
    for tap in range(3):
        term = jnp.dot(
            shifted[plane, tap, :, lanes],
            band[512 * tap : 512 * tap + 512, :],
            preferred_element_type=F32,
        )
        total = term if total is None else total + term
    return total


def windows_of(shifted):
    planes = shifted.shape[0]
    windows = (shifted.shape[-1] - 256) // 256
    return [(plane, window) for plane in range(planes) for window in range(windows)]


def weight_grad(delta, shifted, step, grads, first_piece):
    rows = delta.shape[1]
    own = slice(HALO, rows - HALO)
    for tap in range(3):
        total = None
        for plane, window in windows_of(shifted):
            term = lax.dot_general(
                delta[plane, own, 256 * window : 256 * window + 256],
                shifted[plane, tap, own, 256 * window : 256 * window + 512],
                CONTRACT_ROWS,
                preferred_element_type=F32,
            )
            total = term if total is None else total + term
        folded = None
        for r in range(4):
            near = total[32 * r : 32 * r + 32, 0:384]
            far = total[32 * r + 128 : 32 * r + 160, 128:512]
            part = near + far
            if r:
                part = pltpu.roll(part, 384 - 32 * r, 1)
            folded = part if folded is None else folded + part
        for row_tap in range(3):
            at = 32 * (4 + step * (row_tap - 1))
            put_piece(grads, first_piece + 3 * row_tap + tap, folded[:, at : at + 32])


def put_piece(grads, index, value):
    row, lane = 32 * (index // 4), 32 * (index % 4)
    grads[row : row + value.shape[0], lane : lane + 32] = value


def band_kernel(plans, *refs):
    weights, bands = refs[: len(plans)], refs[len(plans) :]
    lane = lax.broadcasted_iota(jnp.int32, (32, 128), 1) // 32
    for (step, backward), weight, band in zip(plans, weights, bands):
        for col_tap in range(3):
            cut = []
            for row_tap in range(3):
                if backward:
                    block = weight[2 - row_tap, 2 - col_tap].astype(F32)
                else:
                    block = weight[row_tap, col_tap].astype(F32).T
                block = jnp.concatenate([block] * 4, axis=1)
                cut.append([jnp.where(lane == q, block, 0.0) for q in range(4)])
            for source in range(16):
                for group in range(2):
                    panel = None
                    for q in range(4):
                        off = source - 4 - (4 * group + q)
                        if off % step == 0 and abs(off) <= step:
                            term = cut[off // step + 1][q]
                            panel = term if panel is None else panel + term
                    if panel is None:
                        panel = jnp.zeros((32, 128), F32)
                    row = 512 * col_tap + 32 * source
                    band[row : row + 32, 128 * group : 128 * group + 128] = panel.astype(BF16)


def load_stem(before, stem, after, stem_s):
    for window in range(4):
        lanes = slice(256 * window, 256 * window + 256)
        value = jnp.concatenate([before[:, lanes], stem[:, lanes], after[:, lanes]], axis=0)
        store_shifted(stem_s, 0, 256 * window, value.astype(F32), 1)


def forward_xy_kernel(
    before, stem, after, band_a, band_b, hidden_one, hidden_two, message, stem_s, one_s
):
    gates = edge_gates()
    clear_margins(stem_s)
    clear_margins(one_s)
    load_stem(before, stem, after, stem_s)
    for window in range(4):
        value = gated(softplus(conv_window(stem_s, 0, window, band_a)), gates)
        hidden_one[:, 256 * window : 256 * window + 256] = value.astype(BF16)
        store_shifted(one_s, 0, 256 * window, value, 2)
    for window in range(4):
        value = gated(softplus(conv_window(one_s, 0, window, band_b)), gates).astype(BF16)
        hidden_two[:, 256 * window : 256 * window + 256] = value
        half = value.shape[0] // 2
        for peer in range(4):
            lanes = slice(64 * peer, 64 * peer + 64)
            message[4 * window + peer] = jnp.concatenate(
                [value[:half, lanes], value[half:, lanes]], axis=1
            )


def load_features(message, two_s):
    for plane in range(2):
        for group in range(4):
            parts = []
            for side in range(2):
                at = 64 * side + 32 * plane
                parts.append(
                    jnp.concatenate(
                        [message[4 * group + q][:, at : at + 32] for q in range(4)], axis=1
                    )
                )
            value = jnp.concatenate(parts, axis=0).astype(F32)
            store_shifted(two_s, plane, 128 * group, value, 1)


def own_voxel():
    voxel = lax.broadcasted_iota(jnp.int32, (32, 1024), 0)
    return voxel == lax.broadcasted_iota(jnp.int32, (32, 1024), 1) // 32


def split(error):
    high = error.astype(BF16)
    low = (error - high.astype(F32)).astype(BF16)
    return jnp.concatenate([high, low], axis=1)


def section_xz_kernel(
    message, labels, head_one, head_two, band_c, band_d, band_dt, band_ct,
    probability, back, ref_one, ref_two, delta_two, delta_one, errors_one, errors_two,
    two_s, ref_one_s, delta_two_s, delta_one_s,
):
    gates = edge_gates()
    rows = labels.shape[0]
    half = rows // 2
    own = slice(HALO, rows - HALO)
    for shifted in (two_s, ref_one_s, delta_two_s, delta_one_s):
        clear_margins(shifted)
    load_features(message, two_s)
    for plane, window in windows_of(two_s):
        at = 256 * window
        value = gated(softplus(conv_window(two_s, plane, window, band_c)), gates)
        ref_one[plane, :, at : at + 256] = value.astype(BF16)
        store_shifted(ref_one_s, plane, at, value, 2)
    for plane, window in windows_of(two_s):
        value = softplus(conv_window(ref_one_s, plane, window, band_d))
        ref_two[plane, :, 256 * window : 256 * window + 256] = value.astype(BF16)

    same = own_voxel()
    spread_one = jnp.where(same, head_one[...], 0.0).astype(BF16)
    spread_two = jnp.where(same, head_two[...], 0.0).astype(BF16)
    first, second = None, None
    for plane in range(2):
        lanes = slice(512 * plane, 512 * plane + 512)
        one = lax.dot_general(
            two_s[plane, 1, :, 128:640], spread_one[:, lanes], CONTRACT_LANES,
            preferred_element_type=F32,
        )
        two = lax.dot_general(
            ref_two[plane], spread_two[:, lanes], CONTRACT_LANES, preferred_element_type=F32
        )
        first = one if first is None else first + one
        second = two if second is None else second + two
    first = first.astype(BF16).astype(F32)
    second = second + first
    share = 1.0 / (1.0 + jnp.exp(-second))
    probability[...] = share[own]
    error_two = gated(share - labels[...], gates)
    error_one = 1.0 / (1.0 + jnp.exp(-first)) - labels[...] + error_two
    error_two = split(error_two)
    error_one = split(error_one)
    errors_one[...] = error_one
    errors_two[...] = error_two
    spread_one = jnp.concatenate([spread_one, spread_one], axis=0)
    spread_two = jnp.concatenate([spread_two, spread_two], axis=0)

    for plane, window in windows_of(two_s):
        at = 256 * window
        lanes = slice(512 * plane + at, 512 * plane + at + 256)
        value = jnp.dot(error_two, spread_two[:, lanes], preferred_element_type=F32)
        value = value * slope(ref_two[plane, :, at : at + 256])
        delta_two[plane, :, at : at + 256] = value.astype(BF16)
        store_shifted(delta_two_s, plane, at, value, 2)
    for plane, window in windows_of(two_s):
        at = 256 * window
        value = conv_window(delta_two_s, plane, window, band_dt)
        value = gated(value * slope(ref_one[plane, :, at : at + 256]), gates)
        delta_one[plane, :, at : at + 256] = value.astype(BF16)
        store_shifted(delta_one_s, plane, at, value, 1)
    for window in range(2):
        values = []
        for plane in range(2):
            at = 256 * window
            lanes = slice(512 * plane + at, 512 * plane + at + 256)
            value = conv_window(delta_one_s, plane, window, band_ct)
            value = value + jnp.dot(error_one, spread_one[:, lanes], preferred_element_type=F32)
            values.append(value.astype(BF16))
        for z in range(8):
            lanes = slice(32 * z, 32 * z + 32)
            back[8 * window + z] = jnp.concatenate(
                [
                    values[0][:half, lanes], values[1][:half, lanes],
                    values[0][half:, lanes], values[1][half:, lanes],
                ],
                axis=1,
            )


def section_grads_kernel(
    message, ref_one, ref_two, delta_two, delta_one, errors_one, errors_two,
    grads_out, two_s, ref_one_s, grads,
):
    rows = errors_one.shape[0]
    own = slice(HALO, rows - HALO)
    same = own_voxel()
    same = jnp.concatenate([same, same], axis=0)
    clear_margins(two_s)
    clear_margins(ref_one_s)
    load_features(message, two_s)
    for plane, window in windows_of(two_s):
        at = 256 * window
        value = ref_one[plane, :, at : at + 256].astype(F32)
        store_shifted(ref_one_s, plane, at, value, 2)

    def head_grad(error, planes):
        total = None
        for plane, feature in enumerate(planes):
            full = lax.dot_general(
                error[own, :], feature, CONTRACT_ROWS, preferred_element_type=F32
            )
            kept = jnp.where(same[:, 512 * plane : 512 * plane + 512], full, 0.0)
            kept = jnp.sum(kept, axis=0, keepdims=True)
            kept = kept[:, 0:128] + kept[:, 128:256] + kept[:, 256:384] + kept[:, 384:512]
            total = kept if total is None else total + kept
        total = total + pltpu.roll(total, 64, 1)
        total = total + pltpu.roll(total, 32, 1)
        return total[:, 0:32]

    grads[...] = jnp.zeros(grads.shape, F32)
    features = [two_s[plane, 1, own, 128:640] for plane in range(2)]
    put_piece(grads, 18, head_grad(errors_one, features))
    put_piece(grads, 19, head_grad(errors_two, [ref_two[plane, own, :] for plane in range(2)]))
    weight_grad(delta_two, ref_one_s, 2, grads, 9)
    weight_grad(delta_one, two_s, 1, grads, 0)
    grads_out[...] = grads[...].astype(BF16)


def backward_xy_kernel(
    back, before, stem, after, hidden_one, hidden_two, band_bt, grads_cd,
    delta_a, grads_out,
    stem_s, one_s, delta_b_s, delta_b, grads,
):
    gates = edge_gates()
    for shifted in (stem_s, one_s, delta_b_s):
        clear_margins(shifted)
    load_stem(before, stem, after, stem_s)
    for window in range(4):
        lanes = slice(256 * window, 256 * window + 256)
        store_shifted(one_s, 0, 256 * window, hidden_one[:, lanes].astype(F32), 2)
    for group in range(8):
        parts = []
        for side in range(2):
            at = 64 * side
            parts.append(
                jnp.concatenate(
                    [back[2 * group + q][:, at : at + 64] for q in range(2)], axis=1
                )
            )
        lanes = slice(128 * group, 128 * group + 128)
        value = jnp.concatenate(parts, axis=0).astype(F32)
        value = gated(value * slope(hidden_two[:, lanes]), gates)
        delta_b[0, :, lanes] = value.astype(BF16)
        store_shifted(delta_b_s, 0, 128 * group, value, 2)
    grads[...] = jnp.zeros(grads.shape, F32)
    for window in range(4):
        at = 256 * window
        value = conv_window(delta_b_s, 0, window, band_bt)
        value = gated(value * slope(hidden_one[:, at : at + 256]), gates)
        delta_a[0, :, at : at + 256] = value.astype(BF16)
    weight_grad(delta_b, one_s, 2, grads, 9)
    weight_grad(delta_a, stem_s, 1, grads, 0)
    for peer in range(8):
        grads_out[peer] = grads[20 * peer : 20 * peer + 20, :].astype(BF16)
        grads_out[8 + peer] = grads_cd[20 * peer : 20 * peer + 20, :]


def stem_grad_kernel(delta_a, band_at, stem_grad, delta_a_s):
    rows = delta_a.shape[1]
    clear_margins(delta_a_s)
    for window in range(4):
        lanes = slice(256 * window, 256 * window + 256)
        store_shifted(delta_a_s, 0, 256 * window, delta_a[0, :, lanes].astype(F32), 1)
    for window in range(4):
        at = 256 * window
        value = conv_window(delta_a_s, 0, window, band_at)
        stem_grad[:, at : at + 256] = value[HALO : rows - HALO].astype(BF16)


def finish_kernel(factor, total, grad_a, grad_b, grad_c, grad_d, head_one, head_two):
    flat = total[...].reshape(320, 128) * factor

    def piece(pair, index):
        row, lane = 160 * pair + 32 * (index // 4), 32 * (index % 4)
        return flat[row : row + 32, lane : lane + 32]

    for pair, (near, far) in enumerate(((grad_a, grad_b), (grad_c, grad_d))):
        for tap in range(9):
            near[tap // 3, tap % 3] = piece(pair, tap)
            far[tap // 3, tap % 3] = piece(pair, 9 + tap)
    head_one[...] = piece(1, 18)[0:1]
    head_two[...] = piece(1, 19)[0:1]


def call(kernel, outs, count, scratch=(), flops=0, megabytes=16):
    return pl.pallas_call(
        kernel,
        out_shape=outs,
        in_specs=[VMEM] * count,
        out_specs=jax.tree.map(lambda _: VMEM, outs),
        scratch_shapes=scratch,
        compiler_params=pltpu.CompilerParams(vmem_limit_bytes=megabytes * 1024 * 1024),
        cost_estimate=pl.CostEstimate(flops=flops, bytes_accessed=1 << 20, transcendentals=0),
    )


def shape(dims, dtype):
    return jax.ShapeDtypeStruct(dims, dtype)


def sum_everywhere(grads, slab, gx):
    peers, copies = lax.axis_size(gx), lax.axis_size(slab)
    mine = lax.all_to_all(grads, gx, 0, 0, tiled=True)
    mine = jnp.sum(mine.astype(F32), axis=0)
    spread = jnp.broadcast_to(mine[None], (copies,) + mine.shape)
    mine = jnp.sum(lax.all_to_all(spread, slab, 0, 0, tiled=True), axis=0)
    spread = jnp.broadcast_to(mine[None], (peers,) + mine.shape)
    return lax.all_to_all(spread, gx, 0, 0, tiled=True)


def per_device(stem_features, labels, conv_a, conv_b, conv_c, conv_d, head_one, head_two):
    _, depth, height, cols = stem_features.shape
    rows = cols + 2 * HALO
    half = rows // 2
    peers = lax.axis_size("gx")
    up = [(i, i + 1) for i in range(peers - 1)]
    down = [(j, i) for i, j in up]

    def columns_first(part):
        return jnp.transpose(part, (2, 1, 0)).reshape(part.shape[2], -1)

    slab = stem_features[:, 0]
    last = columns_first(slab[:, :, cols - HALO :])
    initial = columns_first(slab[:, :, :HALO])
    before = lax.ppermute(last, "gx", up)
    after = lax.ppermute(initial, "gx", down)
    stem = columns_first(slab)

    weights = [jnp.transpose(w, (1, 2, 0, 3)) for w in (conv_a, conv_b, conv_c, conv_d)]
    band = shape((1536, 256), BF16)
    band_a, band_b = call(
        functools.partial(band_kernel, ((1, False), (2, False))),
        [band] * 2, 2, flops=1 << 29, megabytes=8,
    )(*weights[:2])

    wide = pltpu.VMEM((1, 3, rows, 1280), BF16)
    tall = pltpu.VMEM((2, 3, rows, 768), BF16)
    whole = shape((rows, 1024), BF16)
    sections = shape((2, rows, 512), BF16)
    hidden_one, hidden_two, message = call(
        forward_xy_kernel,
        [whole, whole, shape((16, half, 128), BF16)],
        5, [wide, wide], flops=1 << 30, megabytes=16,
    )(before, stem, after, band_a, band_b)

    message, labels, weights, head_one, head_two = lax.optimization_barrier(
        (message, labels, weights, head_one, head_two)
    )
    message = lax.all_to_all(message, "slab", 0, 0, tiled=True)
    marks = columns_first(labels).astype(F32)
    marks_before = lax.ppermute(marks[cols - HALO :], "gx", up)
    marks_after = lax.ppermute(marks[:HALO], "gx", down)
    marks = jnp.concatenate([marks_before, marks, marks_after], axis=0)
    band_c, band_d, band_ct, band_dt, band_bt, band_at = call(
        functools.partial(
            band_kernel,
            ((1, False), (2, False), (1, True), (2, True), (2, True), (1, True)),
        ),
        [band] * 6, 6, flops=1 << 31, megabytes=8,
    )(weights[2], weights[3], weights[2], weights[3], weights[1], weights[0])
    tile_one = jnp.tile(head_one.astype(F32), 32)[None]
    tile_two = jnp.tile(head_two.astype(F32), 32)[None]

    pairs = shape((rows, 64), BF16)
    probability, back, ref_one, ref_two, delta_two, delta_one, errors_one, errors_two = call(
        section_xz_kernel,
        [shape((cols, 32), F32), shape((16, half, 128), BF16)] + [sections] * 4 + [pairs] * 2,
        8, [tall, tall, tall, tall], flops=1 << 31, megabytes=24,
    )(message, marks, tile_one, tile_two, band_c, band_d, band_dt, band_ct)
    back = lax.all_to_all(back, "slab", 0, 0, tiled=True)
    grads_cd = call(
        section_grads_kernel,
        shape((160, 128), BF16),
        7, [tall, tall, pltpu.VMEM((160, 128), F32)], flops=1 << 31, megabytes=16,
    )(message, ref_one, ref_two, delta_two, delta_one, errors_one, errors_two)

    delta_a, grads = call(
        backward_xy_kernel,
        [shape((1, rows, 1024), BF16), shape((16, 20, 128), BF16)],
        8,
        [wide, wide, wide, pltpu.VMEM((1, rows, 1024), BF16), pltpu.VMEM((160, 128), F32)],
        flops=1 << 31, megabytes=24,
    )(back, before, stem, after, hidden_one, hidden_two, band_bt, grads_cd)
    stem_grad = call(
        stem_grad_kernel,
        shape((cols, 1024), BF16),
        2, [wide], flops=1 << 30, megabytes=12,
    )(delta_a, band_at)
    stem_grad = jnp.transpose(stem_grad.reshape(cols, height, C), (2, 1, 0))[:, None]
    probability = jnp.transpose(probability.reshape(cols, 2, 16), (2, 1, 0))

    total = sum_everywhere(grads, "slab", "gx")
    taps = shape((3, 3, C, C), F32)
    finals = call(
        functools.partial(finish_kernel, 1.0 / (depth * height * cols)),
        [taps] * 4 + [shape((1, C), F32)] * 2,
        1, flops=1 << 20, megabytes=8,
    )(total)
    kernels = [jnp.transpose(grad, (2, 0, 1, 3)) for grad in finals[:4]]
    return (probability, stem_grad, *kernels, finals[4][0], finals[5][0])


def solution(mesh):
    return jax.shard_map(
        per_device,
        mesh=mesh,
        in_specs=(P(None, "slab", None, "gx"), P(None, "slab", "gx"), P(), P(), P(), P(), P(), P()),
        out_specs=(
            P(None, "slab", "gx"),
            P(None, "slab", None, "gx"),
            P(),
            P(),
            P(),
            P(),
            P(),
            P(),
        ),
        check_vma=False,
    )
```

```python
import functools

import jax
import jax.numpy as jnp
from jax import lax
from jax.experimental import pallas as pl
from jax.experimental.pallas import tpu as pltpu
from jax.sharding import PartitionSpec as P

HALO = 32
LEFT = 16
C = 32
F32 = jnp.float32
BF16 = jnp.bfloat16
VMEM = pl.BlockSpec(memory_space=pltpu.VMEM)
HBM = pl.BlockSpec(memory_space=pltpu.HBM)
CONTRACT_ROWS = (((0,), (0,)), ((), ()))
CONTRACT_LANES = (((1,), (1,)), ((), ()))


def softplus(v):
    small = jnp.exp(-jnp.abs(v))
    tail = jnp.where(small < 1e-4, small, jnp.log(1.0 + small))
    return jnp.maximum(v, 0.0) + tail


def slope(stored):
    return 1.0 - jnp.exp(-stored.astype(F32))


def edge_gates():
    me, peers = lax.axis_index("gx"), lax.axis_size("gx")
    return jnp.where(me > 0, 0.0, 1.0), jnp.where(me < peers - 1, 1.0, 0.0)


def gated(value, inside):
    cols = value.shape[0] - HALO
    return jnp.concatenate([value[:cols], value[cols:] * inside], axis=0)


def clear_margins(shifted):
    lanes = shifted.shape[-1]
    edge = jnp.zeros(shifted.shape[:-1] + (128,), BF16)
    shifted[..., 0:128] = edge
    shifted[..., lanes - 128 : lanes] = edge


def store_shifted(shifted, plane, start, value, step):
    rows, lanes = value.shape
    where = slice(128 + start, 128 + start + lanes)
    shifted[plane, 1, :, where] = value.astype(BF16)
    lower = pltpu.roll(value, step, 0)
    row = lax.broadcasted_iota(jnp.int32, (8, lanes), 0)
    lower = jnp.concatenate([jnp.where(row < step, 0.0, lower[:8]), lower[8:]], axis=0)
    shifted[plane, 0, :, where] = lower.astype(BF16)
    shifted[plane, 2, :, where] = pltpu.roll(value, rows - step, 0).astype(BF16)


def conv_window(shifted, plane, window, band):
    lanes = slice(256 * window, 256 * window + 512)
    total = None
    for tap in range(3):
        term = jnp.dot(
            shifted[plane, tap, :, lanes],
            band[512 * tap : 512 * tap + 512, :],
            preferred_element_type=F32,
        )
        total = term if total is None else total + term
    return total


def windows_of(shifted):
    planes = shifted.shape[0]
    windows = (shifted.shape[-1] - 256) // 256
    return [(plane, window) for plane in range(planes) for window in range(windows)]


def weight_grad(delta, shifted, step, grads, first_piece, first):
    own = slice(LEFT, delta.shape[1] - LEFT)
    places = windows_of(shifted)
    head = jnp.concatenate(
        [delta[plane, :LEFT, 256 * window : 256 * window + 256] for plane, window in places], axis=0
    )
    head = (head.astype(F32) * first).astype(BF16)
    for tap in range(3):
        total = lax.dot_general(
            head,
            jnp.concatenate(
                [
                    shifted[plane, tap, :LEFT, 256 * window : 256 * window + 512]
                    for plane, window in places
                ],
                axis=0,
            ),
            CONTRACT_ROWS,
            preferred_element_type=F32,
        )
        for plane, window in places:
            total = total + lax.dot_general(
                delta[plane, own, 256 * window : 256 * window + 256],
                shifted[plane, tap, own, 256 * window : 256 * window + 512],
                CONTRACT_ROWS,
                preferred_element_type=F32,
            )
        folded = None
        for r in range(4):
            near = total[32 * r : 32 * r + 32, 0:384]
            far = total[32 * r + 128 : 32 * r + 160, 128:512]
            part = near + far
            if r:
                part = pltpu.roll(part, 384 - 32 * r, 1)
            folded = part if folded is None else folded + part
        for row_tap in range(3):
            at = 32 * (4 + step * (row_tap - 1))
            put_piece(grads, first_piece + 3 * row_tap + tap, folded[:, at : at + 32])


def put_piece(grads, index, value):
    row, lane = 32 * (index // 4), 32 * (index % 4)
    grads[row : row + value.shape[0], lane : lane + 32] = value


def fill_tap(weight, band, step, backward, col_tap):
    lane = lax.broadcasted_iota(jnp.int32, (32, 128), 1) // 32
    cut = []
    for row_tap in range(3):
        if backward:
            block = weight[2 - row_tap, 2 - col_tap].astype(F32)
        else:
            block = weight[row_tap, col_tap].astype(F32).T
        block = jnp.concatenate([block] * 4, axis=1)
        cut.append([jnp.where(lane == q, block, 0.0) for q in range(4)])
    for source in range(16):
        for group in range(2):
            panel = None
            for q in range(4):
                off = source - 4 - (4 * group + q)
                if off % step == 0 and abs(off) <= step:
                    term = cut[off // step + 1][q]
                    panel = term if panel is None else panel + term
            if panel is None:
                panel = jnp.zeros((32, 128), F32)
            row = 512 * col_tap + 32 * source
            band[row : row + 32, 128 * group : 128 * group + 128] = panel.astype(BF16)


def fill_band(weight, band, step, backward):
    for col_tap in range(3):
        fill_tap(weight, band, step, backward, col_tap)


class Copies:
    def __init__(self, sems):
        self.sems, self.started = sems, []

    def start(self, source, target):
        copy = pltpu.make_async_copy(source, target, self.sems.at[len(self.started)])
        copy.start()
        self.started.append(copy)
        return copy

    def start_lanes(self, source, target, parts):
        size = source.shape[-1] // parts
        return [
            self.start(
                source.at[..., pl.ds(size * k, size)], target.at[..., pl.ds(size * k, size)]
            )
            for k in range(parts)
        ]


def wait_all(copies):
    for copy in copies:
        copy.wait()


def centre(shifted):
    return shifted.at[:, 1, :, pl.ds(128, shifted.shape[-1] - 256)]


def arrange_kernel(stem_in, labels_in, stem_out, marks_out, initial, flat, stem, labels, sems):
    cols = stem.shape[2]
    copies = Copies(sems)
    for k in range(4):
        rows = pl.ds(8 * k, 8)
        copies.start(stem_in.at[rows], stem.at[rows])
    labels_here = copies.start(labels_in, labels)
    wait_all(copies.started[:4])
    for side in range(cols // 128):
        part = stem[:, :, 128 * side : 128 * side + 128].reshape(1024, 128)
        flat[1024 * side : 1024 * side + 1024, :] = part.astype(F32)
    for group in range(8):
        sides = []
        for side in range(cols // 128):
            first = 1024 * side + 4 * group
            rows = [flat[pl.ds(first + k, 32, stride=32), :] for k in range(4)]
            sides.append(jnp.concatenate(rows, axis=0).T)
        lanes = slice(128 * group, 128 * group + 128)
        value = jnp.concatenate(sides, axis=0).astype(BF16)
        stem_out[:, lanes] = value
        initial[:, lanes] = value[:HALO]
    labels_here.wait()
    marks = labels[...].astype(F32)
    marks = jnp.concatenate([marks[:, 0, :], marks[:, 1, :], jnp.zeros((96, cols), F32)], axis=0)
    marks = marks.T.astype(BF16)
    marks_out[...] = marks
    initial[:, 1024:1152] = marks[:HALO]


def own_voxel():
    voxel = lax.broadcasted_iota(jnp.int32, (32, 1024), 0)
    return voxel == lax.broadcasted_iota(jnp.int32, (32, 1024), 1) // 32


def first_bands_kernel(conv_a, conv_b, head_one, head_two, band_a, band_b, spread_out, spread, sems):
    same = own_voxel()
    for k, head in enumerate((head_one, head_two)):
        four = jnp.concatenate([head[...].astype(F32)] * 4, axis=1)
        along = jnp.concatenate([four] * 8, axis=1)
        spread[32 * k : 32 * k + 32, :] = jnp.where(same, along, 0.0).astype(BF16)
    copies = Copies(sems)
    copies.start(spread, spread_out)
    fill_band(conv_a, band_a, 1, False)
    fill_band(conv_b, band_b, 2, False)
    wait_all(copies.started)


def forward_xy_kernel(
    stem, marks, after, band_a, band_b,
    stem_frame, hidden_one, hidden_two, marks_out, message,
    stem_s, one_s, two, packed, sems,
):
    _, inside = edge_gates()
    copies = Copies(sems)
    clear_margins(stem_s)
    clear_margins(one_s)
    for window in range(4):
        lanes = slice(256 * window, 256 * window + 256)
        value = jnp.concatenate([stem[:, lanes], after[:, lanes]], axis=0)
        store_shifted(stem_s, 0, 256 * window, value.astype(F32), 1)
    copies.start(centre(stem_s), stem_frame)
    marks_out[...] = jnp.concatenate([marks[...], after[:, 1024:1152]], axis=0)
    for window in range(4):
        value = gated(softplus(conv_window(stem_s, 0, window, band_a)), inside)
        store_shifted(one_s, 0, 256 * window, value, 2)
    copies.start(centre(one_s), hidden_one)
    for window in range(4):
        value = gated(softplus(conv_window(one_s, 0, window, band_b)), inside).astype(BF16)
        lanes = pl.ds(256 * window, 256)
        two[0, :, lanes] = value
        copies.start(two.at[:, :, lanes], hidden_two.at[:, :, lanes])
        half = value.shape[0] // 2
        for peer in range(4):
            lanes = slice(64 * peer, 64 * peer + 64)
            packed[4 * window + peer] = jnp.concatenate(
                [value[:half, lanes], value[half:, lanes]], axis=1
            )
        peers = pl.ds(4 * window, 4)
        copies.start(packed.at[peers], message.at[peers])
    wait_all(copies.started)


def load_features(message, two_s):
    for plane in range(2):
        for group in range(4):
            parts = []
            for side in range(2):
                at = 64 * side + 32 * plane
                parts.append(
                    jnp.concatenate(
                        [message[4 * group + q][:, at : at + 32] for q in range(4)], axis=1
                    )
                )
            value = jnp.concatenate(parts, axis=0).astype(F32)
            store_shifted(two_s, plane, 128 * group, value, 1)


def split(error):
    high = error.astype(BF16)
    low = (error - high.astype(F32)).astype(BF16)
    return jnp.concatenate([high, low], axis=1)


def section_xz_kernel(
    message, marks, conv_c, conv_d, spread_in,
    probability, errors_one, errors_two, back, ref_one_out, ref_two_out, delta_two_out, delta_one_out,
    two_s, ref_one_s, delta_two_s, delta_one_s, ref_two, packed, bands, spread, sems,
):
    _, inside = edge_gates()
    copies = Copies(sems)
    spread_here = copies.start(spread_in, spread)
    band_c, band_d, band_dt, band_ct = [bands.at[k] for k in range(4)]
    rows = marks.shape[0]
    half = rows // 2
    for shifted in (two_s, ref_one_s, delta_two_s, delta_one_s):
        clear_margins(shifted)
    places = windows_of(two_s)
    fill_band(conv_c, band_c, 1, False)
    load_features(message, two_s)
    for plane, window in places:
        value = gated(softplus(conv_window(two_s, plane, window, band_c)), inside)
        store_shifted(ref_one_s, plane, 256 * window, value, 2)
    copies.start(centre(ref_one_s), ref_one_out)
    fill_band(conv_d, band_d, 2, False)
    for plane, window in places:
        value = softplus(conv_window(ref_one_s, plane, window, band_d))
        ref_two[plane, :, 256 * window : 256 * window + 256] = value.astype(BF16)
    copies.start(ref_two, ref_two_out)
    fill_band(conv_d, band_dt, 2, True)

    labels = marks[:, 0:32].astype(F32)
    spread_here.wait()
    spread_one, spread_two = spread[0:32, :], spread[32:64, :]
    first, second = None, None
    for plane in range(2):
        lanes = slice(512 * plane, 512 * plane + 512)
        one = lax.dot_general(
            two_s[plane, 1, :, 128:640], spread_one[:, lanes], CONTRACT_LANES,
            preferred_element_type=F32,
        )
        two = lax.dot_general(
            ref_two[plane], spread_two[:, lanes], CONTRACT_LANES, preferred_element_type=F32
        )
        first = one if first is None else first + one
        second = two if second is None else second + two
    first = first.astype(BF16).astype(F32)
    second = second + first
    share = 1.0 / (1.0 + jnp.exp(-second))
    probability[...] = share[: rows - LEFT]
    error_two = gated(share - labels, inside)
    error_one = 1.0 / (1.0 + jnp.exp(-first)) - labels + error_two
    error_two = split(error_two)
    error_one = split(error_one)
    errors_one[...] = error_one
    errors_two[...] = error_two
    spread_one = jnp.concatenate([spread_one, spread_one], axis=0)
    spread_two = jnp.concatenate([spread_two, spread_two], axis=0)

    for plane, window in places:
        at = 256 * window
        lanes = slice(512 * plane + at, 512 * plane + at + 256)
        value = jnp.dot(error_two, spread_two[:, lanes], preferred_element_type=F32)
        value = value * slope(ref_two[plane, :, at : at + 256])
        store_shifted(delta_two_s, plane, at, value, 2)
    copies.start(centre(delta_two_s), delta_two_out)
    fill_band(conv_c, band_ct, 1, True)
    for plane, window in places:
        at = 256 * window
        value = conv_window(delta_two_s, plane, window, band_dt)
        stored = ref_one_s[plane, 1, :, 128 + at : 384 + at]
        value = gated(value * slope(stored), inside)
        store_shifted(delta_one_s, plane, at, value, 1)
    copies.start(centre(delta_one_s), delta_one_out)
    for window in range(2):
        values = []
        for plane in range(2):
            at = 256 * window
            lanes = slice(512 * plane + at, 512 * plane + at + 256)
            value = conv_window(delta_one_s, plane, window, band_ct)
            value = value + jnp.dot(error_one, spread_one[:, lanes], preferred_element_type=F32)
            values.append(value.astype(BF16))
        for z in range(8):
            lanes = slice(32 * z, 32 * z + 32)
            packed[8 * window + z] = jnp.concatenate(
                [
                    values[0][:half, lanes], values[1][:half, lanes],
                    values[0][half:, lanes], values[1][half:, lanes],
                ],
                axis=1,
            )
        for part in range(2):
            peers = pl.ds(8 * window + 4 * part, 4)
            copies.start(packed.at[peers], back.at[peers])
    wait_all(copies.started[1:])


def section_grads_kernel(message, errors_one, errors_two, *refs):
    sources, grads_out = refs[:4], refs[4]
    two_s, ref_one_s, grads, ref_one, ref_two, delta_two, delta_one, sems = refs[5:]
    first, _ = edge_gates()
    copies = Copies(sems)
    for source, target in zip(sources, (ref_one, ref_two, delta_two, delta_one)):
        copies.start(source, target)
    rows = errors_one.shape[0]
    own = slice(0, rows - LEFT)
    same = own_voxel()
    same = jnp.concatenate([same, same], axis=0)
    clear_margins(two_s)
    clear_margins(ref_one_s)
    load_features(message, two_s)
    wait_all(copies.started)
    for plane, window in windows_of(two_s):
        at = 256 * window
        value = ref_one[plane, :, at : at + 256].astype(F32)
        store_shifted(ref_one_s, plane, at, value, 2)

    def head_grad(errors, planes):
        error = errors[own, :].astype(F32)
        error = jnp.concatenate([error[:LEFT] * first, error[LEFT:]], axis=0).astype(BF16)
        total = None
        for plane, feature in enumerate(planes):
            full = lax.dot_general(error, feature, CONTRACT_ROWS, preferred_element_type=F32)
            kept = jnp.where(same[:, 512 * plane : 512 * plane + 512], full, 0.0)
            kept = jnp.sum(kept, axis=0, keepdims=True)
            kept = kept[:, 0:128] + kept[:, 128:256] + kept[:, 256:384] + kept[:, 384:512]
            total = kept if total is None else total + kept
        total = total + pltpu.roll(total, 64, 1)
        total = total + pltpu.roll(total, 32, 1)
        return total[:, 0:32]

    grads[...] = jnp.zeros(grads.shape, F32)
    features = [two_s[plane, 1, own, 128:640] for plane in range(2)]
    put_piece(grads, 18, head_grad(errors_one, features))
    put_piece(grads, 19, head_grad(errors_two, [ref_two[plane, own, :] for plane in range(2)]))
    weight_grad(delta_two, ref_one_s, 2, grads, 9, first)
    weight_grad(delta_one, two_s, 1, grads, 0, first)
    grads_out[...] = grads[...].astype(BF16)


def backward_xy_kernel(
    back, grads_cd, conv_b, hidden_two_in, hidden_one_in, stem_in,
    grads_out, delta_a_out,
    stem_s, one_s, delta_b_s, delta_b, delta_a, grads, hidden_two, band_bt, hidden_one, stem, sems,
):
    first, inside = edge_gates()
    copies = Copies(sems)
    two_here = copies.start_lanes(hidden_two_in, hidden_two, 4)
    one_here = copies.start_lanes(hidden_one_in, hidden_one, 4)
    stem_here = copies.start_lanes(stem_in, stem, 4)
    for shifted in (stem_s, one_s, delta_b_s):
        clear_margins(shifted)
    fill_band(conv_b, band_bt, 2, True)
    for group in range(8):
        parts = []
        for side in range(2):
            at = 64 * side
            parts.append(
                jnp.concatenate(
                    [back[2 * group + q][:, at : at + 64] for q in range(2)], axis=1
                )
            )
        lanes = slice(128 * group, 128 * group + 128)
        value = jnp.concatenate(parts, axis=0).astype(F32)
        if group % 2 == 0:
            two_here[group // 2].wait()
        value = gated(value * slope(hidden_two[0, :, lanes]), inside)
        delta_b[0, :, lanes] = value.astype(BF16)
        store_shifted(delta_b_s, 0, 128 * group, value, 2)
    wait_all(one_here)
    for window in range(4):
        at = 256 * window
        value = conv_window(delta_b_s, 0, window, band_bt)
        stored = hidden_one[0, :, at : at + 256]
        value = gated(value * slope(stored), inside)
        delta_a[0, :, at : at + 256] = value.astype(BF16)
        store_shifted(one_s, 0, at, stored.astype(F32), 2)
    leaving = copies.start(delta_a, delta_a_out)
    wait_all(stem_here)
    for window in range(4):
        lanes = slice(256 * window, 256 * window + 256)
        store_shifted(stem_s, 0, 256 * window, stem[0, :, lanes].astype(F32), 1)
    grads[...] = jnp.zeros(grads.shape, F32)
    weight_grad(delta_b, one_s, 2, grads, 9, first)
    weight_grad(delta_a, stem_s, 1, grads, 0, first)
    for peer in range(8):
        grads_out[peer] = grads[20 * peer : 20 * peer + 20, :].astype(BF16)
        grads_out[8 + peer] = grads_cd[20 * peer : 20 * peer + 20, :]
    leaving.wait()


def stem_grad_kernel(delta_a_in, conv_a, stem_grad, delta_a_s, delta_a, band_at, sems):
    copies = Copies(sems)
    copies.start(delta_a_in, delta_a)
    rows = delta_a.shape[1]
    clear_margins(delta_a_s)
    fill_band(conv_a, band_at, 1, True)
    wait_all(copies.started)
    for window in range(4):
        lanes = slice(256 * window, 256 * window + 256)
        store_shifted(delta_a_s, 0, 256 * window, delta_a[0, :, lanes].astype(F32), 1)
    for window in range(4):
        at = 256 * window
        value = conv_window(delta_a_s, 0, window, band_at)
        stem_grad[:, at : at + 256] = value[: rows - LEFT].astype(BF16)


def finish_kernel(factor, total, grad_a, grad_b, grad_c, grad_d, head_one, head_two):
    flat = total[...].reshape(320, 128) * factor

    def piece(pair, index):
        row, lane = 160 * pair + 32 * (index // 4), 32 * (index % 4)
        return flat[row : row + 32, lane : lane + 32]

    for pair, (near, far) in enumerate(((grad_a, grad_b), (grad_c, grad_d))):
        for tap in range(9):
            near[tap // 3, tap % 3] = piece(pair, tap)
            far[tap // 3, tap % 3] = piece(pair, 9 + tap)
    head_one[...] = piece(1, 18)[0:1]
    head_two[...] = piece(1, 19)[0:1]


def call(kernel, outs, ins, scratch=(), flops=0, megabytes=16):
    places = [place for _, place in outs]
    shapes = [pltpu.HBM(out.shape, out.dtype) if place is HBM else out for out, place in outs]

    def run(*operands):
        operands = [
            pltpu.with_memory_space_constraint(operand, pltpu.HBM) if place is HBM else operand
            for operand, place in zip(operands, ins)
        ]
        return bound(*operands)

    bound = pl.pallas_call(
        kernel,
        out_shape=shapes,
        in_specs=ins,
        out_specs=list(places),
        scratch_shapes=scratch,
        compiler_params=pltpu.CompilerParams(vmem_limit_bytes=megabytes * 1024 * 1024),
        cost_estimate=pl.CostEstimate(flops=flops, bytes_accessed=1 << 20, transcendentals=0),
    )
    return run


def shape(dims, dtype):
    return jax.ShapeDtypeStruct(dims, dtype)


def sum_everywhere(grads, beside, slab, gx):
    peers, copies = lax.axis_size(gx), lax.axis_size(slab)
    mine = lax.all_to_all(grads, gx, 0, 0, tiled=True)
    mine, beside = lax.optimization_barrier((mine, beside))
    mine = jnp.sum(mine.astype(F32), axis=0)
    spread = jnp.broadcast_to(mine[None], (copies,) + mine.shape)
    mine = jnp.sum(lax.all_to_all(spread, slab, 0, 0, tiled=True), axis=0)
    spread = jnp.broadcast_to(mine[None], (peers,) + mine.shape)
    return lax.all_to_all(spread, gx, 0, 0, tiled=True), beside


def per_device(stem_features, labels, conv_a, conv_b, conv_c, conv_d, head_one, head_two):
    _, depth, height, cols = stem_features.shape
    rows = cols + HALO
    half = rows // 2
    peers = lax.axis_size("gx")
    up = [(i, i + 1) for i in range(peers - 1)]
    down = [(j, i) for i, j in up]
    sems = lambda count: pltpu.SemaphoreType.DMA((count,))
    vmem = lambda kind: pltpu.VMEM(kind.shape, kind.dtype)

    stem_features = stem_features[:, 0]
    stem, marks, initial = call(
        arrange_kernel,
        [
            (shape((cols, 1024), BF16), VMEM),
            (shape((cols, 128), BF16), VMEM),
            (shape((HALO, 1152), BF16), VMEM),
        ],
        [HBM, HBM],
        [pltpu.VMEM((1024 * cols // 128, 128), F32), vmem(stem_features), vmem(labels), sems(5)],
        flops=1 << 28, megabytes=6,
    )(stem_features, labels)
    after = lax.ppermute(initial, "gx", down)

    taps_a, taps_b, taps_c, taps_d = [
        jnp.transpose(w, (1, 2, 0, 3)) for w in (conv_a, conv_b, conv_c, conv_d)
    ]
    band = shape((1536, 256), BF16)
    spreads = shape((64, 1024), BF16)
    band_a, band_b, spread = call(
        first_bands_kernel, [(band, VMEM)] * 2 + [(spreads, HBM)], [VMEM] * 4,
        [vmem(spreads), sems(1)], flops=1 << 29, megabytes=3,
    )(taps_a, taps_b, head_one[None], head_two[None])

    wide = pltpu.VMEM((1, 3, rows, 1280), BF16)
    tall = pltpu.VMEM((2, 3, rows, 768), BF16)
    whole = shape((1, rows, 1024), BF16)
    planes = shape((2, rows, 512), BF16)
    messages = shape((16, half, 128), BF16)
    stem, hidden_one, hidden_two, marks, message = call(
        forward_xy_kernel,
        [(whole, HBM)] * 3 + [(shape((rows, 128), BF16), VMEM), (messages, HBM)],
        [VMEM] * 5,
        [wide, wide, vmem(whole), vmem(messages), sems(10)], flops=1 << 30, megabytes=8,
    )(stem, marks, after, band_a, band_b)
    message = lax.all_to_all(message, "slab", 0, 0, tiled=True)

    pairs = shape((rows, 64), BF16)
    probability, errors_one, errors_two, back, *held = call(
        section_xz_kernel,
        [(shape((rows - LEFT, 32), F32), VMEM), (pairs, VMEM), (pairs, VMEM), (messages, HBM)]
        + [(planes, HBM)] * 4,
        [VMEM] * 4 + [HBM],
        [tall, tall, tall, tall, vmem(planes), vmem(messages), pltpu.VMEM((4, 1536, 256), BF16)]
        + [vmem(spreads), sems(9)],
        flops=1 << 31, megabytes=18,
    )(message, marks, taps_c, taps_d, spread)
    back = lax.all_to_all(back, "slab", 0, 0, tiled=True)
    (grads_cd,) = call(
        section_grads_kernel,
        [(shape((160, 128), BF16), VMEM)],
        [VMEM] * 3 + [HBM] * 4,
        [tall, tall, pltpu.VMEM((160, 128), F32)] + [vmem(planes)] * 4 + [sems(4)],
        flops=1 << 31, megabytes=12,
    )(message, errors_one, errors_two, *held)

    grads, delta_a = call(
        backward_xy_kernel,
        [(shape((16, 20, 128), BF16), VMEM), (whole, HBM)],
        [VMEM] * 3 + [HBM] * 3,
        [wide, wide, wide, vmem(whole), vmem(whole), pltpu.VMEM((160, 128), F32)]
        + [vmem(whole), vmem(band), vmem(whole), vmem(whole), sems(13)],
        flops=1 << 31, megabytes=15,
    )(back, grads_cd, taps_b, hidden_two, hidden_one, stem)
    (stem_grad,) = call(
        stem_grad_kernel,
        [(shape((rows - LEFT, 1024), BF16), VMEM)],
        [HBM, VMEM], [wide, vmem(whole), vmem(band), sems(1)], flops=1 << 30, megabytes=6,
    )(delta_a, taps_a)

    total, stem_grad = sum_everywhere(grads, stem_grad, "slab", "gx")

    def in_place(found):
        moved = lax.ppermute(found[cols:], "gx", up)
        moved = jnp.where(lax.axis_index("gx") > 0, moved, found[:LEFT])
        return jnp.concatenate([moved, found[LEFT:cols]], axis=0)

    stem_grad = in_place(stem_grad).reshape(cols, height, C)
    stem_grad = jnp.transpose(stem_grad, (2, 1, 0))[:, None]
    probability = in_place(probability).reshape(cols, 2, 16)
    probability = jnp.transpose(probability, (2, 1, 0))

    taps = shape((3, 3, C, C), F32)
    finals = call(
        functools.partial(finish_kernel, 1.0 / (depth * height * cols)),
        [(taps, VMEM)] * 4 + [(shape((1, C), F32), VMEM)] * 2,
        [VMEM], flops=1 << 20, megabytes=2,
    )(total)
    kernels = [jnp.transpose(grad, (2, 0, 1, 3)) for grad in finals[:4]]
    return (probability, stem_grad, *kernels, finals[4][0], finals[5][0])


def solution(mesh):
    return jax.shard_map(
        per_device,
        mesh=mesh,
        in_specs=(P(None, "slab", None, "gx"), P(None, "slab", "gx"), P(), P(), P(), P(), P(), P()),
        out_specs=(
            P(None, "slab", "gx"),
            P(None, "slab", None, "gx"),
            P(),
            P(),
            P(),
            P(),
            P(),
            P(),
        ),
        check_vma=False,
    )
```

```python
import functools

import jax
import jax.numpy as jnp
from jax import lax
from jax.experimental import pallas as pl
from jax.experimental.pallas import tpu as pltpu
from jax.sharding import PartitionSpec as P

HALO = 32
LEFT = 16
C = 32
F32 = jnp.float32
BF16 = jnp.bfloat16
VMEM = pl.BlockSpec(memory_space=pltpu.VMEM)
HBM = pl.BlockSpec(memory_space=pltpu.HBM)
CONTRACT_ROWS = (((0,), (0,)), ((), ()))
CONTRACT_LANES = (((1,), (1,)), ((), ()))


def softplus(v):
    small = jnp.exp(-jnp.abs(v))
    tail = jnp.where(small < 1e-4, small, jnp.log(1.0 + small))
    return jnp.maximum(v, 0.0) + tail


def slope(stored):
    return 1.0 - jnp.exp(-stored.astype(F32))


def edge_gates():
    me, peers = lax.axis_index("gx"), lax.axis_size("gx")
    return jnp.where(me > 0, 0.0, 1.0), jnp.where(me < peers - 1, 1.0, 0.0)


def gated(value, inside):
    cols = value.shape[0] - HALO
    return jnp.concatenate([value[:cols], value[cols:] * inside], axis=0)


def clear_margins(shifted):
    lanes = shifted.shape[-1]
    edge = jnp.zeros(shifted.shape[:-1] + (128,), BF16)
    shifted[..., 0:128] = edge
    shifted[..., lanes - 128 : lanes] = edge


def store_shifted(shifted, plane, start, value, step):
    rows, lanes = value.shape
    where = slice(128 + start, 128 + start + lanes)
    shifted[plane, 1, :, where] = value.astype(BF16)
    lower = pltpu.roll(value, step, 0)
    row = lax.broadcasted_iota(jnp.int32, (8, lanes), 0)
    lower = jnp.concatenate([jnp.where(row < step, 0.0, lower[:8]), lower[8:]], axis=0)
    shifted[plane, 0, :, where] = lower.astype(BF16)
    shifted[plane, 2, :, where] = pltpu.roll(value, rows - step, 0).astype(BF16)


def conv_window(shifted, plane, window, band):
    lanes = slice(256 * window, 256 * window + 512)
    columns = jnp.concatenate([shifted[plane, tap, :, lanes] for tap in range(3)], axis=1)
    return jnp.dot(columns, band[...], preferred_element_type=F32)


def windows_of(shifted):
    planes = shifted.shape[0]
    windows = (shifted.shape[-1] - 256) // 256
    return [(plane, window) for plane in range(planes) for window in range(windows)]


def weight_grad(delta, shifted, step, grads, first_piece, first):
    own = slice(LEFT, delta.shape[1] - LEFT)
    places = windows_of(shifted)
    head = jnp.concatenate(
        [delta[plane, :LEFT, 256 * window : 256 * window + 256] for plane, window in places], axis=0
    )
    head = (head.astype(F32) * first).astype(BF16)
    for tap in range(3):
        total = lax.dot_general(
            head,
            jnp.concatenate(
                [
                    shifted[plane, tap, :LEFT, 256 * window : 256 * window + 512]
                    for plane, window in places
                ],
                axis=0,
            ),
            CONTRACT_ROWS,
            preferred_element_type=F32,
        )
        for plane, window in places:
            total = total + lax.dot_general(
                delta[plane, own, 256 * window : 256 * window + 256],
                shifted[plane, tap, own, 256 * window : 256 * window + 512],
                CONTRACT_ROWS,
                preferred_element_type=F32,
            )
        folded = None
        for r in range(4):
            near = total[32 * r : 32 * r + 32, 0:384]
            far = total[32 * r + 128 : 32 * r + 160, 128:512]
            part = near + far
            if r:
                part = pltpu.roll(part, 384 - 32 * r, 1)
            folded = part if folded is None else folded + part
        for row_tap in range(3):
            at = 32 * (4 + step * (row_tap - 1))
            put_piece(grads, first_piece + 3 * row_tap + tap, folded[:, at : at + 32])


def put_piece(grads, index, value):
    row, lane = 32 * (index // 4), 32 * (index % 4)
    grads[row : row + value.shape[0], lane : lane + 32] = value


def fill_tap(weight, band, step, backward, col_tap):
    lane = lax.broadcasted_iota(jnp.int32, (32, 128), 1) // 32
    cut = []
    for row_tap in range(3):
        if backward:
            block = weight[2 - row_tap, 2 - col_tap].astype(F32)
        else:
            block = weight[row_tap, col_tap].astype(F32).T
        block = jnp.concatenate([block] * 4, axis=1)
        cut.append([jnp.where(lane == q, block, 0.0) for q in range(4)])
    for source in range(16):
        for group in range(2):
            panel = None
            for q in range(4):
                off = source - 4 - (4 * group + q)
                if off % step == 0 and abs(off) <= step:
                    term = cut[off // step + 1][q]
                    panel = term if panel is None else panel + term
            if panel is None:
                panel = jnp.zeros((32, 128), F32)
            row = 512 * col_tap + 32 * source
            band[row : row + 32, 128 * group : 128 * group + 128] = panel.astype(BF16)


def fill_band(weight, band, step, backward):
    for col_tap in range(3):
        fill_tap(weight, band, step, backward, col_tap)


class Copies:
    def __init__(self, sems):
        self.sems, self.started = sems, []

    def start(self, source, target):
        copy = pltpu.make_async_copy(source, target, self.sems.at[len(self.started)])
        copy.start()
        self.started.append(copy)
        return copy

    def start_lanes(self, source, target, parts):
        size = source.shape[-1] // parts
        return [
            self.start(
                source.at[..., pl.ds(size * k, size)], target.at[..., pl.ds(size * k, size)]
            )
            for k in range(parts)
        ]


def wait_all(copies):
    for copy in copies:
        copy.wait()


def centre(shifted):
    return shifted.at[:, 1, :, pl.ds(128, shifted.shape[-1] - 256)]


def columns_first(stem, flat, side, group):
    first = 1024 * side + 4 * group
    rows = [flat[pl.ds(first + k, 32, stride=32), :] for k in range(4)]
    return jnp.concatenate(rows, axis=0).T


def fill_flat(stem, flat, side):
    part = stem[:, :, 128 * side : 128 * side + 128].reshape(1024, 128)
    flat[1024 * side : 1024 * side + 1024, :] = part.astype(F32)


def marks_first(labels):
    marks = labels.astype(F32)
    blank = jnp.zeros((96, labels.shape[2]), F32)
    marks = jnp.concatenate([marks[:, 0, :], marks[:, 1, :], blank], axis=0)
    return marks.T.astype(BF16)


def edge_kernel(stem_in, labels_in, initial, flat, stem, labels, sems):
    copies = Copies(sems)
    near = pl.ds(0, 128)
    for k in range(4):
        rows = pl.ds(8 * k, 8)
        copies.start(stem_in.at[rows, :, near], stem.at[rows])
    copies.start(labels_in.at[:, :, near], labels)
    wait_all(copies.started)
    fill_flat(stem, flat, 0)
    for group in range(8):
        value = columns_first(stem, flat, 0, group)
        initial[:, 128 * group : 128 * group + 128] = value[:HALO].astype(BF16)
    initial[:, 1024:1152] = marks_first(labels[...])[:HALO]


def arrange_kernel(
    stem_in, labels_in, conv_a_in, conv_b_in, head_one_in, head_two_in,
    stem_out, marks_out, band_a, band_b, spread_out,
    flat, stem, labels, conv_a, conv_b, heads, spread, sems,
):
    cols = stem.shape[2]
    copies = Copies(sems)
    copies.start(conv_a_in, conv_a)
    copies.start(conv_b_in, conv_b)
    copies.start(head_one_in, heads.at[0])
    copies.start(head_two_in, heads.at[1])
    copies.start(labels_in, labels)
    for k in range(4):
        rows = pl.ds(8 * k, 8)
        copies.start(stem_in.at[rows], stem.at[rows])
    wait_all(copies.started[:5])
    same = own_voxel()
    for k in range(2):
        four = jnp.concatenate([heads[k].astype(F32)] * 4, axis=1)
        along = jnp.concatenate([four] * 8, axis=1)
        spread[32 * k : 32 * k + 32, :] = jnp.where(same, along, 0.0).astype(BF16)
    leaving = copies.start(spread, spread_out)
    marks_out[...] = marks_first(labels[...])
    fill_band(conv_a, band_a, 1, False)
    fill_band(conv_b, band_b, 2, False)
    wait_all(copies.started[5:9])
    for side in range(cols // 128):
        fill_flat(stem, flat, side)
    for group in range(8):
        sides = [columns_first(stem, flat, side, group) for side in range(cols // 128)]
        value = jnp.concatenate(sides, axis=0).astype(BF16)
        stem_out[:, 128 * group : 128 * group + 128] = value
    leaving.wait()


def own_voxel():
    voxel = lax.broadcasted_iota(jnp.int32, (32, 1024), 0)
    return voxel == lax.broadcasted_iota(jnp.int32, (32, 1024), 1) // 32


def forward_xy_kernel(
    stem, marks, after, band_a, band_b,
    stem_frame, hidden_one, hidden_two, marks_out, message,
    stem_s, one_s, two, sems,
):
    _, inside = edge_gates()
    copies = Copies(sems)
    clear_margins(stem_s)
    clear_margins(one_s)
    for window in range(4):
        lanes = slice(256 * window, 256 * window + 256)
        value = jnp.concatenate([stem[:, lanes], after[:, lanes]], axis=0)
        store_shifted(stem_s, 0, 256 * window, value.astype(F32), 1)
    copies.start(centre(stem_s), stem_frame)
    marks_out[...] = jnp.concatenate([marks[...], after[:, 1024:1152]], axis=0)
    for window in range(4):
        value = gated(softplus(conv_window(stem_s, 0, window, band_a)), inside)
        store_shifted(one_s, 0, 256 * window, value, 2)
    copies.start(centre(one_s), hidden_one)
    for window in range(4):
        value = gated(softplus(conv_window(one_s, 0, window, band_b)), inside).astype(BF16)
        lanes = pl.ds(256 * window, 256)
        two[0, :, lanes] = value
        copies.start(two.at[:, :, lanes], hidden_two.at[:, :, lanes])
        half = value.shape[0] // 2
        for peer in range(4):
            lanes = slice(64 * peer, 64 * peer + 64)
            message[4 * window + peer] = jnp.concatenate(
                [value[:half, lanes], value[half:, lanes]], axis=1
            )
    wait_all(copies.started)


def load_features(message, two_s):
    for plane in range(2):
        for group in range(4):
            parts = []
            for side in range(2):
                at = 64 * side + 32 * plane
                parts.append(
                    jnp.concatenate(
                        [message[4 * group + q][:, at : at + 32] for q in range(4)], axis=1
                    )
                )
            value = jnp.concatenate(parts, axis=0).astype(F32)
            store_shifted(two_s, plane, 128 * group, value, 1)


def split(error):
    high = error.astype(BF16)
    low = (error - high.astype(F32)).astype(BF16)
    return jnp.concatenate([high, low], axis=1)


def section_xz_kernel(
    message, marks, conv_c, conv_d, spread_in,
    probability, back,
    two_s, ref_one_s, delta_two_s, delta_one_s, ref_two, packed, bands, spread, grads, sems,
):
    left, inside = edge_gates()
    copies = Copies(sems)
    spread_here = copies.start(spread_in, spread)
    band_c, band_d, band_dt, band_ct = [bands.at[k] for k in range(4)]
    rows = marks.shape[0]
    half = rows // 2
    for shifted in (two_s, ref_one_s, delta_two_s, delta_one_s):
        clear_margins(shifted)
    places = windows_of(two_s)
    fill_band(conv_c, band_c, 1, False)
    load_features(message, two_s)
    for plane, window in places:
        value = gated(softplus(conv_window(two_s, plane, window, band_c)), inside)
        store_shifted(ref_one_s, plane, 256 * window, value, 2)
    fill_band(conv_d, band_d, 2, False)
    for plane, window in places:
        value = softplus(conv_window(ref_one_s, plane, window, band_d))
        ref_two[plane, :, 256 * window : 256 * window + 256] = value.astype(BF16)
    fill_band(conv_d, band_dt, 2, True)

    labels = marks[:, 0:32].astype(F32)
    spread_here.wait()
    spread_one, spread_two = spread[0:32, :], spread[32:64, :]
    first, second = None, None
    for plane in range(2):
        lanes = slice(512 * plane, 512 * plane + 512)
        one = lax.dot_general(
            two_s[plane, 1, :, 128:640], spread_one[:, lanes], CONTRACT_LANES,
            preferred_element_type=F32,
        )
        two = lax.dot_general(
            ref_two[plane], spread_two[:, lanes], CONTRACT_LANES, preferred_element_type=F32
        )
        first = one if first is None else first + one
        second = two if second is None else second + two
    first = first.astype(BF16).astype(F32)
    second = second + first
    share = 1.0 / (1.0 + jnp.exp(-second))
    probability[...] = share[: rows - LEFT]
    error_two = gated(share - labels, inside)
    error_one = 1.0 / (1.0 + jnp.exp(-first)) - labels + error_two
    error_two = split(error_two)
    error_one = split(error_one)
    spread_one = jnp.concatenate([spread_one, spread_one], axis=0)
    spread_two = jnp.concatenate([spread_two, spread_two], axis=0)

    for plane, window in places:
        at = 256 * window
        lanes = slice(512 * plane + at, 512 * plane + at + 256)
        value = jnp.dot(error_two, spread_two[:, lanes], preferred_element_type=F32)
        value = value * slope(ref_two[plane, :, at : at + 256])
        store_shifted(delta_two_s, plane, at, value, 2)
    fill_band(conv_c, band_ct, 1, True)
    for plane, window in places:
        at = 256 * window
        value = conv_window(delta_two_s, plane, window, band_dt)
        stored = ref_one_s[plane, 1, :, 128 + at : 384 + at]
        value = gated(value * slope(stored), inside)
        store_shifted(delta_one_s, plane, at, value, 1)
    for window in range(2):
        values = []
        for plane in range(2):
            at = 256 * window
            lanes = slice(512 * plane + at, 512 * plane + at + 256)
            value = conv_window(delta_one_s, plane, window, band_ct)
            value = value + jnp.dot(error_one, spread_one[:, lanes], preferred_element_type=F32)
            values.append(value.astype(BF16))
        for z in range(8):
            lanes = slice(32 * z, 32 * z + 32)
            packed[8 * window + z, :half] = jnp.concatenate(
                [
                    values[0][:half, lanes], values[1][:half, lanes],
                    values[0][half:, lanes], values[1][half:, lanes],
                ],
                axis=1,
            )
        for part in range(2):
            peers = pl.ds(8 * window + 4 * part, 4)
            rows_sent = pl.ds(0, half)
            copies.start(packed.at[peers, rows_sent], back.at[peers, rows_sent])

    same = own_voxel()
    same = jnp.concatenate([same, same], axis=0)
    kept_rows = slice(0, rows - LEFT)

    def head_grad(errors, planes):
        error = errors[kept_rows].astype(F32)
        error = jnp.concatenate([error[:LEFT] * left, error[LEFT:]], axis=0).astype(BF16)
        total = None
        for plane, feature in enumerate(planes):
            full = lax.dot_general(error, feature, CONTRACT_ROWS, preferred_element_type=F32)
            kept = jnp.where(same[:, 512 * plane : 512 * plane + 512], full, 0.0)
            kept = jnp.sum(kept, axis=0, keepdims=True)
            kept = kept[:, 0:128] + kept[:, 128:256] + kept[:, 256:384] + kept[:, 384:512]
            total = kept if total is None else total + kept
        total = total + pltpu.roll(total, 64, 1)
        total = total + pltpu.roll(total, 32, 1)
        return total[:, 0:32]

    grads[...] = jnp.zeros(grads.shape, F32)
    features = [two_s[plane, 1, kept_rows, 128:640] for plane in range(2)]
    put_piece(grads, 18, head_grad(error_one, features))
    features = [ref_two[plane, kept_rows, :] for plane in range(2)]
    put_piece(grads, 19, head_grad(error_two, features))
    weight_grad(centre(delta_two_s), ref_one_s, 2, grads, 9, left)
    weight_grad(centre(delta_one_s), two_s, 1, grads, 0, left)
    blank = jnp.zeros((6, 128), F32)
    for peer in range(16):
        chunk = jnp.concatenate([grads[10 * peer : 10 * peer + 10, :], blank], axis=0)
        packed[peer, half : half + 16, :] = chunk.astype(BF16)
    rows_sent = pl.ds(half, 16)
    copies.start(packed.at[:, rows_sent], back.at[:, rows_sent])
    wait_all(copies.started[1:])


def ready_kernel(conv_b, hidden_two_in, hidden_two, band_bt, sems):
    copies = Copies(sems)
    copies.start(hidden_two_in, hidden_two)
    fill_band(conv_b, band_bt, 2, True)
    wait_all(copies.started)


def backward_xy_kernel(
    back, hidden_two, band_bt, hidden_one_in, stem_in,
    mine_out, theirs_out, delta_a_out,
    one_s, stem_s, delta_b_s, delta_b, delta_a, grads, hidden_one, stem, sems,
):
    first, inside = edge_gates()
    copies = Copies(sems)
    one_here = copies.start_lanes(hidden_one_in, hidden_one, 2)
    stem_here = copies.start_lanes(stem_in, stem, 2)
    for shifted in (one_s, stem_s, delta_b_s):
        clear_margins(shifted)
    half = back.shape[1] - 16
    for group in range(8):
        parts = []
        for side in range(2):
            at = 64 * side
            parts.append(
                jnp.concatenate(
                    [back[2 * group + q, :half, at : at + 64] for q in range(2)], axis=1
                )
            )
        lanes = slice(128 * group, 128 * group + 128)
        value = jnp.concatenate(parts, axis=0).astype(F32)
        value = gated(value * slope(hidden_two[0, :, lanes]), inside)
        delta_b[0, :, lanes] = value.astype(BF16)
        store_shifted(delta_b_s, 0, 128 * group, value, 2)
    wait_all(one_here)
    for window in range(4):
        at = 256 * window
        value = conv_window(delta_b_s, 0, window, band_bt)
        stored = hidden_one[0, :, at : at + 256]
        value = gated(value * slope(stored), inside)
        delta_a[0, :, at : at + 256] = value.astype(BF16)
        store_shifted(one_s, 0, at, stored.astype(F32), 2)
    leaving = copies.start(delta_a, delta_a_out)
    wait_all(stem_here)
    for window in range(4):
        lanes = slice(256 * window, 256 * window + 256)
        store_shifted(stem_s, 0, 256 * window, stem[0, :, lanes].astype(F32), 1)
    grads[...] = jnp.zeros(grads.shape, F32)
    weight_grad(delta_b, one_s, 2, grads, 9, first)
    weight_grad(delta_a, stem_s, 1, grads, 0, first)
    chunk = back[0, half:, :].astype(F32)
    for peer in range(1, 16):
        chunk = chunk + back[peer, half:, :].astype(F32)
    last = [grads[128 + 16 * (k % 2) : 144 + 16 * (k % 2), 32 * (k // 2) : 32 * (k // 2) + 32] for k in range(4)]
    grads[128:144, :] = jnp.concatenate(last, axis=1)
    core = lax.rem(lax.axis_index("gx"), 2)
    mine_out[0:72, :] = grads[pl.ds(pl.multiple_of(72 * core, 8), 72), :]
    theirs_out[0:72, :] = grads[pl.ds(pl.multiple_of(72 * (1 - core), 8), 72), :]
    mine_out[72:88, :] = chunk
    theirs_out[72:88, :] = chunk
    leaving.wait()


def stem_grad_kernel(delta_a_in, conv_a, stem_grad, delta_a_s, delta_a, band_at, sems):
    copies = Copies(sems)
    copies.start(delta_a_in, delta_a)
    rows = delta_a.shape[1]
    clear_margins(delta_a_s)
    fill_band(conv_a, band_at, 1, True)
    wait_all(copies.started)
    for window in range(4):
        lanes = slice(256 * window, 256 * window + 256)
        store_shifted(delta_a_s, 0, 256 * window, delta_a[0, :, lanes].astype(F32), 1)
    for window in range(4):
        at = 256 * window
        value = conv_window(delta_a_s, 0, window, band_at)
        stem_grad[:, at : at + 256] = value[: rows - LEFT].astype(BF16)


def place_kernel(found, moved, stem_grad, flat):
    cols = stem_grad.shape[2]
    first, _ = edge_gates()
    for group in range(8):
        lanes = slice(128 * group, 128 * group + 128)
        mine = found[:cols, lanes].astype(F32)
        head = mine[:LEFT] * first + moved[:, lanes].astype(F32) * (1.0 - first)
        value = jnp.concatenate([head, mine[LEFT:]], axis=0)
        for side in range(cols // 128):
            turned = value[128 * side : 128 * side + 128].T
            for k in range(4):
                start = 1024 * side + 4 * group + k
                flat[pl.ds(start, 32, stride=32), :] = turned[32 * k : 32 * k + 32]
    for side in range(cols // 128):
        part = flat[1024 * side : 1024 * side + 1024, :].reshape(32, 32, 128)
        stem_grad[:, :, 128 * side : 128 * side + 128] = part.astype(BF16)


def finish_kernel(factor, mine, theirs, chunks, grad_a, grad_b, grad_c, grad_d, head_one, head_two, flat):
    core = lax.rem(lax.axis_index("gx"), 2)
    flat[pl.ds(pl.multiple_of(72 * core, 8), 72), :] = mine[...] * factor
    flat[pl.ds(pl.multiple_of(72 * (1 - core), 8), 72), :] = theirs[...] * factor
    for peer in range(16):
        flat[160 + 10 * peer : 170 + 10 * peer, :] = chunks[peer, 0:10, :].astype(F32) * factor

    def piece(pair, index):
        row, lane = 160 * pair + 32 * (index // 4), 32 * (index % 4)
        if pair == 0 and index >= 16:
            lane = 64 * (index % 4)
            halves = [flat[row : row + 16, lane + at : lane + at + 32] for at in (0, 32)]
            return jnp.concatenate(halves, axis=0)
        return flat[row : row + 32, lane : lane + 32]

    for pair, (near, far) in enumerate(((grad_a, grad_b), (grad_c, grad_d))):
        for tap in range(9):
            near[tap // 3, tap % 3] = piece(pair, tap)
            far[tap // 3, tap % 3] = piece(pair, 9 + tap)
    head_one[...] = piece(1, 18)[0:1]
    head_two[...] = piece(1, 19)[0:1]


def call(kernel, outs, ins, scratch=(), flops=0, megabytes=16):
    places = [place for _, place in outs]
    shapes = [pltpu.HBM(out.shape, out.dtype) if place is HBM else out for out, place in outs]

    def run(*operands):
        operands = [
            pltpu.with_memory_space_constraint(operand, pltpu.HBM) if place is HBM else operand
            for operand, place in zip(operands, ins)
        ]
        return bound(*operands)

    bound = pl.pallas_call(
        kernel,
        out_shape=shapes,
        in_specs=ins,
        out_specs=list(places),
        scratch_shapes=scratch,
        compiler_params=pltpu.CompilerParams(vmem_limit_bytes=megabytes * 1024 * 1024),
        cost_estimate=pl.CostEstimate(flops=flops, bytes_accessed=1 << 20, transcendentals=0),
    )
    return run


def shape(dims, dtype):
    return jax.ShapeDtypeStruct(dims, dtype)


def sum_everywhere(mine, theirs, beside, later, slab, gx):
    peers, copies = lax.axis_size(gx), lax.axis_size(slab)
    swap = [(i, i ^ 1) for i in range(peers)]
    mine = mine + lax.ppermute(theirs, gx, swap)
    spread = jnp.broadcast_to(mine.astype(BF16)[None], (peers // 2,) + mine.shape)
    same_core = [[i for i in range(peers) if i % 2 == core] for core in range(2)]
    mine = lax.all_to_all(spread, gx, 0, 0, tiled=True, axis_index_groups=same_core)
    mine, beside = lax.optimization_barrier((mine, beside))
    mine = jnp.sum(mine.astype(F32), axis=0)
    spread = jnp.broadcast_to(mine.astype(BF16)[None], (copies,) + mine.shape)
    found = lax.all_to_all(spread, slab, 0, 0, tiled=True)
    found, beside = lax.optimization_barrier((found, later(beside)))
    mine = jnp.sum(found[:, :72].astype(F32), axis=0)
    return (mine, lax.ppermute(mine, gx, swap), found[:, 72:]), beside


def per_device(stem_features, labels, conv_a, conv_b, conv_c, conv_d, head_one, head_two):
    _, depth, height, cols = stem_features.shape
    rows = cols + HALO
    half = rows // 2
    peers = lax.axis_size("gx")
    up = [(i, i + 1) for i in range(peers - 1)]
    down = [(j, i) for i, j in up]
    sems = lambda count: pltpu.SemaphoreType.DMA((count,))
    vmem = lambda kind: pltpu.VMEM(kind.shape, kind.dtype)

    stem_features = stem_features[:, 0]
    near = pltpu.VMEM((C, height, 128), BF16)
    near_labels = pltpu.VMEM((16, 2, 128), labels.dtype)
    (initial,) = call(
        edge_kernel, [(shape((HALO, 1152), BF16), VMEM)], [HBM, HBM],
        [pltpu.VMEM((1024, 128), F32), near, near_labels, sems(5)], flops=1 << 28, megabytes=3,
    )(stem_features, labels)
    after = lax.ppermute(initial, "gx", down)

    taps_a, taps_b, taps_c, taps_d = [
        jnp.transpose(w, (1, 2, 0, 3)) for w in (conv_a, conv_b, conv_c, conv_d)
    ]
    band = shape((1536, 256), BF16)
    spreads = shape((64, 1024), BF16)
    stem, marks, band_a, band_b, spread = call(
        arrange_kernel,
        [
            (shape((cols, 1024), BF16), VMEM),
            (shape((cols, 128), BF16), VMEM),
            (band, VMEM),
            (band, VMEM),
            (spreads, HBM),
        ],
        [HBM] * 6,
        [pltpu.VMEM((1024 * cols // 128, 128), F32), vmem(stem_features), vmem(labels)]
        + [vmem(taps_a), vmem(taps_b), pltpu.VMEM((2, 1, C), BF16), vmem(spreads), sems(10)],
        flops=1 << 29, megabytes=6,
    )(stem_features, labels, taps_a, taps_b, head_one[None], head_two[None])

    wide = pltpu.VMEM((1, 3, rows, 1280), BF16)
    tall = pltpu.VMEM((2, 3, rows, 768), BF16)
    whole = shape((1, rows, 1024), BF16)
    planes = shape((2, rows, 512), BF16)
    messages = shape((16, half, 128), BF16)
    stem, hidden_one, hidden_two, marks, message = call(
        forward_xy_kernel,
        [(whole, HBM)] * 3 + [(shape((rows, 128), BF16), VMEM), (messages, VMEM)],
        [VMEM] * 5,
        [wide, wide, vmem(whole), sems(6)], flops=1 << 30, megabytes=8,
    )(stem, marks, after, band_a, band_b)
    message = lax.all_to_all(message, "slab", 0, 0, tiled=True)

    larger = shape((16, half + 16, 128), BF16)
    probability, back = call(
        section_xz_kernel,
        [(shape((rows - LEFT, 32), F32), VMEM), (larger, HBM)],
        [VMEM] * 4 + [HBM],
        [tall, tall, tall, tall, vmem(planes), vmem(larger), pltpu.VMEM((4, 1536, 256), BF16)]
        + [vmem(spreads), pltpu.VMEM((160, 128), F32), sems(6)],
        flops=1 << 31, megabytes=28,
    )(message, marks, taps_c, taps_d, spread)
    back = lax.all_to_all(back, "slab", 0, 0, tiled=True)

    def in_place(found):
        moved = lax.ppermute(found[cols:], "gx", up)
        moved = jnp.where(lax.axis_index("gx") > 0, moved, found[:LEFT])
        return jnp.concatenate([moved, found[LEFT:cols]], axis=0)

    probability = in_place(probability).reshape(cols, 2, 16)
    probability = jnp.transpose(probability, (2, 1, 0))
    back, probability = lax.optimization_barrier((back, probability))
    hidden_two, band_bt = call(
        ready_kernel, [(whole, VMEM), (band, VMEM)], [VMEM, HBM], [sems(1)],
        flops=1 << 31, megabytes=3,
    )(taps_b, hidden_two)

    half_sums = shape((88, 128), F32)
    mine, theirs, delta_a = call(
        backward_xy_kernel,
        [(half_sums, VMEM), (half_sums, VMEM), (whole, HBM)],
        [VMEM] * 3 + [HBM] * 2,
        [wide, wide, wide, vmem(whole), vmem(whole), pltpu.VMEM((160, 128), F32)]
        + [vmem(whole), vmem(whole), sems(5)],
        flops=1 << 31, megabytes=16,
    )(back, hidden_two, band_bt, hidden_one, stem)
    (stem_grad,) = call(
        stem_grad_kernel,
        [(shape((rows - LEFT, 1024), BF16), VMEM)],
        [HBM, VMEM], [wide, vmem(whole), vmem(band), sems(1)], flops=1 << 30, megabytes=6,
    )(delta_a, taps_a)

    def outermost_last(found):
        moved = lax.ppermute(found[cols:], "gx", up)
        (placed,) = call(
            place_kernel, [(shape((C, height, cols), BF16), VMEM)], [VMEM, VMEM],
            [pltpu.VMEM((1024 * cols // 128, 128), F32)], flops=1 << 28, megabytes=4,
        )(found, moved)
        return placed

    sums, stem_grad = sum_everywhere(mine, theirs, stem_grad, outermost_last, "slab", "gx")

    taps = shape((3, 3, C, C), F32)
    finals = call(
        functools.partial(finish_kernel, 1.0 / (depth * height * cols)),
        [(taps, VMEM)] * 4 + [(shape((1, C), F32), VMEM)] * 2,
        [VMEM] * 3, [pltpu.VMEM((320, 128), F32)], flops=1 << 20, megabytes=2,
    )(*sums)
    kernels = [jnp.transpose(grad, (2, 0, 1, 3)) for grad in finals[:4]]
    return (probability, stem_grad[:, None], *kernels, finals[4][0], finals[5][0])


def solution(mesh):
    return jax.shard_map(
        per_device,
        mesh=mesh,
        in_specs=(P(None, "slab", None, "gx"), P(None, "slab", "gx"), P(), P(), P(), P(), P(), P()),
        out_specs=(
            P(None, "slab", "gx"),
            P(None, "slab", None, "gx"),
            P(),
            P(),
            P(),
            P(),
            P(),
            P(),
        ),
        check_vma=False,
    )
```

```python
import functools

import jax
import jax.numpy as jnp
from jax import lax
from jax.experimental import pallas as pl
from jax.experimental.pallas import tpu as pltpu
from jax.sharding import PartitionSpec as P

HALO = 32
LEFT = 16
C = 32
F32 = jnp.float32
BF16 = jnp.bfloat16
VMEM = pl.BlockSpec(memory_space=pltpu.VMEM)
HBM = pl.BlockSpec(memory_space=pltpu.HBM)
CONTRACT_ROWS = (((0,), (0,)), ((), ()))
CONTRACT_LANES = (((1,), (1,)), ((), ()))


def softplus(v):
    small = jnp.exp(-jnp.abs(v))
    tail = jnp.where(small < 1e-4, small, jnp.log(1.0 + small))
    return jnp.maximum(v, 0.0) + tail


def slope(stored):
    return 1.0 - jnp.exp(-stored.astype(F32))


def edge_gates():
    me, peers = lax.axis_index("gx"), lax.axis_size("gx")
    return jnp.where(me > 0, 0.0, 1.0), jnp.where(me < peers - 1, 1.0, 0.0)


def gated(value, inside):
    cols = value.shape[0] - HALO
    return jnp.concatenate([value[:cols], value[cols:] * inside], axis=0)


def clear_margins(shifted):
    lanes = shifted.shape[-1]
    edge = jnp.zeros(shifted.shape[:-1] + (128,), BF16)
    shifted[..., 0:128] = edge
    shifted[..., lanes - 128 : lanes] = edge


def store_shifted(shifted, plane, start, value, step):
    rows, lanes = value.shape
    where = slice(128 + start, 128 + start + lanes)
    shifted[plane, 1, :, where] = value.astype(BF16)
    lower = pltpu.roll(value, step, 0)
    row = lax.broadcasted_iota(jnp.int32, (8, lanes), 0)
    lower = jnp.concatenate([jnp.where(row < step, 0.0, lower[:8]), lower[8:]], axis=0)
    shifted[plane, 0, :, where] = lower.astype(BF16)
    shifted[plane, 2, :, where] = pltpu.roll(value, rows - step, 0).astype(BF16)


def conv_window(shifted, plane, window, band):
    lanes = slice(256 * window, 256 * window + 512)
    columns = jnp.concatenate([shifted[plane, tap, :, lanes] for tap in range(3)], axis=1)
    return jnp.dot(columns, band[...], preferred_element_type=F32)


def windows_of(shifted):
    planes = shifted.shape[0]
    windows = (shifted.shape[-1] - 256) // 256
    return [(plane, window) for plane in range(planes) for window in range(windows)]


def weight_grad(delta, shifted, step, grads, first_piece, first):
    own = slice(LEFT, delta.shape[1] - LEFT)
    places = windows_of(shifted)
    head = jnp.concatenate(
        [delta[plane, :LEFT, 256 * window : 256 * window + 256] for plane, window in places], axis=0
    )
    head = (head.astype(F32) * first).astype(BF16)
    for tap in range(3):
        total = lax.dot_general(
            head,
            jnp.concatenate(
                [
                    shifted[plane, tap, :LEFT, 256 * window : 256 * window + 512]
                    for plane, window in places
                ],
                axis=0,
            ),
            CONTRACT_ROWS,
            preferred_element_type=F32,
        )
        for plane, window in places:
            total = total + lax.dot_general(
                delta[plane, own, 256 * window : 256 * window + 256],
                shifted[plane, tap, own, 256 * window : 256 * window + 512],
                CONTRACT_ROWS,
                preferred_element_type=F32,
            )
        folded = None
        for r in range(4):
            near = total[32 * r : 32 * r + 32, 0:384]
            far = total[32 * r + 128 : 32 * r + 160, 128:512]
            part = near + far
            if r:
                part = pltpu.roll(part, 384 - 32 * r, 1)
            folded = part if folded is None else folded + part
        for row_tap in range(3):
            at = 32 * (4 + step * (row_tap - 1))
            put_piece(grads, first_piece + 3 * row_tap + tap, folded[:, at : at + 32])


def put_piece(grads, index, value):
    row, lane = 32 * (index // 4), 32 * (index % 4)
    grads[row : row + value.shape[0], lane : lane + 32] = value


def fill_tap(weight, band, step, backward, col_tap):
    lane = lax.broadcasted_iota(jnp.int32, (32, 128), 1) // 32
    cut = []
    for row_tap in range(3):
        if backward:
            block = weight[2 - row_tap, 2 - col_tap].astype(F32)
        else:
            block = weight[row_tap, col_tap].astype(F32).T
        block = jnp.concatenate([block] * 4, axis=1)
        cut.append([jnp.where(lane == q, block, 0.0) for q in range(4)])
    for source in range(16):
        for group in range(2):
            panel = None
            for q in range(4):
                off = source - 4 - (4 * group + q)
                if off % step == 0 and abs(off) <= step:
                    term = cut[off // step + 1][q]
                    panel = term if panel is None else panel + term
            if panel is None:
                panel = jnp.zeros((32, 128), F32)
            row = 512 * col_tap + 32 * source
            band[row : row + 32, 128 * group : 128 * group + 128] = panel.astype(BF16)


def fill_band(weight, band, step, backward):
    for col_tap in range(3):
        fill_tap(weight, band, step, backward, col_tap)


class Copies:
    def __init__(self, sems):
        self.sems, self.started = sems, []

    def start(self, source, target):
        copy = pltpu.make_async_copy(source, target, self.sems.at[len(self.started)])
        copy.start()
        self.started.append(copy)
        return copy

    def start_lanes(self, source, target, parts):
        size = source.shape[-1] // parts
        return [
            self.start(
                source.at[..., pl.ds(size * k, size)], target.at[..., pl.ds(size * k, size)]
            )
            for k in range(parts)
        ]


def wait_all(copies):
    for copy in copies:
        copy.wait()


def centre(shifted):
    return shifted.at[:, 1, :, pl.ds(128, shifted.shape[-1] - 256)]


def columns_first(stem, flat, side, group):
    first = 1024 * side + 4 * group
    rows = [flat[pl.ds(first + k, 32, stride=32), :] for k in range(4)]
    return jnp.concatenate(rows, axis=0).T


def fill_flat(stem, flat, side):
    part = stem[:, :, 128 * side : 128 * side + 128].reshape(1024, 128)
    flat[1024 * side : 1024 * side + 1024, :] = part.astype(F32)


def marks_first(labels):
    marks = labels.astype(F32)
    blank = jnp.zeros((96, labels.shape[2]), F32)
    marks = jnp.concatenate([marks[:, 0, :], marks[:, 1, :], blank], axis=0)
    return marks.T.astype(BF16)


def edge_kernel(stem_in, labels_in, initial, flat, stem, labels, sems):
    copies = Copies(sems)
    near = pl.ds(0, 128)
    for k in range(4):
        rows = pl.ds(8 * k, 8)
        copies.start(stem_in.at[rows, :, near], stem.at[rows])
    copies.start(labels_in.at[:, :, near], labels)
    wait_all(copies.started)
    fill_flat(stem, flat, 0)
    for group in range(8):
        value = columns_first(stem, flat, 0, group)
        initial[:, 128 * group : 128 * group + 128] = value[:HALO].astype(BF16)
    initial[:, 1024:1152] = marks_first(labels[...])[:HALO]


def arrange_kernel(
    stem_in, labels_in, conv_a_in, conv_b_in, head_one_in, head_two_in,
    stem_out, marks_out, band_a, band_b, spread,
    flat, stem, labels, conv_a, conv_b, heads, sems,
):
    cols = stem.shape[2]
    copies = Copies(sems)
    copies.start(conv_a_in, conv_a)
    copies.start(conv_b_in, conv_b)
    copies.start(head_one_in, heads.at[0])
    copies.start(head_two_in, heads.at[1])
    copies.start(labels_in, labels)
    for k in range(4):
        rows = pl.ds(8 * k, 8)
        copies.start(stem_in.at[rows], stem.at[rows])
    wait_all(copies.started[:5])
    same = own_voxel()
    for k in range(2):
        four = jnp.concatenate([heads[k].astype(F32)] * 4, axis=1)
        along = jnp.concatenate([four] * 8, axis=1)
        spread[32 * k : 32 * k + 32, :] = jnp.where(same, along, 0.0).astype(BF16)
    marks_out[...] = marks_first(labels[...])
    fill_band(conv_a, band_a, 1, False)
    fill_band(conv_b, band_b, 2, False)
    wait_all(copies.started[5:9])
    for side in range(cols // 128):
        fill_flat(stem, flat, side)
    for group in range(8):
        sides = [columns_first(stem, flat, side, group) for side in range(cols // 128)]
        value = jnp.concatenate(sides, axis=0).astype(BF16)
        stem_out[:, 128 * group : 128 * group + 128] = value


def own_voxel():
    voxel = lax.broadcasted_iota(jnp.int32, (32, 1024), 0)
    return voxel == lax.broadcasted_iota(jnp.int32, (32, 1024), 1) // 32


def forward_xy_kernel(
    stem, marks, after, band_a, band_b,
    stem_frame, hidden_one, hidden_two, marks_out, message,
    stem_s, one_s,
):
    _, inside = edge_gates()
    clear_margins(stem_s)
    clear_margins(one_s)
    for window in range(4):
        lanes = slice(256 * window, 256 * window + 256)
        value = jnp.concatenate([stem[:, lanes], after[:, lanes]], axis=0)
        stem_frame[0, :, lanes] = value
        store_shifted(stem_s, 0, 256 * window, value.astype(F32), 1)
    marks_out[...] = jnp.concatenate([marks[...], after[:, 1024:1152]], axis=0)
    for window in range(4):
        value = gated(softplus(conv_window(stem_s, 0, window, band_a)), inside)
        hidden_one[0, :, 256 * window : 256 * window + 256] = value.astype(BF16)
        store_shifted(one_s, 0, 256 * window, value, 2)
    for window in range(4):
        value = gated(softplus(conv_window(one_s, 0, window, band_b)), inside).astype(BF16)
        hidden_two[0, :, 256 * window : 256 * window + 256] = value
        half = value.shape[0] // 2
        for peer in range(4):
            lanes = slice(64 * peer, 64 * peer + 64)
            message[4 * window + peer] = jnp.concatenate(
                [value[:half, lanes], value[half:, lanes]], axis=1
            )


def load_features(message, two_s):
    for plane in range(2):
        for group in range(4):
            parts = []
            for side in range(2):
                at = 64 * side + 32 * plane
                parts.append(
                    jnp.concatenate(
                        [message[4 * group + q][:, at : at + 32] for q in range(4)], axis=1
                    )
                )
            value = jnp.concatenate(parts, axis=0).astype(F32)
            store_shifted(two_s, plane, 128 * group, value, 1)


def split(error):
    high = error.astype(BF16)
    low = (error - high.astype(F32)).astype(BF16)
    return jnp.concatenate([high, low], axis=1)


def section_xz_kernel(
    message, marks, conv_c, conv_d, spread,
    probability, back,
    two_s, ref_one_s, delta_two_s, delta_one_s, ref_two, bands, grads,
):
    left, inside = edge_gates()
    band_c, band_d, band_dt, band_ct = [bands.at[k] for k in range(4)]
    rows = marks.shape[0]
    half = rows // 2
    for shifted in (two_s, ref_one_s, delta_two_s, delta_one_s):
        clear_margins(shifted)
    places = windows_of(two_s)
    fill_band(conv_c, band_c, 1, False)
    load_features(message, two_s)
    for plane, window in places:
        value = gated(softplus(conv_window(two_s, plane, window, band_c)), inside)
        store_shifted(ref_one_s, plane, 256 * window, value, 2)
    fill_band(conv_d, band_d, 2, False)
    for plane, window in places:
        value = softplus(conv_window(ref_one_s, plane, window, band_d))
        ref_two[plane, :, 256 * window : 256 * window + 256] = value.astype(BF16)
    fill_band(conv_d, band_dt, 2, True)

    labels = marks[:, 0:32].astype(F32)
    spread_one, spread_two = spread[0:32, :], spread[32:64, :]
    first, second = None, None
    for plane in range(2):
        lanes = slice(512 * plane, 512 * plane + 512)
        one = lax.dot_general(
            two_s[plane, 1, :, 128:640], spread_one[:, lanes], CONTRACT_LANES,
            preferred_element_type=F32,
        )
        two = lax.dot_general(
            ref_two[plane], spread_two[:, lanes], CONTRACT_LANES, preferred_element_type=F32
        )
        first = one if first is None else first + one
        second = two if second is None else second + two
    first = first.astype(BF16).astype(F32)
    second = second + first
    share = 1.0 / (1.0 + jnp.exp(-second))
    probability[...] = share[: rows - LEFT]
    error_two = gated(share - labels, inside)
    error_one = 1.0 / (1.0 + jnp.exp(-first)) - labels + error_two
    error_two = split(error_two)
    error_one = split(error_one)
    spread_one = jnp.concatenate([spread_one, spread_one], axis=0)
    spread_two = jnp.concatenate([spread_two, spread_two], axis=0)

    for plane, window in places:
        at = 256 * window
        lanes = slice(512 * plane + at, 512 * plane + at + 256)
        value = jnp.dot(error_two, spread_two[:, lanes], preferred_element_type=F32)
        value = value * slope(ref_two[plane, :, at : at + 256])
        store_shifted(delta_two_s, plane, at, value, 2)
    fill_band(conv_c, band_ct, 1, True)
    for plane, window in places:
        at = 256 * window
        value = conv_window(delta_two_s, plane, window, band_dt)
        stored = ref_one_s[plane, 1, :, 128 + at : 384 + at]
        value = gated(value * slope(stored), inside)
        store_shifted(delta_one_s, plane, at, value, 1)
    for window in range(2):
        values = []
        for plane in range(2):
            at = 256 * window
            lanes = slice(512 * plane + at, 512 * plane + at + 256)
            value = conv_window(delta_one_s, plane, window, band_ct)
            value = value + jnp.dot(error_one, spread_one[:, lanes], preferred_element_type=F32)
            values.append(value.astype(BF16))
        for z in range(8):
            lanes = slice(32 * z, 32 * z + 32)
            back[8 * window + z, :half] = jnp.concatenate(
                [
                    values[0][:half, lanes], values[1][:half, lanes],
                    values[0][half:, lanes], values[1][half:, lanes],
                ],
                axis=1,
            )

    same = own_voxel()
    same = jnp.concatenate([same, same], axis=0)
    kept_rows = slice(0, rows - LEFT)

    def head_grad(errors, planes):
        error = errors[kept_rows].astype(F32)
        error = jnp.concatenate([error[:LEFT] * left, error[LEFT:]], axis=0).astype(BF16)
        total = None
        for plane, feature in enumerate(planes):
            full = lax.dot_general(error, feature, CONTRACT_ROWS, preferred_element_type=F32)
            kept = jnp.where(same[:, 512 * plane : 512 * plane + 512], full, 0.0)
            kept = jnp.sum(kept, axis=0, keepdims=True)
            kept = kept[:, 0:128] + kept[:, 128:256] + kept[:, 256:384] + kept[:, 384:512]
            total = kept if total is None else total + kept
        total = total + pltpu.roll(total, 64, 1)
        total = total + pltpu.roll(total, 32, 1)
        return total[:, 0:32]

    grads[...] = jnp.zeros(grads.shape, F32)
    features = [two_s[plane, 1, kept_rows, 128:640] for plane in range(2)]
    put_piece(grads, 18, head_grad(error_one, features))
    features = [ref_two[plane, kept_rows, :] for plane in range(2)]
    put_piece(grads, 19, head_grad(error_two, features))
    weight_grad(centre(delta_two_s), ref_one_s, 2, grads, 9, left)
    weight_grad(centre(delta_one_s), two_s, 1, grads, 0, left)
    blank = jnp.zeros((6, 128), F32)
    for peer in range(16):
        chunk = jnp.concatenate([grads[10 * peer : 10 * peer + 10, :], blank], axis=0)
        back[peer, half : half + 16, :] = chunk.astype(BF16)


def backward_xy_kernel(
    back, hidden_two, hidden_one, stem, conv_b,
    mine_out, theirs_out, delta_a,
    one_s, stem_s, delta_b_s, delta_b, grads, band_bt,
):
    first, inside = edge_gates()
    fill_band(conv_b, band_bt, 2, True)
    for shifted in (one_s, stem_s, delta_b_s):
        clear_margins(shifted)
    half = back.shape[1] - 16
    for group in range(8):
        parts = []
        for side in range(2):
            at = 64 * side
            parts.append(
                jnp.concatenate(
                    [back[2 * group + q, :half, at : at + 64] for q in range(2)], axis=1
                )
            )
        lanes = slice(128 * group, 128 * group + 128)
        value = jnp.concatenate(parts, axis=0).astype(F32)
        value = gated(value * slope(hidden_two[0, :, lanes]), inside)
        delta_b[0, :, lanes] = value.astype(BF16)
        store_shifted(delta_b_s, 0, 128 * group, value, 2)
    for window in range(4):
        at = 256 * window
        value = conv_window(delta_b_s, 0, window, band_bt)
        stored = hidden_one[0, :, at : at + 256]
        value = gated(value * slope(stored), inside)
        delta_a[0, :, at : at + 256] = value.astype(BF16)
        store_shifted(one_s, 0, at, stored.astype(F32), 2)
    for window in range(4):
        lanes = slice(256 * window, 256 * window + 256)
        store_shifted(stem_s, 0, 256 * window, stem[0, :, lanes].astype(F32), 1)
    grads[...] = jnp.zeros(grads.shape, F32)
    weight_grad(delta_b, one_s, 2, grads, 9, first)
    weight_grad(delta_a, stem_s, 1, grads, 0, first)
    chunk = back[0, half:, :].astype(F32)
    for peer in range(1, 16):
        chunk = chunk + back[peer, half:, :].astype(F32)
    last = [grads[128 + 16 * (k % 2) : 144 + 16 * (k % 2), 32 * (k // 2) : 32 * (k // 2) + 32] for k in range(4)]
    grads[128:144, :] = jnp.concatenate(last, axis=1)
    core = lax.rem(lax.axis_index("gx"), 2)
    mine_out[0:72, :] = grads[pl.ds(pl.multiple_of(72 * core, 8), 72), :]
    theirs_out[0:72, :] = grads[pl.ds(pl.multiple_of(72 * (1 - core), 8), 72), :]
    mine_out[72:88, :] = chunk
    theirs_out[72:88, :] = chunk


def stem_grad_kernel(delta_a, probability, conv_a, stem_grad, leaving, delta_a_s, band_at):
    rows = delta_a.shape[1]
    tail = slice(rows - 2 * LEFT, rows - LEFT)
    clear_margins(delta_a_s)
    fill_band(conv_a, band_at, 1, True)
    for window in range(4):
        lanes = slice(256 * window, 256 * window + 256)
        store_shifted(delta_a_s, 0, 256 * window, delta_a[0, :, lanes].astype(F32), 1)
    for window in range(4):
        lanes = slice(256 * window, 256 * window + 256)
        value = conv_window(delta_a_s, 0, window, band_at).astype(BF16)
        stem_grad[:, lanes] = value[: rows - 2 * LEFT]
        leaving[:, lanes] = value[tail]
    rest = probability[tail, :]
    parts = []
    for _ in range(3):
        parts.append(rest.astype(BF16))
        rest = rest - parts[-1].astype(F32)
    parts.append(jnp.zeros((LEFT, 32), BF16))
    leaving[:, 1024:1152] = jnp.concatenate(parts, axis=1)


def place_kernel(found, probability, moved, stem_grad, share, flat):
    cols = stem_grad.shape[2]
    first, _ = edge_gates()
    for group in range(8):
        lanes = slice(128 * group, 128 * group + 128)
        mine = found[:, lanes].astype(F32)
        head = mine[:LEFT] * first + moved[:, lanes].astype(F32) * (1.0 - first)
        value = jnp.concatenate([head, mine[LEFT:]], axis=0)
        for side in range(cols // 128):
            turned = value[128 * side : 128 * side + 128].T
            for k in range(4):
                start = 1024 * side + 4 * group + k
                flat[pl.ds(start, 32, stride=32), :] = turned[32 * k : 32 * k + 32]
    for side in range(cols // 128):
        part = flat[1024 * side : 1024 * side + 1024, :].reshape(32, 32, 128)
        stem_grad[:, :, 128 * side : 128 * side + 128] = part.astype(BF16)
    parts = moved[:, 1024:1152].astype(F32)
    head = parts[:, 0:32] + parts[:, 32:64] + parts[:, 64:96]
    head = probability[:LEFT, :] * first + head * (1.0 - first)
    value = jnp.concatenate([head, probability[LEFT:cols, :]], axis=0).T
    share[:, 0, :] = value[0:16]
    share[:, 1, :] = value[16:32]


def finish_cd_kernel(factor, chunks, grad_c, grad_d, head_one, head_two, flat):
    for peer in range(16):
        flat[10 * peer : 10 * peer + 10, :] = chunks[peer, 0:10, :].astype(F32) * factor

    def piece(index):
        row, lane = 32 * (index // 4), 32 * (index % 4)
        return flat[row : row + 32, lane : lane + 32]

    for tap in range(9):
        grad_c[tap // 3, tap % 3] = piece(tap)
        grad_d[tap // 3, tap % 3] = piece(9 + tap)
    head_one[...] = piece(18)[0:1]
    head_two[...] = piece(19)[0:1]


def finish_ab_kernel(factor, mine, theirs, grad_a, grad_b, flat):
    core = lax.rem(lax.axis_index("gx"), 2)
    flat[pl.ds(pl.multiple_of(72 * core, 8), 72), :] = mine[...] * factor
    flat[pl.ds(pl.multiple_of(72 * (1 - core), 8), 72), :] = theirs[...] * factor

    def piece(index):
        row, lane = 32 * (index // 4), 32 * (index % 4)
        if index >= 16:
            lane = 64 * (index % 4)
            halves = [flat[row : row + 16, lane + at : lane + at + 32] for at in (0, 32)]
            return jnp.concatenate(halves, axis=0)
        return flat[row : row + 32, lane : lane + 32]

    for tap in range(9):
        grad_a[tap // 3, tap % 3] = piece(tap)
        grad_b[tap // 3, tap % 3] = piece(9 + tap)


def call(kernel, outs, ins, scratch=(), flops=0, megabytes=16):
    places = [place for _, place in outs]
    shapes = [pltpu.HBM(out.shape, out.dtype) if place is HBM else out for out, place in outs]

    def run(*operands):
        operands = [
            pltpu.with_memory_space_constraint(operand, pltpu.HBM) if place is HBM else operand
            for operand, place in zip(operands, ins)
        ]
        return bound(*operands)

    bound = pl.pallas_call(
        kernel,
        out_shape=shapes,
        in_specs=ins,
        out_specs=list(places),
        scratch_shapes=scratch,
        compiler_params=pltpu.CompilerParams(vmem_limit_bytes=megabytes * 1024 * 1024),
        cost_estimate=pl.CostEstimate(flops=flops, bytes_accessed=1 << 20, transcendentals=0),
    )
    return run


def shape(dims, dtype):
    return jax.ShapeDtypeStruct(dims, dtype)


def sum_everywhere(mine, theirs, beside, later, slab, gx):
    peers, copies = lax.axis_size(gx), lax.axis_size(slab)
    swap = [(i, i ^ 1) for i in range(peers)]
    mine = mine + lax.ppermute(theirs, gx, swap)
    spread = jnp.broadcast_to(mine.astype(BF16)[None], (peers // 2,) + mine.shape)
    same_core = [[i for i in range(peers) if i % 2 == core] for core in range(2)]
    mine = lax.all_to_all(spread, gx, 0, 0, tiled=True, axis_index_groups=same_core)
    mine, beside = lax.optimization_barrier((mine, beside))
    mine = jnp.sum(mine.astype(F32), axis=0)
    spread = jnp.broadcast_to(mine.astype(BF16)[None], (copies,) + mine.shape)
    found = lax.all_to_all(spread, slab, 0, 0, tiled=True)
    found, beside = lax.optimization_barrier((found, later(beside)))
    mine = jnp.sum(found[:, :72].astype(F32), axis=0)
    return (mine, lax.ppermute(mine, gx, swap), found[:, 72:]), beside


def per_device(stem_features, labels, conv_a, conv_b, conv_c, conv_d, head_one, head_two):
    _, depth, height, cols = stem_features.shape
    rows = cols + HALO
    half = rows // 2
    peers = lax.axis_size("gx")
    up = [(i, i + 1) for i in range(peers - 1)]
    down = [(j, i) for i, j in up]
    sems = lambda count: pltpu.SemaphoreType.DMA((count,))
    vmem = lambda kind: pltpu.VMEM(kind.shape, kind.dtype)

    stem_features = stem_features[:, 0]
    near = pltpu.VMEM((C, height, 128), BF16)
    near_labels = pltpu.VMEM((16, 2, 128), labels.dtype)
    (initial,) = call(
        edge_kernel, [(shape((HALO, 1152), BF16), VMEM)], [HBM, HBM],
        [pltpu.VMEM((1024, 128), F32), near, near_labels, sems(5)], flops=1 << 28, megabytes=3,
    )(stem_features, labels)
    after = lax.ppermute(initial, "gx", down)

    taps_a, taps_b, taps_c, taps_d = [
        jnp.transpose(w, (1, 2, 0, 3)) for w in (conv_a, conv_b, conv_c, conv_d)
    ]
    band = shape((1536, 256), BF16)
    spreads = shape((64, 1024), BF16)
    stem, marks, band_a, band_b, spread = call(
        arrange_kernel,
        [
            (shape((cols, 1024), BF16), VMEM),
            (shape((cols, 128), BF16), VMEM),
            (band, VMEM),
            (band, VMEM),
            (spreads, VMEM),
        ],
        [HBM] * 6,
        [pltpu.VMEM((1024 * cols // 128, 128), F32), vmem(stem_features), vmem(labels)]
        + [vmem(taps_a), vmem(taps_b), pltpu.VMEM((2, 1, C), BF16), sems(9)],
        flops=1 << 29, megabytes=6,
    )(stem_features, labels, taps_a, taps_b, head_one[None], head_two[None])

    wide = pltpu.VMEM((1, 3, rows, 1280), BF16)
    tall = pltpu.VMEM((2, 3, rows, 768), BF16)
    whole = shape((1, rows, 1024), BF16)
    planes = shape((2, rows, 512), BF16)
    messages = shape((16, half, 128), BF16)
    stem, hidden_one, hidden_two, marks, message = call(
        forward_xy_kernel,
        [(whole, VMEM)] * 3 + [(shape((rows, 128), BF16), VMEM), (messages, VMEM)],
        [VMEM] * 5,
        [wide, wide], flops=1 << 30, megabytes=8,
    )(stem, marks, after, band_a, band_b)
    message = lax.all_to_all(message, "slab", 0, 0, tiled=True)

    larger = shape((16, half + 16, 128), BF16)
    probability, back = call(
        section_xz_kernel,
        [(shape((rows - LEFT, 32), F32), VMEM), (larger, VMEM)],
        [VMEM] * 5,
        [tall, tall, tall, tall, vmem(planes), pltpu.VMEM((4, 1536, 256), BF16)]
        + [pltpu.VMEM((160, 128), F32)],
        flops=1 << 31, megabytes=28,
    )(message, marks, taps_c, taps_d, spread)
    back = lax.all_to_all(back, "slab", 0, 0, tiled=True)

    half_sums = shape((88, 128), F32)
    mine, theirs, delta_a = call(
        backward_xy_kernel,
        [(half_sums, VMEM), (half_sums, VMEM), (whole, VMEM)],
        [VMEM] * 5,
        [wide, wide, wide, vmem(whole), pltpu.VMEM((160, 128), F32), vmem(band)],
        flops=1 << 31, megabytes=16,
    )(back, hidden_two, hidden_one, stem, taps_b)
    edge = shape((LEFT, 1152), BF16)
    beside = call(
        stem_grad_kernel,
        [(shape((cols, 1024), BF16), VMEM), (edge, VMEM)],
        [VMEM] * 3, [wide, vmem(band)], flops=1 << 30, megabytes=6,
    )(delta_a, probability, taps_a)

    def place(beside):
        found, leaving = beside
        moved = lax.ppermute(leaving, "gx", up)
        return call(
            place_kernel,
            [(shape((C, height, cols), BF16), VMEM), (shape((16, 2, cols), F32), VMEM)],
            [VMEM] * 3, [pltpu.VMEM((1024 * cols // 128, 128), F32)], flops=1 << 28, megabytes=4,
        )(found, probability, moved)

    (mine, theirs, chunks), (stem_grad, probability) = sum_everywhere(
        mine, theirs, beside, place, "slab", "gx"
    )

    taps = shape((3, 3, C, C), F32)
    head = shape((1, C), F32)
    factor = 1.0 / (depth * height * cols)
    grad_c, grad_d, grad_one, grad_two = call(
        functools.partial(finish_cd_kernel, factor), [(taps, VMEM)] * 2 + [(head, VMEM)] * 2,
        [VMEM], [pltpu.VMEM((160, 128), F32)], flops=1 << 24, megabytes=2,
    )(chunks)
    grad_a, grad_b = call(
        functools.partial(finish_ab_kernel, factor), [(taps, VMEM)] * 2,
        [VMEM] * 2, [pltpu.VMEM((144, 128), F32)], flops=1 << 20, megabytes=2,
    )(mine, theirs)
    kernels = [jnp.transpose(grad, (2, 0, 1, 3)) for grad in (grad_a, grad_b, grad_c, grad_d)]
    return (probability, stem_grad[:, None], *kernels, grad_one[0], grad_two[0])


def solution(mesh):
    return jax.shard_map(
        per_device,
        mesh=mesh,
        in_specs=(P(None, "slab", None, "gx"), P(None, "slab", "gx"), P(), P(), P(), P(), P(), P()),
        out_specs=(
            P(None, "slab", "gx"),
            P(None, "slab", None, "gx"),
            P(),
            P(),
            P(),
            P(),
            P(),
            P(),
        ),
        check_vma=False,
    )
```

```python
import functools

import jax
import jax.numpy as jnp
from jax import lax
from jax.experimental import pallas as pl
from jax.experimental.pallas import tpu as pltpu
from jax.sharding import PartitionSpec as P

HALO = 32
LEFT = 12
MORE = 16
C = 32
F32 = jnp.float32
BF16 = jnp.bfloat16
VMEM = pl.BlockSpec(memory_space=pltpu.VMEM)
HBM = pl.BlockSpec(memory_space=pltpu.HBM)
CONTRACT_ROWS = (((0,), (0,)), ((), ()))
CONTRACT_LANES = (((1,), (1,)), ((), ()))


def softplus(v):
    small = jnp.exp(-jnp.abs(v))
    tail = jnp.where(small < 1e-4, small, jnp.log(1.0 + small))
    return jnp.maximum(v, 0.0) + tail


def slope(stored):
    return 1.0 - jnp.exp(-stored.astype(F32))


def edge_gates():
    me, peers = lax.axis_index("gx"), lax.axis_size("gx")
    return jnp.where(me > 0, 0.0, 1.0), jnp.where(me < peers - 1, 1.0, 0.0)


def counted(value, first):
    row = lax.broadcasted_iota(jnp.int32, (MORE, 1), 0)
    cols = value.shape[0] - MORE
    head = value[:MORE].astype(F32) * jnp.where(row < LEFT, first, 1.0)
    tail = value[cols:].astype(F32) * jnp.where(row < LEFT, 1.0, 0.0)
    head, tail = head.astype(value.dtype), tail.astype(value.dtype)
    return jnp.concatenate([head, value[MORE:cols], tail], axis=0)


def gated(value, inside):
    cols = value.shape[0] - HALO
    return jnp.concatenate([value[:cols], value[cols:] * inside], axis=0)


def clear_margins(shifted):
    lanes = shifted.shape[-1]
    edge = jnp.zeros(shifted.shape[:-1] + (128,), BF16)
    shifted[..., 0:128] = edge
    shifted[..., lanes - 128 : lanes] = edge


def store_shifted(shifted, plane, start, value, step):
    rows, lanes = value.shape
    where = slice(128 + start, 128 + start + lanes)
    shifted[plane, 1, :, where] = value.astype(BF16)
    lower = pltpu.roll(value, step, 0)
    row = lax.broadcasted_iota(jnp.int32, (8, lanes), 0)
    lower = jnp.concatenate([jnp.where(row < step, 0.0, lower[:8]), lower[8:]], axis=0)
    shifted[plane, 0, :, where] = lower.astype(BF16)
    shifted[plane, 2, :, where] = pltpu.roll(value, rows - step, 0).astype(BF16)


def conv_window(shifted, plane, window, band):
    lanes = slice(256 * window, 256 * window + 512)
    columns = jnp.concatenate([shifted[plane, tap, :, lanes] for tap in range(3)], axis=1)
    return jnp.dot(columns, band[...], preferred_element_type=F32)


def windows_of(shifted):
    planes = shifted.shape[0]
    windows = (shifted.shape[-1] - 256) // 256
    return [(plane, window) for plane in range(planes) for window in range(windows)]


def weight_grad(delta, shifted, step, grads, first_piece, first):
    part = slice(0, delta.shape[1] - MORE)
    places = windows_of(shifted)
    left = jnp.concatenate(
        [
            counted(delta[plane, part, 256 * window : 256 * window + 256], first)
            for plane, window in places
        ],
        axis=0,
    )

    def step_of(tap):
        right = jnp.concatenate(
            [
                shifted[plane, tap, part, 256 * window : 256 * window + 512]
                for plane, window in places
            ],
            axis=0,
        )
        total = lax.dot_general(left, right, CONTRACT_ROWS, preferred_element_type=F32)
        folded = None
        for r in range(4):
            near = total[32 * r : 32 * r + 32, 0:384]
            far = total[32 * r + 128 : 32 * r + 160, 128:512]
            both = near + far
            if r:
                both = pltpu.roll(both, 384 - 32 * r, 1)
            folded = both if folded is None else folded + both
        for row_tap in range(3):
            at = 32 * (4 + step * (row_tap - 1))
            put_piece(grads, first_piece + 3 * row_tap + tap, folded[:, at : at + 32])

    return [functools.partial(step_of, tap) for tap in range(3)]


def run(steps):
    for step in steps:
        step()


def put_piece(grads, index, value):
    row, lane = 32 * (index // 4), 32 * (index % 4)
    grads[row : row + value.shape[0], lane : lane + 32] = value


def fill_tap(weight, band, step, backward, col_tap):
    lane = lax.broadcasted_iota(jnp.int32, (32, 128), 1) // 32
    cut = []
    for row_tap in range(3):
        if backward:
            block = weight[2 - row_tap, 2 - col_tap].astype(F32)
        else:
            block = weight[row_tap, col_tap].astype(F32).T
        block = jnp.concatenate([block] * 4, axis=1)
        cut.append([jnp.where(lane == q, block, 0.0) for q in range(4)])
    for source in range(16):
        for group in range(2):
            panel = None
            for q in range(4):
                off = source - 4 - (4 * group + q)
                if off % step == 0 and abs(off) <= step:
                    term = cut[off // step + 1][q]
                    panel = term if panel is None else panel + term
            if panel is None:
                panel = jnp.zeros((32, 128), F32)
            row = 512 * col_tap + 32 * source
            band[row : row + 32, 128 * group : 128 * group + 128] = panel.astype(BF16)


def fill_band(weight, band, step, backward):
    return [
        functools.partial(fill_tap, weight, band, step, backward, col_tap) for col_tap in range(3)
    ]


class Copies:
    def __init__(self, sems):
        self.sems, self.started = sems, []

    def start(self, source, target):
        copy = pltpu.make_async_copy(source, target, self.sems.at[len(self.started)])
        copy.start()
        self.started.append(copy)
        return copy

    def start_lanes(self, source, target, parts):
        size = source.shape[-1] // parts
        return [
            self.start(
                source.at[..., pl.ds(size * k, size)], target.at[..., pl.ds(size * k, size)]
            )
            for k in range(parts)
        ]


def wait_all(copies):
    for copy in copies:
        copy.wait()


def centre(shifted):
    return shifted.at[:, 1, :, pl.ds(128, shifted.shape[-1] - 256)]


def columns_first(stem, flat, side, group):
    first = 1024 * side + 4 * group
    rows = [flat[pl.ds(first + k, 32, stride=32), :] for k in range(4)]
    return jnp.concatenate(rows, axis=0).T


def fill_flat(stem, flat, side):
    part = stem[:, :, 128 * side : 128 * side + 128].reshape(1024, 128)
    flat[1024 * side : 1024 * side + 1024, :] = part.astype(F32)


def marks_first(labels):
    marks = labels.astype(F32)
    blank = jnp.zeros((96, labels.shape[2]), F32)
    marks = jnp.concatenate([marks[:, 0, :], marks[:, 1, :], blank], axis=0)
    return marks.T.astype(BF16)


def edge_kernel(stem_in, labels_in, initial, flat, stem, labels, sems):
    copies = Copies(sems)
    near = pl.ds(0, 128)
    for k in range(4):
        rows = pl.ds(8 * k, 8)
        copies.start(stem_in.at[rows, :, near], stem.at[rows])
    copies.start(labels_in.at[:, :, near], labels)
    wait_all(copies.started)
    fill_flat(stem, flat, 0)
    for group in range(8):
        value = columns_first(stem, flat, 0, group)
        initial[:, 128 * group : 128 * group + 128] = value[:HALO].astype(BF16)
    initial[:, 1024:1152] = marks_first(labels[...])[:HALO]


def arrange_kernel(
    stem_in, labels_in, conv_a_in, conv_b_in, head_one_in, head_two_in,
    stem_out, marks_out, band_a, band_b, spread,
    flat, stem, labels, conv_a, conv_b, heads, sems,
):
    cols = stem.shape[2]
    copies = Copies(sems)
    copies.start(conv_a_in, conv_a)
    copies.start(conv_b_in, conv_b)
    copies.start(head_one_in, heads.at[0])
    copies.start(head_two_in, heads.at[1])
    copies.start(labels_in, labels)
    for k in range(4):
        rows = pl.ds(8 * k, 8)
        copies.start(stem_in.at[rows], stem.at[rows])
    wait_all(copies.started[:5])
    same = own_voxel()
    for k in range(2):
        four = jnp.concatenate([heads[k].astype(F32)] * 4, axis=1)
        along = jnp.concatenate([four] * 8, axis=1)
        spread[32 * k : 32 * k + 32, :] = jnp.where(same, along, 0.0).astype(BF16)
    marks_out[...] = marks_first(labels[...])
    run(fill_band(conv_a, band_a, 1, False))
    run(fill_band(conv_b, band_b, 2, False))
    wait_all(copies.started[5:9])
    for side in range(cols // 128):
        fill_flat(stem, flat, side)
    for group in range(8):
        sides = [columns_first(stem, flat, side, group) for side in range(cols // 128)]
        value = jnp.concatenate(sides, axis=0).astype(BF16)
        stem_out[:, 128 * group : 128 * group + 128] = value


def own_voxel():
    voxel = lax.broadcasted_iota(jnp.int32, (32, 1024), 0)
    return voxel == lax.broadcasted_iota(jnp.int32, (32, 1024), 1) // 32


def forward_xy_kernel(
    stem, marks, after, band_a, band_b,
    stem_s, one_s, hidden_two, marks_out, message,
):
    _, inside = edge_gates()
    clear_margins(stem_s)
    clear_margins(one_s)
    for window in range(4):
        lanes = slice(256 * window, 256 * window + 256)
        value = jnp.concatenate([stem[:, lanes], after[:, lanes]], axis=0)
        store_shifted(stem_s, 0, 256 * window, value.astype(F32), 1)
    marks_out[...] = jnp.concatenate([marks[...], after[:, 1024:1152]], axis=0)
    for window in range(4):
        value = gated(softplus(conv_window(stem_s, 0, window, band_a)), inside)
        store_shifted(one_s, 0, 256 * window, value, 2)
    for window in range(4):
        value = gated(softplus(conv_window(one_s, 0, window, band_b)), inside).astype(BF16)
        hidden_two[0, :, 256 * window : 256 * window + 256] = value
        half = value.shape[0] // 2
        for peer in range(4):
            lanes = slice(64 * peer, 64 * peer + 64)
            message[4 * window + peer] = jnp.concatenate(
                [value[:half, lanes], value[half:, lanes]], axis=1
            )


def load_features(message, two_s):
    for plane in range(2):
        for group in range(4):
            parts = []
            for side in range(2):
                at = 64 * side + 32 * plane
                parts.append(
                    jnp.concatenate(
                        [message[4 * group + q][:, at : at + 32] for q in range(4)], axis=1
                    )
                )
            value = jnp.concatenate(parts, axis=0).astype(F32)
            store_shifted(two_s, plane, 128 * group, value, 1)


def split(error):
    high = error.astype(BF16)
    low = (error - high.astype(F32)).astype(BF16)
    return jnp.concatenate([high, low], axis=1)


def section_xz_kernel(
    message, marks, conv_c, conv_d, spread,
    probability, back,
    two_s, ref_one_s, delta_two_s, delta_one_s, ref_two, bands, grads,
):
    left, inside = edge_gates()
    band_c, band_d, band_dt, band_ct = [bands.at[k] for k in range(4)]
    rows = marks.shape[0]
    half = (rows - MORE) // 2
    upper = slice(half, 2 * half)
    for shifted in (two_s, ref_one_s, delta_two_s, delta_one_s):
        clear_margins(shifted)
    places = windows_of(two_s)
    run(fill_band(conv_c, band_c, 1, False))
    load_features(message, two_s)
    steps = fill_band(conv_d, band_d, 2, False)
    for plane, window in places:
        value = gated(softplus(conv_window(two_s, plane, window, band_c)), inside)
        store_shifted(ref_one_s, plane, 256 * window, value, 2)
        run(steps[:1])
        steps = steps[1:]
    steps = fill_band(conv_d, band_dt, 2, True)
    for plane, window in places:
        value = softplus(conv_window(ref_one_s, plane, window, band_d))
        ref_two[plane, :, 256 * window : 256 * window + 256] = value.astype(BF16)
        run(steps[:1])
        steps = steps[1:]

    labels = marks[:, 0:32].astype(F32)
    spread_one, spread_two = spread[0:32, :], spread[32:64, :]
    first, second = None, None
    for plane in range(2):
        lanes = slice(512 * plane, 512 * plane + 512)
        one = lax.dot_general(
            two_s[plane, 1, :, 128:640], spread_one[:, lanes], CONTRACT_LANES,
            preferred_element_type=F32,
        )
        two = lax.dot_general(
            ref_two[plane], spread_two[:, lanes], CONTRACT_LANES, preferred_element_type=F32
        )
        first = one if first is None else first + one
        second = two if second is None else second + two
    first = first.astype(BF16).astype(F32)
    second = second + first
    share = 1.0 / (1.0 + jnp.exp(-second))
    probability[...] = share[: rows - MORE]
    error_two = gated(share - labels, inside)
    error_one = 1.0 / (1.0 + jnp.exp(-first)) - labels + error_two
    error_two = split(error_two)
    error_one = split(error_one)
    spread_one = jnp.concatenate([spread_one, spread_one], axis=0)
    spread_two = jnp.concatenate([spread_two, spread_two], axis=0)

    for plane, window in places:
        at = 256 * window
        lanes = slice(512 * plane + at, 512 * plane + at + 256)
        value = jnp.dot(error_two, spread_two[:, lanes], preferred_element_type=F32)
        value = value * slope(ref_two[plane, :, at : at + 256])
        store_shifted(delta_two_s, plane, at, value, 2)
    grads[...] = jnp.zeros(grads.shape, F32)
    fills = fill_band(conv_c, band_ct, 1, True)
    sums = weight_grad(centre(delta_two_s), ref_one_s, 2, grads, 9, left)
    for plane, window in places:
        at = 256 * window
        value = conv_window(delta_two_s, plane, window, band_dt)
        stored = ref_one_s[plane, 1, :, 128 + at : 384 + at]
        value = gated(value * slope(stored), inside)
        store_shifted(delta_one_s, plane, at, value, 1)
        run(fills[:1] + sums[:1])
        fills, sums = fills[1:], sums[1:]
    sums = weight_grad(centre(delta_one_s), two_s, 1, grads, 0, left)
    for window in range(2):
        values = []
        for plane in range(2):
            at = 256 * window
            lanes = slice(512 * plane + at, 512 * plane + at + 256)
            value = conv_window(delta_one_s, plane, window, band_ct)
            value = value + jnp.dot(error_one, spread_one[:, lanes], preferred_element_type=F32)
            values.append([value[:half].astype(BF16), value[upper].astype(BF16)])
        for z in range(8):
            lanes = slice(32 * z, 32 * z + 32)
            back[8 * window + z, :half] = jnp.concatenate(
                [
                    values[0][0][:, lanes], values[1][0][:, lanes],
                    values[0][1][:, lanes], values[1][1][:, lanes],
                ],
                axis=1,
            )
        run(sums[:1])
        sums = sums[1:]

    same = own_voxel()
    same = jnp.concatenate([same, same], axis=0)
    kept_rows = slice(0, rows - MORE)

    def head_grad(errors, planes):
        error = counted(errors[kept_rows], left)
        total = None
        for plane, feature in enumerate(planes):
            full = lax.dot_general(error, feature, CONTRACT_ROWS, preferred_element_type=F32)
            kept = jnp.where(same[:, 512 * plane : 512 * plane + 512], full, 0.0)
            kept = jnp.sum(kept, axis=0, keepdims=True)
            kept = kept[:, 0:128] + kept[:, 128:256] + kept[:, 256:384] + kept[:, 384:512]
            total = kept if total is None else total + kept
        total = total + pltpu.roll(total, 64, 1)
        total = total + pltpu.roll(total, 32, 1)
        return total[:, 0:32]

    run(sums)
    features = [two_s[plane, 1, kept_rows, 128:640] for plane in range(2)]
    put_piece(grads, 18, head_grad(error_one, features))
    features = [ref_two[plane, kept_rows, :] for plane in range(2)]
    put_piece(grads, 19, head_grad(error_two, features))
    blank = jnp.zeros((6, 128), F32)
    for peer in range(16):
        chunk = jnp.concatenate([grads[10 * peer : 10 * peer + 10, :], blank], axis=0)
        back[peer, half : half + 16, :] = chunk.astype(BF16)


def backward_xy_kernel(
    back, hidden_two, one_s, stem_s, conv_b,
    mine_out, theirs_out, delta_a,
    delta_b_s, delta_b, grads, band_bt,
):
    first, inside = edge_gates()
    run(fill_band(conv_b, band_bt, 2, True))
    clear_margins(delta_b_s)
    half = back.shape[1] - 16
    for group in range(8):
        parts = []
        for side in range(2):
            at = 64 * side
            parts.append(
                jnp.concatenate(
                    [back[2 * group + q, :half, at : at + 64] for q in range(2)], axis=1
                ).astype(F32)
            )
        lanes = slice(128 * group, 128 * group + 128)
        value = jnp.concatenate(parts + [jnp.zeros((MORE, 128), F32)], axis=0)
        value = gated(value * slope(hidden_two[0, :, lanes]), inside)
        delta_b[0, :, lanes] = value.astype(BF16)
        store_shifted(delta_b_s, 0, 128 * group, value, 2)
    for window in range(4):
        at = 256 * window
        value = conv_window(delta_b_s, 0, window, band_bt)
        stored = one_s[0, 1, :, 128 + at : 384 + at]
        value = gated(value * slope(stored), inside)
        delta_a[0, :, at : at + 256] = value.astype(BF16)
    grads[...] = jnp.zeros(grads.shape, F32)
    run(weight_grad(delta_b, one_s, 2, grads, 9, first))
    run(weight_grad(delta_a, stem_s, 1, grads, 0, first))
    chunk = back[0, half:, :].astype(F32)
    for peer in range(1, 16):
        chunk = chunk + back[peer, half:, :].astype(F32)
    last = [grads[128 + 16 * (k % 2) : 144 + 16 * (k % 2), 32 * (k // 2) : 32 * (k // 2) + 32] for k in range(4)]
    grads[128:144, :] = jnp.concatenate(last, axis=1)
    core = lax.rem(lax.axis_index("gx"), 2)
    mine_out[0:72, :] = grads[pl.ds(pl.multiple_of(72 * core, 8), 72), :]
    theirs_out[0:72, :] = grads[pl.ds(pl.multiple_of(72 * (1 - core), 8), 72), :]
    mine_out[72:88, :] = chunk
    theirs_out[72:88, :] = chunk


def stem_grad_kernel(delta_a, probability, conv_a, stem_grad, leaving, delta_a_s, band_at):
    rows = delta_a.shape[1]
    cols = rows - 2 * MORE
    tail = slice(cols, cols + MORE)
    clear_margins(delta_a_s)
    run(fill_band(conv_a, band_at, 1, True))
    for window in range(4):
        lanes = slice(256 * window, 256 * window + 256)
        store_shifted(delta_a_s, 0, 256 * window, delta_a[0, :, lanes].astype(F32), 1)
    for window in range(4):
        lanes = slice(256 * window, 256 * window + 256)
        value = conv_window(delta_a_s, 0, window, band_at).astype(BF16)
        stem_grad[:, lanes] = value[:cols]
        leaving[:, lanes] = value[tail]
    rest = probability[tail, :]
    parts = []
    for _ in range(3):
        parts.append(rest.astype(BF16))
        rest = rest - parts[-1].astype(F32)
    parts.append(jnp.zeros((MORE, 32), BF16))
    leaving[:, 1024:1152] = jnp.concatenate(parts, axis=1)


def place_kernel(found, probability, moved, stem_grad, share, flat):
    cols = stem_grad.shape[2]
    first, _ = edge_gates()
    row = lax.broadcasted_iota(jnp.int32, (MORE, 1), 0)
    taken = jnp.where(row < LEFT, 1.0 - first, 0.0)
    for group in range(8):
        lanes = slice(128 * group, 128 * group + 128)
        mine = found[:, lanes].astype(F32)
        head = mine[:MORE] * (1.0 - taken) + moved[:, lanes].astype(F32) * taken
        value = jnp.concatenate([head, mine[MORE:]], axis=0)
        for side in range(cols // 128):
            turned = value[128 * side : 128 * side + 128].T
            for k in range(4):
                start = 1024 * side + 4 * group + k
                flat[pl.ds(start, 32, stride=32), :] = turned[32 * k : 32 * k + 32]
    for side in range(cols // 128):
        part = flat[1024 * side : 1024 * side + 1024, :].reshape(32, 32, 128)
        stem_grad[:, :, 128 * side : 128 * side + 128] = part.astype(BF16)
    parts = moved[:, 1024:1152].astype(F32)
    head = parts[:, 0:32] + parts[:, 32:64] + parts[:, 64:96]
    head = probability[:MORE, :] * (1.0 - taken) + head * taken
    value = jnp.concatenate([head, probability[MORE:cols, :]], axis=0).T
    share[:, 0, :] = value[0:16]
    share[:, 1, :] = value[16:32]


def finish_cd_kernel(factor, chunks, grad_c, grad_d, head_one, head_two, flat):
    for peer in range(16):
        flat[10 * peer : 10 * peer + 10, :] = chunks[peer, 0:10, :].astype(F32) * factor

    def piece(index):
        row, lane = 32 * (index // 4), 32 * (index % 4)
        return flat[row : row + 32, lane : lane + 32]

    for tap in range(9):
        grad_c[tap // 3, tap % 3] = piece(tap)
        grad_d[tap // 3, tap % 3] = piece(9 + tap)
    head_one[...] = piece(18)[0:1]
    head_two[...] = piece(19)[0:1]


def finish_ab_kernel(factor, mine, theirs, grad_a, grad_b, flat):
    core = lax.rem(lax.axis_index("gx"), 2)
    flat[pl.ds(pl.multiple_of(72 * core, 8), 72), :] = mine[...] * factor
    flat[pl.ds(pl.multiple_of(72 * (1 - core), 8), 72), :] = theirs[...] * factor

    def piece(index):
        row, lane = 32 * (index // 4), 32 * (index % 4)
        if index >= 16:
            lane = 64 * (index % 4)
            halves = [flat[row : row + 16, lane + at : lane + at + 32] for at in (0, 32)]
            return jnp.concatenate(halves, axis=0)
        return flat[row : row + 32, lane : lane + 32]

    for tap in range(9):
        grad_a[tap // 3, tap % 3] = piece(tap)
        grad_b[tap // 3, tap % 3] = piece(9 + tap)


def call(kernel, outs, ins, scratch=(), flops=0, megabytes=16):
    places = [place for _, place in outs]
    shapes = [pltpu.HBM(out.shape, out.dtype) if place is HBM else out for out, place in outs]

    def run(*operands):
        operands = [
            pltpu.with_memory_space_constraint(operand, pltpu.HBM) if place is HBM else operand
            for operand, place in zip(operands, ins)
        ]
        return bound(*operands)

    bound = pl.pallas_call(
        kernel,
        out_shape=shapes,
        in_specs=ins,
        out_specs=list(places),
        scratch_shapes=scratch,
        compiler_params=pltpu.CompilerParams(vmem_limit_bytes=megabytes * 1024 * 1024),
        cost_estimate=pl.CostEstimate(flops=flops, bytes_accessed=1 << 20, transcendentals=0),
    )
    return run


def shape(dims, dtype):
    return jax.ShapeDtypeStruct(dims, dtype)


def sum_everywhere(mine, theirs, beside, later, slab, gx):
    peers, copies = lax.axis_size(gx), lax.axis_size(slab)
    swap = [(i, i ^ 1) for i in range(peers)]
    theirs, beside = lax.optimization_barrier((lax.ppermute(theirs, gx, swap), beside))
    mine = mine + theirs
    spread = jnp.broadcast_to(mine.astype(BF16)[None], (peers // 2,) + mine.shape)
    same_core = [[i for i in range(peers) if i % 2 == core] for core in range(2)]
    mine = lax.all_to_all(spread, gx, 0, 0, tiled=True, axis_index_groups=same_core)
    mine = jnp.sum(mine.astype(F32), axis=0)
    spread = jnp.broadcast_to(mine.astype(BF16)[None], (copies,) + mine.shape)
    found = lax.all_to_all(spread, slab, 0, 0, tiled=True)
    found, beside = lax.optimization_barrier((found, later(beside)))
    mine = jnp.sum(found[:, :72].astype(F32), axis=0)
    return (mine, lax.ppermute(mine, gx, swap), found[:, 72:]), beside


def per_device(stem_features, labels, conv_a, conv_b, conv_c, conv_d, head_one, head_two):
    _, depth, height, cols = stem_features.shape
    rows = cols + HALO
    half = rows // 2
    peers = lax.axis_size("gx")
    up = [(i, i + 1) for i in range(peers - 1)]
    down = [(j, i) for i, j in up]
    sems = lambda count: pltpu.SemaphoreType.DMA((count,))
    vmem = lambda kind: pltpu.VMEM(kind.shape, kind.dtype)

    stem_features = stem_features[:, 0]
    near = pltpu.VMEM((C, height, 128), BF16)
    near_labels = pltpu.VMEM((16, 2, 128), labels.dtype)
    (initial,) = call(
        edge_kernel, [(shape((HALO, 1152), BF16), VMEM)], [HBM, HBM],
        [pltpu.VMEM((1024, 128), F32), near, near_labels, sems(5)], flops=1 << 28, megabytes=3,
    )(stem_features, labels)
    after = lax.ppermute(initial, "gx", down)

    taps_a, taps_b, taps_c, taps_d = [
        jnp.transpose(w, (1, 2, 0, 3)) for w in (conv_a, conv_b, conv_c, conv_d)
    ]
    band = shape((1536, 256), BF16)
    spreads = shape((64, 1024), BF16)
    stem, marks, band_a, band_b, spread = call(
        arrange_kernel,
        [
            (shape((cols, 1024), BF16), VMEM),
            (shape((cols, 128), BF16), VMEM),
            (band, VMEM),
            (band, VMEM),
            (spreads, VMEM),
        ],
        [HBM] * 6,
        [pltpu.VMEM((1024 * cols // 128, 128), F32), vmem(stem_features), vmem(labels)]
        + [vmem(taps_a), vmem(taps_b), pltpu.VMEM((2, 1, C), BF16), sems(9)],
        flops=1 << 29, megabytes=6,
    )(stem_features, labels, taps_a, taps_b, head_one[None], head_two[None])

    shifted = shape((1, 3, rows, 1280), BF16)
    wide = vmem(shifted)
    tall = pltpu.VMEM((2, 3, rows, 768), BF16)
    whole = shape((1, rows, 1024), BF16)
    planes = shape((2, rows, 512), BF16)
    messages = shape((16, half, 128), BF16)
    stem_s, one_s, hidden_two, marks, message = call(
        forward_xy_kernel,
        [(shifted, VMEM)] * 2
        + [(whole, VMEM), (shape((rows, 128), BF16), VMEM), (messages, VMEM)],
        [VMEM] * 5, flops=1 << 30, megabytes=8,
    )(stem, marks, after, band_a, band_b)
    message = lax.all_to_all(message, "slab", 0, 0, tiled=True)

    larger = shape((16, (cols + MORE) // 2 + MORE, 128), BF16)
    probability, back = call(
        section_xz_kernel,
        [(shape((rows - MORE, 32), F32), VMEM), (larger, VMEM)],
        [VMEM] * 5,
        [tall, tall, tall, tall, vmem(planes), pltpu.VMEM((4, 1536, 256), BF16)]
        + [pltpu.VMEM((160, 128), F32)],
        flops=1 << 31, megabytes=28,
    )(message, marks, taps_c, taps_d, spread)
    back = lax.all_to_all(back, "slab", 0, 0, tiled=True)

    half_sums = shape((88, 128), F32)
    mine, theirs, delta_a = call(
        backward_xy_kernel,
        [(half_sums, VMEM), (half_sums, VMEM), (whole, VMEM)],
        [VMEM] * 5,
        [wide, vmem(whole), pltpu.VMEM((160, 128), F32), vmem(band)],
        flops=1 << 31, megabytes=16,
    )(back, hidden_two, one_s, stem_s, taps_b)
    edge = shape((MORE, 1152), BF16)
    beside = call(
        stem_grad_kernel,
        [(shape((cols, 1024), BF16), VMEM), (edge, VMEM)],
        [VMEM] * 3, [wide, vmem(band)], flops=1 << 30, megabytes=6,
    )(delta_a, probability, taps_a)

    def place(beside):
        found, leaving = beside
        moved = lax.ppermute(leaving, "gx", up)
        return call(
            place_kernel,
            [(shape((C, height, cols), BF16), VMEM), (shape((16, 2, cols), F32), VMEM)],
            [VMEM] * 3, [pltpu.VMEM((1024 * cols // 128, 128), F32)], flops=1 << 28, megabytes=4,
        )(found, probability, moved)

    (mine, theirs, chunks), (stem_grad, probability) = sum_everywhere(
        mine, theirs, beside, place, "slab", "gx"
    )

    taps = shape((3, 3, C, C), F32)
    head = shape((1, C), F32)
    factor = 1.0 / (depth * height * cols)
    grad_c, grad_d, grad_one, grad_two = call(
        functools.partial(finish_cd_kernel, factor), [(taps, VMEM)] * 2 + [(head, VMEM)] * 2,
        [VMEM], [pltpu.VMEM((160, 128), F32)], flops=1 << 24, megabytes=2,
    )(chunks)
    grad_a, grad_b = call(
        functools.partial(finish_ab_kernel, factor), [(taps, VMEM)] * 2,
        [VMEM] * 2, [pltpu.VMEM((144, 128), F32)], flops=1 << 20, megabytes=2,
    )(mine, theirs)
    kernels = [jnp.transpose(grad, (2, 0, 1, 3)) for grad in (grad_a, grad_b, grad_c, grad_d)]
    return (probability, stem_grad[:, None], *kernels, grad_one[0], grad_two[0])


def solution(mesh):
    return jax.shard_map(
        per_device,
        mesh=mesh,
        in_specs=(P(None, "slab", None, "gx"), P(None, "slab", "gx"), P(), P(), P(), P(), P(), P()),
        out_specs=(
            P(None, "slab", "gx"),
            P(None, "slab", None, "gx"),
            P(),
            P(),
            P(),
            P(),
            P(),
            P(),
        ),
        check_vma=False,
    )
```

```python
import functools

import jax
import jax.numpy as jnp
from jax import lax
from jax.experimental import pallas as pl
from jax.experimental.pallas import tpu as pltpu
from jax.sharding import PartitionSpec as P

HALO = 32
LEFT = 12
MORE = 16
C = 32
F32 = jnp.float32
BF16 = jnp.bfloat16
VMEM = pl.BlockSpec(memory_space=pltpu.VMEM)
HBM = pl.BlockSpec(memory_space=pltpu.HBM)
CONTRACT_ROWS = (((0,), (0,)), ((), ()))
CONTRACT_LANES = (((1,), (1,)), ((), ()))


def softplus(v):
    small = jnp.exp(-jnp.abs(v))
    tail = jnp.where(small < 1e-4, small, jnp.log(1.0 + small))
    return jnp.maximum(v, 0.0) + tail


def slope(stored):
    return 1.0 - jnp.exp(-stored.astype(F32))


def edge_gates():
    me, peers = lax.axis_index("gx"), lax.axis_size("gx")
    return jnp.where(me > 0, 0.0, 1.0), jnp.where(me < peers - 1, 1.0, 0.0)


def counted(value, first):
    row = lax.broadcasted_iota(jnp.int32, (MORE, 1), 0)
    cols = value.shape[0] - MORE
    head = value[:MORE].astype(F32) * jnp.where(row < LEFT, first, 1.0)
    tail = value[cols:].astype(F32) * jnp.where(row < LEFT, 1.0, 0.0)
    head, tail = head.astype(value.dtype), tail.astype(value.dtype)
    return jnp.concatenate([head, value[MORE:cols], tail], axis=0)


def gated(value, inside):
    cols = value.shape[0] - HALO
    return jnp.concatenate([value[:cols], value[cols:] * inside], axis=0)


def clear_margins(shifted):
    lanes = shifted.shape[-1]
    edge = jnp.zeros(shifted.shape[:-1] + (128,), BF16)
    shifted[..., 0:128] = edge
    shifted[..., lanes - 128 : lanes] = edge


def store_shifted(shifted, plane, start, value, step):
    rows, lanes = value.shape
    where = slice(128 + start, 128 + start + lanes)
    shifted[plane, 1, :, where] = value.astype(BF16)
    lower = pltpu.roll(value, step, 0)
    row = lax.broadcasted_iota(jnp.int32, (8, lanes), 0)
    lower = jnp.concatenate([jnp.where(row < step, 0.0, lower[:8]), lower[8:]], axis=0)
    shifted[plane, 0, :, where] = lower.astype(BF16)
    shifted[plane, 2, :, where] = pltpu.roll(value, rows - step, 0).astype(BF16)


def conv_window(shifted, plane, window, band):
    lanes = slice(256 * window, 256 * window + 512)
    columns = jnp.concatenate([shifted[plane, tap, :, lanes] for tap in range(3)], axis=1)
    return jnp.dot(columns, band[...], preferred_element_type=F32)


def windows_of(shifted):
    planes = shifted.shape[0]
    windows = (shifted.shape[-1] - 256) // 256
    return [(plane, window) for plane in range(planes) for window in range(windows)]


def weight_grad(delta, shifted, step, grads, first_piece, first):
    part = slice(0, delta.shape[1] - MORE)
    places = windows_of(shifted)
    left = jnp.concatenate(
        [
            counted(delta[plane, part, 256 * window : 256 * window + 256], first)
            for plane, window in places
        ],
        axis=0,
    )

    def step_of(tap):
        right = jnp.concatenate(
            [
                shifted[plane, tap, part, 256 * window : 256 * window + 512]
                for plane, window in places
            ],
            axis=0,
        )
        total = lax.dot_general(left, right, CONTRACT_ROWS, preferred_element_type=F32)
        folded = None
        for r in range(4):
            near = total[32 * r : 32 * r + 32, 0:384]
            far = total[32 * r + 128 : 32 * r + 160, 128:512]
            both = near + far
            if r:
                both = pltpu.roll(both, 384 - 32 * r, 1)
            folded = both if folded is None else folded + both
        for row_tap in range(3):
            at = 32 * (4 + step * (row_tap - 1))
            put_piece(grads, first_piece + 3 * row_tap + tap, folded[:, at : at + 32])

    return [functools.partial(step_of, tap) for tap in range(3)]


def run(steps):
    for step in steps:
        step()


def put_piece(grads, index, value):
    row, lane = 32 * (index // 4), 32 * (index % 4)
    grads[row : row + value.shape[0], lane : lane + 32] = value


def fill_tap(weight, band, step, backward, col_tap):
    lane = lax.broadcasted_iota(jnp.int32, (32, 128), 1) // 32
    cut = []
    for row_tap in range(3):
        if backward:
            block = weight[2 - row_tap, 2 - col_tap].astype(F32)
        else:
            block = weight[row_tap, col_tap].astype(F32).T
        block = jnp.concatenate([block] * 4, axis=1)
        cut.append([jnp.where(lane == q, block, 0.0) for q in range(4)])
    for source in range(16):
        for group in range(2):
            panel = None
            for q in range(4):
                off = source - 4 - (4 * group + q)
                if off % step == 0 and abs(off) <= step:
                    term = cut[off // step + 1][q]
                    panel = term if panel is None else panel + term
            if panel is None:
                panel = jnp.zeros((32, 128), F32)
            row = 512 * col_tap + 32 * source
            band[row : row + 32, 128 * group : 128 * group + 128] = panel.astype(BF16)


def fill_band(weight, band, step, backward):
    return [
        functools.partial(fill_tap, weight, band, step, backward, col_tap) for col_tap in range(3)
    ]


class Copies:
    def __init__(self, sems):
        self.sems, self.started = sems, []

    def start(self, source, target):
        copy = pltpu.make_async_copy(source, target, self.sems.at[len(self.started)])
        copy.start()
        self.started.append(copy)
        return copy

    def start_lanes(self, source, target, parts):
        size = source.shape[-1] // parts
        return [
            self.start(
                source.at[..., pl.ds(size * k, size)], target.at[..., pl.ds(size * k, size)]
            )
            for k in range(parts)
        ]


def wait_all(copies):
    for copy in copies:
        copy.wait()


def centre(shifted):
    return shifted.at[:, 1, :, pl.ds(128, shifted.shape[-1] - 256)]


def columns_first(stem, flat, side, group):
    first = 1024 * side + 4 * group
    rows = [flat[pl.ds(first + k, 32, stride=32), :] for k in range(4)]
    return jnp.concatenate(rows, axis=0).T


def fill_flat(stem, flat, side):
    part = stem[:, :, 128 * side : 128 * side + 128].reshape(1024, 128)
    flat[1024 * side : 1024 * side + 1024, :] = part.astype(F32)


def marks_first(labels):
    marks = labels.astype(F32)
    blank = jnp.zeros((96, labels.shape[2]), F32)
    marks = jnp.concatenate([marks[:, 0, :], marks[:, 1, :], blank], axis=0)
    return marks.T.astype(BF16)


def edge_kernel(
    stem_in, labels_in, conv_a_in, conv_b_in, head_one_in, head_two_in,
    initial, stem, labels, conv_a, conv_b, heads, flat, sems,
):
    copies = Copies(sems)
    for side in range(stem.shape[2] // 128):
        lanes = pl.ds(128 * side, 128)
        for k in range(4):
            rows = pl.ds(8 * k, 8)
            copies.start(stem_in.at[rows, :, lanes], stem.at[rows, :, lanes])
        if side == 0:
            copies.start(labels_in, labels)
    copies.start(conv_a_in, conv_a)
    copies.start(conv_b_in, conv_b)
    copies.start(head_one_in, heads.at[0])
    copies.start(head_two_in, heads.at[1])
    wait_all(copies.started[:5])
    fill_flat(stem, flat, 0)
    for group in range(8):
        value = columns_first(stem, flat, 0, group)
        initial[:, 128 * group : 128 * group + 128] = value[:HALO].astype(BF16)
    initial[:, 1024:1152] = marks_first(labels[:, :, :128])[:HALO]
    wait_all(copies.started[5:])


def arrange_kernel(
    stem, labels, conv_a, conv_b, heads,
    stem_out, marks_out, band_a, band_b, spread, flat,
):
    cols = stem.shape[2]
    same = own_voxel()
    for k in range(2):
        four = jnp.concatenate([heads[k].astype(F32)] * 4, axis=1)
        along = jnp.concatenate([four] * 8, axis=1)
        spread[32 * k : 32 * k + 32, :] = jnp.where(same, along, 0.0).astype(BF16)
    marks_out[...] = marks_first(labels[...])
    run(fill_band(conv_a, band_a, 1, False))
    run(fill_band(conv_b, band_b, 2, False))
    for side in range(cols // 128):
        fill_flat(stem, flat, side)
    for group in range(8):
        sides = [columns_first(stem, flat, side, group) for side in range(cols // 128)]
        value = jnp.concatenate(sides, axis=0).astype(BF16)
        stem_out[:, 128 * group : 128 * group + 128] = value


def own_voxel():
    voxel = lax.broadcasted_iota(jnp.int32, (32, 1024), 0)
    return voxel == lax.broadcasted_iota(jnp.int32, (32, 1024), 1) // 32


def forward_xy_kernel(
    stem, marks, after, band_a, band_b,
    stem_s, one_s, hidden_two, marks_out, message,
):
    _, inside = edge_gates()
    clear_margins(stem_s)
    clear_margins(one_s)
    for window in range(4):
        lanes = slice(256 * window, 256 * window + 256)
        value = jnp.concatenate([stem[:, lanes], after[:, lanes]], axis=0)
        store_shifted(stem_s, 0, 256 * window, value.astype(F32), 1)
    marks_out[...] = jnp.concatenate([marks[...], after[:, 1024:1152]], axis=0)
    for window in range(4):
        value = gated(softplus(conv_window(stem_s, 0, window, band_a)), inside)
        store_shifted(one_s, 0, 256 * window, value, 2)
    for window in range(4):
        value = gated(softplus(conv_window(one_s, 0, window, band_b)), inside).astype(BF16)
        hidden_two[0, :, 256 * window : 256 * window + 256] = value
        half = value.shape[0] // 2
        for peer in range(4):
            lanes = slice(64 * peer, 64 * peer + 64)
            message[4 * window + peer] = jnp.concatenate(
                [value[:half, lanes], value[half:, lanes]], axis=1
            )


def load_features(message, two_s):
    for plane in range(2):
        for group in range(4):
            parts = []
            for side in range(2):
                at = 64 * side + 32 * plane
                parts.append(
                    jnp.concatenate(
                        [message[4 * group + q][:, at : at + 32] for q in range(4)], axis=1
                    )
                )
            value = jnp.concatenate(parts, axis=0).astype(F32)
            store_shifted(two_s, plane, 128 * group, value, 1)


def split(error):
    high = error.astype(BF16)
    low = (error - high.astype(F32)).astype(BF16)
    return jnp.concatenate([high, low], axis=1)


def section_xz_kernel(
    message, marks, conv_c, conv_d, spread,
    probability, back,
    two_s, ref_one_s, delta_two_s, delta_one_s, ref_two, bands, grads,
):
    left, inside = edge_gates()
    band_c, band_d, band_dt, band_ct = [bands.at[k] for k in range(4)]
    rows = marks.shape[0]
    half = (rows - MORE) // 2
    upper = slice(half, 2 * half)
    for shifted in (two_s, ref_one_s, delta_two_s, delta_one_s):
        clear_margins(shifted)
    places = windows_of(two_s)
    run(fill_band(conv_c, band_c, 1, False))
    load_features(message, two_s)
    steps = fill_band(conv_d, band_d, 2, False)
    for plane, window in places:
        value = gated(softplus(conv_window(two_s, plane, window, band_c)), inside)
        store_shifted(ref_one_s, plane, 256 * window, value, 2)
        run(steps[:1])
        steps = steps[1:]
    steps = fill_band(conv_d, band_dt, 2, True)
    for plane, window in places:
        value = softplus(conv_window(ref_one_s, plane, window, band_d))
        ref_two[plane, :, 256 * window : 256 * window + 256] = value.astype(BF16)
        run(steps[:1])
        steps = steps[1:]

    labels = marks[:, 0:32].astype(F32)
    spread_one, spread_two = spread[0:32, :], spread[32:64, :]
    first, second = None, None
    for plane in range(2):
        lanes = slice(512 * plane, 512 * plane + 512)
        one = lax.dot_general(
            two_s[plane, 1, :, 128:640], spread_one[:, lanes], CONTRACT_LANES,
            preferred_element_type=F32,
        )
        two = lax.dot_general(
            ref_two[plane], spread_two[:, lanes], CONTRACT_LANES, preferred_element_type=F32
        )
        first = one if first is None else first + one
        second = two if second is None else second + two
    first = first.astype(BF16).astype(F32)
    second = second + first
    share = 1.0 / (1.0 + jnp.exp(-second))
    probability[...] = share[: rows - MORE]
    error_two = gated(share - labels, inside)
    error_one = 1.0 / (1.0 + jnp.exp(-first)) - labels + error_two
    error_two = split(error_two)
    error_one = split(error_one)
    spread_one = jnp.concatenate([spread_one, spread_one], axis=0)
    spread_two = jnp.concatenate([spread_two, spread_two], axis=0)

    for plane, window in places:
        at = 256 * window
        lanes = slice(512 * plane + at, 512 * plane + at + 256)
        value = jnp.dot(error_two, spread_two[:, lanes], preferred_element_type=F32)
        value = value * slope(ref_two[plane, :, at : at + 256])
        store_shifted(delta_two_s, plane, at, value, 2)
    grads[...] = jnp.zeros(grads.shape, F32)
    fills = fill_band(conv_c, band_ct, 1, True)
    sums = weight_grad(centre(delta_two_s), ref_one_s, 2, grads, 9, left)
    for plane, window in places:
        at = 256 * window
        value = conv_window(delta_two_s, plane, window, band_dt)
        stored = ref_one_s[plane, 1, :, 128 + at : 384 + at]
        value = gated(value * slope(stored), inside)
        store_shifted(delta_one_s, plane, at, value, 1)
        run(fills[:1] + sums[:1])
        fills, sums = fills[1:], sums[1:]
    sums = weight_grad(centre(delta_one_s), two_s, 1, grads, 0, left)
    for window in range(2):
        values = []
        for plane in range(2):
            at = 256 * window
            lanes = slice(512 * plane + at, 512 * plane + at + 256)
            value = conv_window(delta_one_s, plane, window, band_ct)
            value = value + jnp.dot(error_one, spread_one[:, lanes], preferred_element_type=F32)
            values.append([value[:half].astype(BF16), value[upper].astype(BF16)])
        for z in range(8):
            lanes = slice(32 * z, 32 * z + 32)
            back[8 * window + z, :half] = jnp.concatenate(
                [
                    values[0][0][:, lanes], values[1][0][:, lanes],
                    values[0][1][:, lanes], values[1][1][:, lanes],
                ],
                axis=1,
            )
        run(sums[:1])
        sums = sums[1:]

    same = own_voxel()
    same = jnp.concatenate([same, same], axis=0)
    kept_rows = slice(0, rows - MORE)

    def head_grad(errors, planes):
        error = counted(errors[kept_rows], left)
        total = None
        for plane, feature in enumerate(planes):
            full = lax.dot_general(error, feature, CONTRACT_ROWS, preferred_element_type=F32)
            kept = jnp.where(same[:, 512 * plane : 512 * plane + 512], full, 0.0)
            kept = jnp.sum(kept, axis=0, keepdims=True)
            kept = kept[:, 0:128] + kept[:, 128:256] + kept[:, 256:384] + kept[:, 384:512]
            total = kept if total is None else total + kept
        total = total + pltpu.roll(total, 64, 1)
        total = total + pltpu.roll(total, 32, 1)
        return total[:, 0:32]

    run(sums)
    features = [two_s[plane, 1, kept_rows, 128:640] for plane in range(2)]
    put_piece(grads, 18, head_grad(error_one, features))
    features = [ref_two[plane, kept_rows, :] for plane in range(2)]
    put_piece(grads, 19, head_grad(error_two, features))
    blank = jnp.zeros((6, 128), F32)
    for peer in range(16):
        chunk = jnp.concatenate([grads[10 * peer : 10 * peer + 10, :], blank], axis=0)
        back[peer, half : half + 16, :] = chunk.astype(BF16)


def backward_xy_kernel(
    back, hidden_two, one_s, stem_s, conv_b,
    mine_out, theirs_out, delta_a,
    delta_b_s, delta_b, grads, band_bt,
):
    first, inside = edge_gates()
    run(fill_band(conv_b, band_bt, 2, True))
    clear_margins(delta_b_s)
    half = back.shape[1] - 16
    for group in range(8):
        parts = []
        for side in range(2):
            at = 64 * side
            parts.append(
                jnp.concatenate(
                    [back[2 * group + q, :half, at : at + 64] for q in range(2)], axis=1
                ).astype(F32)
            )
        lanes = slice(128 * group, 128 * group + 128)
        value = jnp.concatenate(parts + [jnp.zeros((MORE, 128), F32)], axis=0)
        value = gated(value * slope(hidden_two[0, :, lanes]), inside)
        delta_b[0, :, lanes] = value.astype(BF16)
        store_shifted(delta_b_s, 0, 128 * group, value, 2)
    for window in range(4):
        at = 256 * window
        value = conv_window(delta_b_s, 0, window, band_bt)
        stored = one_s[0, 1, :, 128 + at : 384 + at]
        value = gated(value * slope(stored), inside)
        delta_a[0, :, at : at + 256] = value.astype(BF16)
    grads[...] = jnp.zeros(grads.shape, F32)
    run(weight_grad(delta_b, one_s, 2, grads, 9, first))
    run(weight_grad(delta_a, stem_s, 1, grads, 0, first))
    chunk = back[0, half:, :].astype(F32)
    for peer in range(1, 16):
        chunk = chunk + back[peer, half:, :].astype(F32)
    last = [grads[128 + 16 * (k % 2) : 144 + 16 * (k % 2), 32 * (k // 2) : 32 * (k // 2) + 32] for k in range(4)]
    grads[128:144, :] = jnp.concatenate(last, axis=1)
    core = lax.rem(lax.axis_index("gx"), 2)
    mine_out[0:72, :] = grads[pl.ds(pl.multiple_of(72 * core, 8), 72), :]
    theirs_out[0:72, :] = grads[pl.ds(pl.multiple_of(72 * (1 - core), 8), 72), :]
    mine_out[72:88, :] = chunk
    theirs_out[72:88, :] = chunk


def stem_grad_kernel(delta_a, probability, conv_a, stem_grad, leaving, delta_a_s, band_at):
    rows = delta_a.shape[1]
    cols = rows - 2 * MORE
    tail = slice(cols, cols + MORE)
    clear_margins(delta_a_s)
    run(fill_band(conv_a, band_at, 1, True))
    for window in range(4):
        lanes = slice(256 * window, 256 * window + 256)
        store_shifted(delta_a_s, 0, 256 * window, delta_a[0, :, lanes].astype(F32), 1)
    for window in range(4):
        lanes = slice(256 * window, 256 * window + 256)
        value = conv_window(delta_a_s, 0, window, band_at).astype(BF16)
        stem_grad[:, lanes] = value[:cols]
        leaving[:, lanes] = value[tail]
    rest = probability[tail, :]
    parts = []
    for _ in range(3):
        parts.append(rest.astype(BF16))
        rest = rest - parts[-1].astype(F32)
    parts.append(jnp.zeros((MORE, 32), BF16))
    leaving[:, 1024:1152] = jnp.concatenate(parts, axis=1)


def place_kernel(found, probability, moved, stem_grad, share, flat):
    cols = stem_grad.shape[2]
    first, _ = edge_gates()
    row = lax.broadcasted_iota(jnp.int32, (MORE, 1), 0)
    taken = jnp.where(row < LEFT, 1.0 - first, 0.0)
    for group in range(8):
        lanes = slice(128 * group, 128 * group + 128)
        mine = found[:, lanes].astype(F32)
        head = mine[:MORE] * (1.0 - taken) + moved[:, lanes].astype(F32) * taken
        value = jnp.concatenate([head, mine[MORE:]], axis=0)
        for side in range(cols // 128):
            turned = value[128 * side : 128 * side + 128].T
            for k in range(4):
                start = 1024 * side + 4 * group + k
                flat[pl.ds(start, 32, stride=32), :] = turned[32 * k : 32 * k + 32]
    for side in range(cols // 128):
        part = flat[1024 * side : 1024 * side + 1024, :].reshape(32, 32, 128)
        stem_grad[:, :, 128 * side : 128 * side + 128] = part.astype(BF16)
    parts = moved[:, 1024:1152].astype(F32)
    head = parts[:, 0:32] + parts[:, 32:64] + parts[:, 64:96]
    head = probability[:MORE, :] * (1.0 - taken) + head * taken
    value = jnp.concatenate([head, probability[MORE:cols, :]], axis=0).T
    share[:, 0, :] = value[0:16]
    share[:, 1, :] = value[16:32]


def finish_cd_kernel(factor, chunks, grad_c, grad_d, head_one, head_two, flat):
    for peer in range(16):
        upper, z = peer // 8, peer % 8
        chunk = chunks[z, 10 * upper : 10 * upper + 10, :].astype(F32)
        flat[10 * peer : 10 * peer + 10, :] = chunk * factor

    def piece(index):
        row, lane = 32 * (index // 4), 32 * (index % 4)
        return flat[row : row + 32, lane : lane + 32]

    for tap in range(9):
        grad_c[tap // 3, tap % 3] = piece(tap)
        grad_d[tap // 3, tap % 3] = piece(9 + tap)
    head_one[...] = piece(18)[0:1]
    head_two[...] = piece(19)[0:1]


def finish_ab_kernel(factor, mine, theirs, grad_a, grad_b, flat):
    core = lax.rem(lax.axis_index("gx"), 2)
    flat[pl.ds(pl.multiple_of(72 * core, 8), 72), :] = mine[...] * factor
    flat[pl.ds(pl.multiple_of(72 * (1 - core), 8), 72), :] = theirs[...] * factor

    def piece(index):
        row, lane = 32 * (index // 4), 32 * (index % 4)
        if index >= 16:
            lane = 64 * (index % 4)
            halves = [flat[row : row + 16, lane + at : lane + at + 32] for at in (0, 32)]
            return jnp.concatenate(halves, axis=0)
        return flat[row : row + 32, lane : lane + 32]

    for tap in range(9):
        grad_a[tap // 3, tap % 3] = piece(tap)
        grad_b[tap // 3, tap % 3] = piece(9 + tap)


def call(kernel, outs, ins, scratch=(), flops=0, megabytes=16):
    places = [place for _, place in outs]
    shapes = [pltpu.HBM(out.shape, out.dtype) if place is HBM else out for out, place in outs]

    def run(*operands):
        operands = [
            pltpu.with_memory_space_constraint(operand, pltpu.HBM) if place is HBM else operand
            for operand, place in zip(operands, ins)
        ]
        return bound(*operands)

    bound = pl.pallas_call(
        kernel,
        out_shape=shapes,
        in_specs=ins,
        out_specs=list(places),
        scratch_shapes=scratch,
        compiler_params=pltpu.CompilerParams(vmem_limit_bytes=megabytes * 1024 * 1024),
        cost_estimate=pl.CostEstimate(flops=flops, bytes_accessed=1 << 20, transcendentals=0),
    )
    return run


def shape(dims, dtype):
    return jax.ShapeDtypeStruct(dims, dtype)


def sum_everywhere(mine, theirs, beside, later, slab, gx):
    peers, slabs = lax.axis_size(gx), lax.axis_size(slab)
    depth, wide = slabs // 2, peers // 2
    swap = [(i, i ^ 1) for i in range(peers)]
    theirs, beside = lax.optimization_barrier((lax.ppermute(theirs, gx, swap), beside))
    mine = mine + theirs
    across = [
        [(upper * depth + z) * peers + 2 * chip + core for upper in range(2) for chip in range(wide)]
        for z in range(depth)
        for core in range(2)
    ]
    spread = jnp.broadcast_to(mine.astype(BF16)[None], (2 * wide,) + mine.shape)
    found = lax.all_to_all(spread, (slab, gx), 0, 0, tiled=True, axis_index_groups=across)
    found, beside = lax.optimization_barrier((found, later(beside)))
    halves = jnp.sum(found.astype(F32).reshape((2, wide) + mine.shape), axis=1)
    chunks = halves[:, 72:82].reshape(20, 128)
    mine = jnp.concatenate([halves[0, :72] + halves[1, :72], chunks, jnp.zeros((4, 128), F32)])
    along = [[upper * depth + z for z in range(depth)] for upper in range(2)]
    spread = jnp.broadcast_to(mine.astype(BF16)[None], (depth,) + mine.shape)
    found = lax.all_to_all(spread, slab, 0, 0, tiled=True, axis_index_groups=along)
    mine = jnp.sum(found[:, :72].astype(F32), axis=0)
    return (mine, lax.ppermute(mine, gx, swap), found[:, 72:]), beside


def per_device(stem_features, labels, conv_a, conv_b, conv_c, conv_d, head_one, head_two):
    _, depth, height, cols = stem_features.shape
    rows = cols + HALO
    half = rows // 2
    peers = lax.axis_size("gx")
    up = [(i, i + 1) for i in range(peers - 1)]
    down = [(j, i) for i, j in up]
    sems = lambda count: pltpu.SemaphoreType.DMA((count,))
    vmem = lambda kind: pltpu.VMEM(kind.shape, kind.dtype)

    stem_features = stem_features[:, 0]
    taps_a, taps_b, taps_c, taps_d = [
        jnp.transpose(w, (1, 2, 0, 3)) for w in (conv_a, conv_b, conv_c, conv_d)
    ]
    held = [stem_features, labels, taps_a, taps_b]
    initial, *loaded = call(
        edge_kernel,
        [(shape((HALO, 1152), BF16), VMEM)]
        + [(shape(array.shape, array.dtype), VMEM) for array in held]
        + [(shape((2, 1, C), BF16), VMEM)],
        [HBM] * 6, [pltpu.VMEM((1024, 128), F32), sems(13)], flops=1 << 28, megabytes=3,
    )(*held, head_one[None], head_two[None])
    after = lax.ppermute(initial, "gx", down)

    band = shape((1536, 256), BF16)
    spreads = shape((64, 1024), BF16)
    stem, marks, band_a, band_b, spread = call(
        arrange_kernel,
        [
            (shape((cols, 1024), BF16), VMEM),
            (shape((cols, 128), BF16), VMEM),
            (band, VMEM),
            (band, VMEM),
            (spreads, VMEM),
        ],
        [VMEM] * 5,
        [pltpu.VMEM((1024 * cols // 128, 128), F32)],
        flops=1 << 29, megabytes=6,
    )(*loaded)

    shifted = shape((1, 3, rows, 1280), BF16)
    wide = vmem(shifted)
    tall = pltpu.VMEM((2, 3, rows, 768), BF16)
    whole = shape((1, rows, 1024), BF16)
    planes = shape((2, rows, 512), BF16)
    messages = shape((16, half, 128), BF16)
    stem_s, one_s, hidden_two, marks, message = call(
        forward_xy_kernel,
        [(shifted, VMEM)] * 2
        + [(whole, VMEM), (shape((rows, 128), BF16), VMEM), (messages, VMEM)],
        [VMEM] * 5, flops=1 << 30, megabytes=8,
    )(stem, marks, after, band_a, band_b)
    message = lax.all_to_all(message, "slab", 0, 0, tiled=True)

    larger = shape((16, (cols + MORE) // 2 + MORE, 128), BF16)
    probability, back = call(
        section_xz_kernel,
        [(shape((rows - MORE, 32), F32), VMEM), (larger, VMEM)],
        [VMEM] * 5,
        [tall, tall, tall, tall, vmem(planes), pltpu.VMEM((4, 1536, 256), BF16)]
        + [pltpu.VMEM((160, 128), F32)],
        flops=1 << 31, megabytes=28,
    )(message, marks, taps_c, taps_d, spread)
    back = lax.all_to_all(back, "slab", 0, 0, tiled=True)

    half_sums = shape((88, 128), F32)
    mine, theirs, delta_a = call(
        backward_xy_kernel,
        [(half_sums, VMEM), (half_sums, VMEM), (whole, VMEM)],
        [VMEM] * 5,
        [wide, vmem(whole), pltpu.VMEM((160, 128), F32), vmem(band)],
        flops=1 << 31, megabytes=16,
    )(back, hidden_two, one_s, stem_s, taps_b)
    edge = shape((MORE, 1152), BF16)
    beside = call(
        stem_grad_kernel,
        [(shape((cols, 1024), BF16), VMEM), (edge, VMEM)],
        [VMEM] * 3, [wide, vmem(band)], flops=1 << 30, megabytes=6,
    )(delta_a, probability, taps_a)

    def place(beside):
        found, leaving = beside
        moved = lax.ppermute(leaving, "gx", up)
        return call(
            place_kernel,
            [(shape((C, height, cols), BF16), VMEM), (shape((16, 2, cols), F32), VMEM)],
            [VMEM] * 3, [pltpu.VMEM((1024 * cols // 128, 128), F32)], flops=1 << 28, megabytes=4,
        )(found, probability, moved)

    (mine, theirs, chunks), (stem_grad, probability) = sum_everywhere(
        mine, theirs, beside, place, "slab", "gx"
    )

    taps = shape((3, 3, C, C), F32)
    head = shape((1, C), F32)
    factor = 1.0 / (depth * height * cols)
    grad_c, grad_d, grad_one, grad_two = call(
        functools.partial(finish_cd_kernel, factor), [(taps, VMEM)] * 2 + [(head, VMEM)] * 2,
        [VMEM], [pltpu.VMEM((160, 128), F32)], flops=1 << 24, megabytes=2,
    )(chunks)
    grad_a, grad_b = call(
        functools.partial(finish_ab_kernel, factor), [(taps, VMEM)] * 2,
        [VMEM] * 2, [pltpu.VMEM((144, 128), F32)], flops=1 << 20, megabytes=2,
    )(mine, theirs)
    kernels = [jnp.transpose(grad, (2, 0, 1, 3)) for grad in (grad_a, grad_b, grad_c, grad_d)]
    return (probability, stem_grad[:, None], *kernels, grad_one[0], grad_two[0])


def solution(mesh):
    return jax.shard_map(
        per_device,
        mesh=mesh,
        in_specs=(P(None, "slab", None, "gx"), P(None, "slab", "gx"), P(), P(), P(), P(), P(), P()),
        out_specs=(
            P(None, "slab", "gx"),
            P(None, "slab", None, "gx"),
            P(),
            P(),
            P(),
            P(),
            P(),
            P(),
        ),
        check_vma=False,
    )
```

```python
import functools

import jax
import jax.numpy as jnp
from jax import lax
from jax.experimental import pallas as pl
from jax.experimental.pallas import tpu as pltpu
from jax.sharding import PartitionSpec as P

HALO = 32
LEFT = 12
MORE = 16
C = 32
F32 = jnp.float32
BF16 = jnp.bfloat16
VMEM = pl.BlockSpec(memory_space=pltpu.VMEM)
HBM = pl.BlockSpec(memory_space=pltpu.HBM)
CONTRACT_ROWS = (((0,), (0,)), ((), ()))
CONTRACT_LANES = (((1,), (1,)), ((), ()))


def softplus(v):
    small = jnp.exp(-jnp.abs(v))
    tail = jnp.where(small < 1e-4, small, jnp.log(1.0 + small))
    return jnp.maximum(v, 0.0) + tail


def slope(stored):
    return 1.0 - jnp.exp(-stored.astype(F32))


def edge_gates():
    me, peers = lax.axis_index("gx"), lax.axis_size("gx")
    return jnp.where(me > 0, 0.0, 1.0), jnp.where(me < peers - 1, 1.0, 0.0)


def counted(value, first):
    row = lax.broadcasted_iota(jnp.int32, (MORE, 1), 0)
    cols = value.shape[0] - MORE
    head = value[:MORE].astype(F32) * jnp.where(row < LEFT, first, 1.0)
    tail = value[cols:].astype(F32) * jnp.where(row < LEFT, 1.0, 0.0)
    head, tail = head.astype(value.dtype), tail.astype(value.dtype)
    return jnp.concatenate([head, value[MORE:cols], tail], axis=0)


def gated(value, inside):
    cols = value.shape[0] - HALO
    return jnp.concatenate([value[:cols], value[cols:] * inside], axis=0)


def clear_margins(shifted):
    lanes = shifted.shape[-1]
    edge = jnp.zeros(shifted.shape[:-1] + (128,), BF16)
    shifted[..., 0:128] = edge
    shifted[..., lanes - 128 : lanes] = edge


def store_shifted(shifted, plane, start, value, step):
    rows, lanes = value.shape
    where = slice(128 + start, 128 + start + lanes)
    shifted[plane, 1, :, where] = value.astype(BF16)
    lower = pltpu.roll(value, step, 0)
    row = lax.broadcasted_iota(jnp.int32, (8, lanes), 0)
    lower = jnp.concatenate([jnp.where(row < step, 0.0, lower[:8]), lower[8:]], axis=0)
    shifted[plane, 0, :, where] = lower.astype(BF16)
    shifted[plane, 2, :, where] = pltpu.roll(value, rows - step, 0).astype(BF16)


def conv_window(shifted, plane, window, band):
    lanes = slice(256 * window, 256 * window + 512)
    columns = jnp.concatenate([shifted[plane, tap, :, lanes] for tap in range(3)], axis=1)
    return jnp.dot(columns, band[...], preferred_element_type=F32)


def windows_of(shifted):
    planes = shifted.shape[0]
    windows = (shifted.shape[-1] - 256) // 256
    return [(plane, window) for plane in range(planes) for window in range(windows)]


def weight_grad(delta, shifted, step, grads, first_piece, first):
    part = slice(0, delta.shape[1] - MORE)
    places = windows_of(shifted)
    left = jnp.concatenate(
        [
            counted(delta[plane, part, 256 * window : 256 * window + 256], first)
            for plane, window in places
        ],
        axis=0,
    )

    def step_of(tap):
        right = jnp.concatenate(
            [
                shifted[plane, tap, part, 256 * window : 256 * window + 512]
                for plane, window in places
            ],
            axis=0,
        )
        total = lax.dot_general(left, right, CONTRACT_ROWS, preferred_element_type=F32)
        folded = None
        for r in range(4):
            near = total[32 * r : 32 * r + 32, 0:384]
            far = total[32 * r + 128 : 32 * r + 160, 128:512]
            both = near + far
            if r:
                both = pltpu.roll(both, 384 - 32 * r, 1)
            folded = both if folded is None else folded + both
        for row_tap in range(3):
            at = 32 * (4 + step * (row_tap - 1))
            put_piece(grads, first_piece + 3 * row_tap + tap, folded[:, at : at + 32])

    return [functools.partial(step_of, tap) for tap in range(3)]


def run(steps):
    for step in steps:
        step()


def put_piece(grads, index, value):
    row, lane = 32 * (index // 4), 32 * (index % 4)
    grads[row : row + value.shape[0], lane : lane + 32] = value


def fill_tap(weight, band, step, backward, col_tap):
    lane = lax.broadcasted_iota(jnp.int32, (32, 128), 1) // 32
    cut = []
    for row_tap in range(3):
        if backward:
            block = weight[2 - row_tap, 2 - col_tap].astype(F32)
        else:
            block = weight[row_tap, col_tap].astype(F32).T
        block = jnp.concatenate([block] * 4, axis=1)
        cut.append([jnp.where(lane == q, block, 0.0) for q in range(4)])
    for source in range(16):
        for group in range(2):
            panel = None
            for q in range(4):
                off = source - 4 - (4 * group + q)
                if off % step == 0 and abs(off) <= step:
                    term = cut[off // step + 1][q]
                    panel = term if panel is None else panel + term
            if panel is None:
                panel = jnp.zeros((32, 128), F32)
            row = 512 * col_tap + 32 * source
            band[row : row + 32, 128 * group : 128 * group + 128] = panel.astype(BF16)


def fill_band(weight, band, step, backward):
    return [
        functools.partial(fill_tap, weight, band, step, backward, col_tap) for col_tap in range(3)
    ]


class Copies:
    def __init__(self, sems):
        self.sems, self.started = sems, []

    def start(self, source, target):
        copy = pltpu.make_async_copy(source, target, self.sems.at[len(self.started)])
        copy.start()
        self.started.append(copy)
        return copy

    def start_lanes(self, source, target, parts):
        size = source.shape[-1] // parts
        return [
            self.start(
                source.at[..., pl.ds(size * k, size)], target.at[..., pl.ds(size * k, size)]
            )
            for k in range(parts)
        ]


def wait_all(copies):
    for copy in copies:
        copy.wait()


def centre(shifted):
    return shifted.at[:, 1, :, pl.ds(128, shifted.shape[-1] - 256)]


def columns_first(stem, flat, side, group):
    first = 1024 * side + 4 * group
    rows = [flat[pl.ds(first + k, 32, stride=32), :] for k in range(4)]
    return jnp.concatenate(rows, axis=0).T


def fill_flat(stem, flat, side):
    part = stem[:, :, 128 * side : 128 * side + 128].reshape(1024, 128)
    flat[1024 * side : 1024 * side + 1024, :] = part.astype(F32)


def marks_first(labels):
    marks = labels.astype(F32)
    blank = jnp.zeros((96, labels.shape[2]), F32)
    marks = jnp.concatenate([marks[:, 0, :], marks[:, 1, :], blank], axis=0)
    return marks.T.astype(BF16)


def edge_kernel(
    stem_in, labels_in, conv_a_in, conv_b_in, head_one_in, head_two_in,
    initial, stem, labels, conv_a, conv_b, heads, flat, sems,
):
    copies = Copies(sems)
    for side in range(stem.shape[2] // 128):
        lanes = pl.ds(128 * side, 128)
        for k in range(4):
            rows = pl.ds(8 * k, 8)
            copies.start(stem_in.at[rows, :, lanes], stem.at[rows, :, lanes])
        if side == 0:
            copies.start(labels_in, labels)
    copies.start(conv_a_in, conv_a)
    copies.start(conv_b_in, conv_b)
    copies.start(head_one_in, heads.at[0])
    copies.start(head_two_in, heads.at[1])
    wait_all(copies.started[:5])
    fill_flat(stem, flat, 0)
    for group in range(8):
        value = columns_first(stem, flat, 0, group)
        initial[:, 128 * group : 128 * group + 128] = value[:HALO].astype(BF16)
    initial[:, 1024:1152] = marks_first(labels[:, :, :128])[:HALO]
    wait_all(copies.started[5:])


def arrange_kernel(
    stem, labels, conv_a, conv_b, heads,
    stem_out, marks_out, band_a, band_b, spread, flat,
):
    cols = stem.shape[2]
    same = own_voxel()
    for k in range(2):
        four = jnp.concatenate([heads[k].astype(F32)] * 4, axis=1)
        along = jnp.concatenate([four] * 8, axis=1)
        spread[32 * k : 32 * k + 32, :] = jnp.where(same, along, 0.0).astype(BF16)
    marks_out[...] = marks_first(labels[...])
    run(fill_band(conv_a, band_a, 1, False))
    run(fill_band(conv_b, band_b, 2, False))
    for side in range(cols // 128):
        fill_flat(stem, flat, side)
    for group in range(8):
        sides = [columns_first(stem, flat, side, group) for side in range(cols // 128)]
        value = jnp.concatenate(sides, axis=0).astype(BF16)
        stem_out[:, 128 * group : 128 * group + 128] = value


def own_voxel():
    voxel = lax.broadcasted_iota(jnp.int32, (32, 1024), 0)
    return voxel == lax.broadcasted_iota(jnp.int32, (32, 1024), 1) // 32


def forward_xy_kernel(
    stem, marks, after, band_a, band_b,
    stem_s, one_s, hidden_two, marks_out, message,
):
    _, inside = edge_gates()
    clear_margins(stem_s)
    clear_margins(one_s)
    for window in range(4):
        lanes = slice(256 * window, 256 * window + 256)
        value = jnp.concatenate([stem[:, lanes], after[:, lanes]], axis=0)
        store_shifted(stem_s, 0, 256 * window, value.astype(F32), 1)
    marks_out[...] = jnp.concatenate([marks[...], after[:, 1024:1152]], axis=0)
    for window in range(4):
        value = gated(softplus(conv_window(stem_s, 0, window, band_a)), inside)
        store_shifted(one_s, 0, 256 * window, value, 2)
    for window in range(4):
        value = gated(softplus(conv_window(one_s, 0, window, band_b)), inside).astype(BF16)
        hidden_two[0, :, 256 * window : 256 * window + 256] = value
        half = value.shape[0] // 2
        for peer in range(4):
            lanes = slice(64 * peer, 64 * peer + 64)
            message[4 * window + peer] = jnp.concatenate(
                [value[:half, lanes], value[half:, lanes]], axis=1
            )


def load_features(message, two_s):
    for plane in range(2):
        for group in range(4):
            parts = []
            for side in range(2):
                at = 64 * side + 32 * plane
                parts.append(
                    jnp.concatenate(
                        [message[4 * group + q][:, at : at + 32] for q in range(4)], axis=1
                    )
                )
            value = jnp.concatenate(parts, axis=0).astype(F32)
            store_shifted(two_s, plane, 128 * group, value, 1)


def split(error):
    high = error.astype(BF16)
    low = (error - high.astype(F32)).astype(BF16)
    return jnp.concatenate([high, low], axis=1)


def section_xz_kernel(
    message, marks, conv_c, conv_d, spread,
    probability, back,
    two_s, ref_one_s, delta_two_s, delta_one_s, ref_two, bands, grads,
):
    left, inside = edge_gates()
    band_c, band_d, band_dt, band_ct = [bands.at[k] for k in range(4)]
    rows = marks.shape[0]
    half = (rows - MORE) // 2
    upper = slice(half, 2 * half)
    for shifted in (two_s, ref_one_s, delta_two_s, delta_one_s):
        clear_margins(shifted)
    places = windows_of(two_s)
    run(fill_band(conv_c, band_c, 1, False))
    load_features(message, two_s)
    steps = fill_band(conv_d, band_d, 2, False)
    for plane, window in places:
        value = gated(softplus(conv_window(two_s, plane, window, band_c)), inside)
        store_shifted(ref_one_s, plane, 256 * window, value, 2)
        run(steps[:1])
        steps = steps[1:]
    steps = fill_band(conv_d, band_dt, 2, True)
    for plane, window in places:
        value = softplus(conv_window(ref_one_s, plane, window, band_d))
        ref_two[plane, :, 256 * window : 256 * window + 256] = value.astype(BF16)
        run(steps[:1])
        steps = steps[1:]

    labels = marks[:, 0:32].astype(F32)
    spread_one, spread_two = spread[0:32, :], spread[32:64, :]
    first, second = None, None
    for plane in range(2):
        lanes = slice(512 * plane, 512 * plane + 512)
        one = lax.dot_general(
            two_s[plane, 1, :, 128:640], spread_one[:, lanes], CONTRACT_LANES,
            preferred_element_type=F32,
        )
        two = lax.dot_general(
            ref_two[plane], spread_two[:, lanes], CONTRACT_LANES, preferred_element_type=F32
        )
        first = one if first is None else first + one
        second = two if second is None else second + two
    first = first.astype(BF16).astype(F32)
    second = second + first
    share = 1.0 / (1.0 + jnp.exp(-second))
    probability[...] = share[: rows - MORE]
    error_two = gated(share - labels, inside)
    error_one = 1.0 / (1.0 + jnp.exp(-first)) - labels + error_two
    error_two = split(error_two)
    error_one = split(error_one)
    spread_one = jnp.concatenate([spread_one, spread_one], axis=0)
    spread_two = jnp.concatenate([spread_two, spread_two], axis=0)

    for plane, window in places:
        at = 256 * window
        lanes = slice(512 * plane + at, 512 * plane + at + 256)
        value = jnp.dot(error_two, spread_two[:, lanes], preferred_element_type=F32)
        value = value * slope(ref_two[plane, :, at : at + 256])
        store_shifted(delta_two_s, plane, at, value, 2)
    grads[...] = jnp.zeros(grads.shape, F32)
    fills = fill_band(conv_c, band_ct, 1, True)
    sums = weight_grad(centre(delta_two_s), ref_one_s, 2, grads, 9, left)
    for plane, window in places:
        at = 256 * window
        value = conv_window(delta_two_s, plane, window, band_dt)
        stored = ref_one_s[plane, 1, :, 128 + at : 384 + at]
        value = gated(value * slope(stored), inside)
        store_shifted(delta_one_s, plane, at, value, 1)
        run(fills[:1] + sums[:1])
        fills, sums = fills[1:], sums[1:]
    sums = weight_grad(centre(delta_one_s), two_s, 1, grads, 0, left)
    for window in range(2):
        values = []
        for plane in range(2):
            at = 256 * window
            lanes = slice(512 * plane + at, 512 * plane + at + 256)
            value = conv_window(delta_one_s, plane, window, band_ct)
            value = value + jnp.dot(error_one, spread_one[:, lanes], preferred_element_type=F32)
            values.append([value[:half].astype(BF16), value[upper].astype(BF16)])
        for z in range(8):
            lanes = slice(32 * z, 32 * z + 32)
            back[8 * window + z, :half] = jnp.concatenate(
                [
                    values[0][0][:, lanes], values[1][0][:, lanes],
                    values[0][1][:, lanes], values[1][1][:, lanes],
                ],
                axis=1,
            )
        run(sums[:1])
        sums = sums[1:]

    same = own_voxel()
    same = jnp.concatenate([same, same], axis=0)
    kept_rows = slice(0, rows - MORE)

    def head_grad(errors, planes):
        error = counted(errors[kept_rows], left)
        total = None
        for plane, feature in enumerate(planes):
            full = lax.dot_general(error, feature, CONTRACT_ROWS, preferred_element_type=F32)
            kept = jnp.where(same[:, 512 * plane : 512 * plane + 512], full, 0.0)
            kept = jnp.sum(kept, axis=0, keepdims=True)
            kept = kept[:, 0:128] + kept[:, 128:256] + kept[:, 256:384] + kept[:, 384:512]
            total = kept if total is None else total + kept
        total = total + pltpu.roll(total, 64, 1)
        total = total + pltpu.roll(total, 32, 1)
        return total[:, 0:32]

    run(sums)
    features = [two_s[plane, 1, kept_rows, 128:640] for plane in range(2)]
    put_piece(grads, 18, head_grad(error_one, features))
    features = [ref_two[plane, kept_rows, :] for plane in range(2)]
    put_piece(grads, 19, head_grad(error_two, features))
    blank = jnp.zeros((6, 128), F32)
    for peer in range(16):
        chunk = jnp.concatenate([grads[10 * peer : 10 * peer + 10, :], blank], axis=0)
        back[peer, half : half + 16, :] = chunk.astype(BF16)


def backward_xy_kernel(
    back, hidden_two, one_s, stem_s, conv_b,
    mine_out, theirs_out, delta_a,
    delta_b_s, delta_b, grads, band_bt,
):
    first, inside = edge_gates()
    run(fill_band(conv_b, band_bt, 2, True))
    clear_margins(delta_b_s)
    half = back.shape[1] - 16
    for group in range(8):
        parts = []
        for side in range(2):
            at = 64 * side
            parts.append(
                jnp.concatenate(
                    [back[2 * group + q, :half, at : at + 64] for q in range(2)], axis=1
                ).astype(F32)
            )
        lanes = slice(128 * group, 128 * group + 128)
        value = jnp.concatenate(parts + [jnp.zeros((MORE, 128), F32)], axis=0)
        value = gated(value * slope(hidden_two[0, :, lanes]), inside)
        delta_b[0, :, lanes] = value.astype(BF16)
        store_shifted(delta_b_s, 0, 128 * group, value, 2)
    for window in range(4):
        at = 256 * window
        value = conv_window(delta_b_s, 0, window, band_bt)
        stored = one_s[0, 1, :, 128 + at : 384 + at]
        value = gated(value * slope(stored), inside)
        delta_a[0, :, at : at + 256] = value.astype(BF16)
    grads[...] = jnp.zeros(grads.shape, F32)
    run(weight_grad(delta_b, one_s, 2, grads, 9, first))
    run(weight_grad(delta_a, stem_s, 1, grads, 0, first))
    chunk = back[0, half:, :].astype(F32)
    for peer in range(1, 16):
        chunk = chunk + back[peer, half:, :].astype(F32)
    last = [grads[128 + 16 * (k % 2) : 144 + 16 * (k % 2), 32 * (k // 2) : 32 * (k // 2) + 32] for k in range(4)]
    grads[128:144, :] = jnp.concatenate(last, axis=1)
    core = lax.rem(lax.axis_index("gx"), 2)
    mine_out[0:72, :] = grads[pl.ds(pl.multiple_of(72 * core, 8), 72), :]
    theirs_out[0:72, :] = grads[pl.ds(pl.multiple_of(72 * (1 - core), 8), 72), :]
    mine_out[72:88, :] = chunk
    theirs_out[72:88, :] = chunk


def stem_grad_kernel(delta_a, probability, conv_a, stem_grad, leaving, delta_a_s, band_at):
    rows = delta_a.shape[1]
    cols = rows - 2 * MORE
    tail = slice(cols, cols + MORE)
    clear_margins(delta_a_s)
    run(fill_band(conv_a, band_at, 1, True))
    for window in range(4):
        lanes = slice(256 * window, 256 * window + 256)
        store_shifted(delta_a_s, 0, 256 * window, delta_a[0, :, lanes].astype(F32), 1)
    for window in range(4):
        lanes = slice(256 * window, 256 * window + 256)
        value = conv_window(delta_a_s, 0, window, band_at).astype(BF16)
        stem_grad[:, lanes] = value[:cols]
        leaving[:, lanes] = value[tail]
    rest = probability[tail, :]
    parts = []
    for _ in range(3):
        parts.append(rest.astype(BF16))
        rest = rest - parts[-1].astype(F32)
    parts.append(jnp.zeros((MORE, 32), BF16))
    leaving[:, 1024:1152] = jnp.concatenate(parts, axis=1)


def place_kernel(found, probability, moved, stem_grad, share, flat):
    cols = stem_grad.shape[2]
    first, _ = edge_gates()
    row = lax.broadcasted_iota(jnp.int32, (MORE, 1), 0)
    taken = jnp.where(row < LEFT, 1.0 - first, 0.0)
    for group in range(8):
        lanes = slice(128 * group, 128 * group + 128)
        mine = found[:, lanes].astype(F32)
        head = mine[:MORE] * (1.0 - taken) + moved[:, lanes].astype(F32) * taken
        value = jnp.concatenate([head, mine[MORE:]], axis=0)
        for side in range(cols // 128):
            turned = value[128 * side : 128 * side + 128].T
            for k in range(4):
                start = 1024 * side + 4 * group + k
                flat[pl.ds(start, 32, stride=32), :] = turned[32 * k : 32 * k + 32]
    for side in range(cols // 128):
        part = flat[1024 * side : 1024 * side + 1024, :].reshape(32, 32, 128)
        stem_grad[:, :, 128 * side : 128 * side + 128] = part.astype(BF16)
    parts = moved[:, 1024:1152].astype(F32)
    head = parts[:, 0:32] + parts[:, 32:64] + parts[:, 64:96]
    head = probability[:MORE, :] * (1.0 - taken) + head * taken
    value = jnp.concatenate([head, probability[MORE:cols, :]], axis=0).T
    share[:, 0, :] = value[0:16]
    share[:, 1, :] = value[16:32]


def finish_cd_kernel(factor, chunks, grad_c, grad_d, head_one, head_two, flat):
    for peer in range(16):
        upper, z = peer // 8, peer % 8
        chunk = chunks[z, 10 * upper : 10 * upper + 10, :].astype(F32)
        flat[10 * peer : 10 * peer + 10, :] = chunk * factor

    def piece(index):
        row, lane = 32 * (index // 4), 32 * (index % 4)
        return flat[row : row + 32, lane : lane + 32]

    for tap in range(9):
        grad_c[tap // 3, tap % 3] = piece(tap)
        grad_d[tap // 3, tap % 3] = piece(9 + tap)
    head_one[...] = piece(18)[0:1]
    head_two[...] = piece(19)[0:1]


def finish_ab_kernel(factor, mine, theirs, grad_a, grad_b, flat):
    core = lax.rem(lax.axis_index("gx"), 2)
    flat[pl.ds(pl.multiple_of(72 * core, 8), 72), :] = mine[...] * factor
    flat[pl.ds(pl.multiple_of(72 * (1 - core), 8), 72), :] = theirs[...] * factor

    def piece(index):
        row, lane = 32 * (index // 4), 32 * (index % 4)
        if index >= 16:
            lane = 64 * (index % 4)
            halves = [flat[row : row + 16, lane + at : lane + at + 32] for at in (0, 32)]
            return jnp.concatenate(halves, axis=0)
        return flat[row : row + 32, lane : lane + 32]

    for tap in range(9):
        grad_a[tap // 3, tap % 3] = piece(tap)
        grad_b[tap // 3, tap % 3] = piece(9 + tap)


def finish_kernel(
    factor, mine, theirs, chunks, grad_a, grad_b, grad_c, grad_d, head_one, head_two, flat, other
):
    finish_cd_kernel(factor, chunks, grad_c, grad_d, head_one, head_two, other)
    finish_ab_kernel(factor, mine, theirs, grad_a, grad_b, flat)


def call(kernel, outs, ins, scratch=(), flops=0, megabytes=16):
    places = [place for _, place in outs]
    shapes = [pltpu.HBM(out.shape, out.dtype) if place is HBM else out for out, place in outs]

    def run(*operands):
        operands = [
            pltpu.with_memory_space_constraint(operand, pltpu.HBM) if place is HBM else operand
            for operand, place in zip(operands, ins)
        ]
        return bound(*operands)

    bound = pl.pallas_call(
        kernel,
        out_shape=shapes,
        in_specs=ins,
        out_specs=list(places),
        scratch_shapes=scratch,
        compiler_params=pltpu.CompilerParams(vmem_limit_bytes=megabytes * 1024 * 1024),
        cost_estimate=pl.CostEstimate(flops=flops, bytes_accessed=1 << 20, transcendentals=0),
    )
    return run


def shape(dims, dtype):
    return jax.ShapeDtypeStruct(dims, dtype)


def sum_everywhere(mine, theirs, beside, later, slab, gx):
    peers, slabs = lax.axis_size(gx), lax.axis_size(slab)
    depth, wide = slabs // 2, peers // 2
    swap = [(i, i ^ 1) for i in range(peers)]
    theirs, beside = lax.optimization_barrier((lax.ppermute(theirs, gx, swap), beside))
    mine = mine + theirs
    across = [
        [(upper * depth + z) * peers + 2 * chip + core for upper in range(2) for chip in range(wide)]
        for z in range(depth)
        for core in range(2)
    ]
    spread = jnp.broadcast_to(mine.astype(BF16)[None], (2 * wide,) + mine.shape)
    found = lax.all_to_all(spread, (slab, gx), 0, 0, tiled=True, axis_index_groups=across)
    found, beside = lax.optimization_barrier((found, later(beside)))
    halves = jnp.sum(found.astype(F32).reshape((2, wide) + mine.shape), axis=1)
    chunks = halves[:, 72:82].reshape(20, 128)
    mine = jnp.concatenate([halves[0, :72] + halves[1, :72], chunks, jnp.zeros((4, 128), F32)])
    along = [[upper * depth + z for z in range(depth)] for upper in range(2)]
    spread = jnp.broadcast_to(mine.astype(BF16)[None], (depth,) + mine.shape)
    found = lax.all_to_all(spread, slab, 0, 0, tiled=True, axis_index_groups=along)
    mine = jnp.sum(found[:, :72].astype(F32), axis=0)
    return (mine, lax.ppermute(mine, gx, swap), found[:, 72:]), beside


def per_device(stem_features, labels, conv_a, conv_b, conv_c, conv_d, head_one, head_two):
    _, depth, height, cols = stem_features.shape
    rows = cols + HALO
    half = rows // 2
    peers = lax.axis_size("gx")
    up = [(i, i + 1) for i in range(peers - 1)]
    down = [(j, i) for i, j in up]
    sems = lambda count: pltpu.SemaphoreType.DMA((count,))
    vmem = lambda kind: pltpu.VMEM(kind.shape, kind.dtype)

    stem_features = stem_features[:, 0]
    taps_a, taps_b, taps_c, taps_d = [
        jnp.transpose(w, (1, 2, 0, 3)) for w in (conv_a, conv_b, conv_c, conv_d)
    ]
    held = [stem_features, labels, taps_a, taps_b]
    initial, *loaded = call(
        edge_kernel,
        [(shape((HALO, 1152), BF16), VMEM)]
        + [(shape(array.shape, array.dtype), VMEM) for array in held]
        + [(shape((2, 1, C), BF16), VMEM)],
        [HBM] * 6, [pltpu.VMEM((1024, 128), F32), sems(13)], flops=1 << 28, megabytes=3,
    )(*held, head_one[None], head_two[None])
    after = lax.ppermute(initial, "gx", down)

    band = shape((1536, 256), BF16)
    spreads = shape((64, 1024), BF16)
    stem, marks, band_a, band_b, spread = call(
        arrange_kernel,
        [
            (shape((cols, 1024), BF16), VMEM),
            (shape((cols, 128), BF16), VMEM),
            (band, VMEM),
            (band, VMEM),
            (spreads, VMEM),
        ],
        [VMEM] * 5,
        [pltpu.VMEM((1024 * cols // 128, 128), F32)],
        flops=1 << 29, megabytes=6,
    )(*loaded)

    shifted = shape((1, 3, rows, 1280), BF16)
    wide = vmem(shifted)
    tall = pltpu.VMEM((2, 3, rows, 768), BF16)
    whole = shape((1, rows, 1024), BF16)
    planes = shape((2, rows, 512), BF16)
    messages = shape((16, half, 128), BF16)
    stem_s, one_s, hidden_two, marks, message = call(
        forward_xy_kernel,
        [(shifted, VMEM)] * 2
        + [(whole, VMEM), (shape((rows, 128), BF16), VMEM), (messages, VMEM)],
        [VMEM] * 5, flops=1 << 30, megabytes=8,
    )(stem, marks, after, band_a, band_b)
    message = lax.all_to_all(message, "slab", 0, 0, tiled=True)

    larger = shape((16, (cols + MORE) // 2 + MORE, 128), BF16)
    probability, back = call(
        section_xz_kernel,
        [(shape((rows - MORE, 32), F32), VMEM), (larger, VMEM)],
        [VMEM] * 5,
        [tall, tall, tall, tall, vmem(planes), pltpu.VMEM((4, 1536, 256), BF16)]
        + [pltpu.VMEM((160, 128), F32)],
        flops=1 << 31, megabytes=28,
    )(message, marks, taps_c, taps_d, spread)
    back = lax.all_to_all(back, "slab", 0, 0, tiled=True)

    half_sums = shape((88, 128), F32)
    mine, theirs, delta_a = call(
        backward_xy_kernel,
        [(half_sums, VMEM), (half_sums, VMEM), (whole, VMEM)],
        [VMEM] * 5,
        [wide, vmem(whole), pltpu.VMEM((160, 128), F32), vmem(band)],
        flops=1 << 31, megabytes=16,
    )(back, hidden_two, one_s, stem_s, taps_b)
    edge = shape((MORE, 1152), BF16)
    beside = call(
        stem_grad_kernel,
        [(shape((cols, 1024), BF16), VMEM), (edge, VMEM)],
        [VMEM] * 3, [wide, vmem(band)], flops=1 << 30, megabytes=6,
    )(delta_a, probability, taps_a)

    def place(beside):
        found, leaving = beside
        moved = lax.ppermute(leaving, "gx", up)
        return call(
            place_kernel,
            [(shape((C, height, cols), BF16), VMEM), (shape((16, 2, cols), F32), VMEM)],
            [VMEM] * 3, [pltpu.VMEM((1024 * cols // 128, 128), F32)], flops=1 << 28, megabytes=4,
        )(found, probability, moved)

    (mine, theirs, chunks), (stem_grad, probability) = sum_everywhere(
        mine, theirs, beside, place, "slab", "gx"
    )

    taps = shape((3, 3, C, C), F32)
    head = shape((1, C), F32)
    factor = 1.0 / (depth * height * cols)
    grad_a, grad_b, grad_c, grad_d, grad_one, grad_two = call(
        functools.partial(finish_kernel, factor), [(taps, VMEM)] * 4 + [(head, VMEM)] * 2,
        [VMEM] * 3, [pltpu.VMEM((144, 128), F32), pltpu.VMEM((160, 128), F32)],
        flops=1 << 20, megabytes=3,
    )(mine, theirs, chunks)
    kernels = [jnp.transpose(grad, (2, 0, 1, 3)) for grad in (grad_a, grad_b, grad_c, grad_d)]
    return (probability, stem_grad[:, None], *kernels, grad_one[0], grad_two[0])


def solution(mesh):
    return jax.shard_map(
        per_device,
        mesh=mesh,
        in_specs=(P(None, "slab", None, "gx"), P(None, "slab", "gx"), P(), P(), P(), P(), P(), P()),
        out_specs=(
            P(None, "slab", "gx"),
            P(None, "slab", None, "gx"),
            P(),
            P(),
            P(),
            P(),
            P(),
            P(),
        ),
        check_vma=False,
    )
```
